32 devices in a mesh: row: 4 (over y, core), col: 8 (over z, x).
Axes of the slice: x: 2, y: 2, z: 4, core: 2. Of those that a mesh axis runs over, the one named last changes fastest.
Arguments:
- a_window: bfloat16 [320, 1024], P('row', 'col'), may hold values from -60 to 60, as said below
- b_section: bfloat16 [4096, 8192], P('row', 'col'), may hold values from -60 to 60, as said below
- owners: int32 [4, 8, 10, 16, 1], P('row', 'col'), may hold values from 0 to 31; in each aligned block of 160 rows (0 to 159, 160 to 319, ..., all dimensions but the last counted through in order) at most 8 rows name the same one
- pos_rows: int32 [40, 128], P('row', 'col'), may hold values from 80 to 944
- pos_cols: int32 [40, 128], P('row', 'col'), may hold values from 80 to 944
- peaks: int32 [2, 40, 128], P(None, 'row', 'col'), may hold values from -4 to 4
Outputs:
- relaxed_flow: float32 [2, 40, 128], P(None, 'row', 'col')
- runner: float32 [40, 128], P('row', 'col')
The draws below stay inside these ranges and needn't reach their ends.
Inputs may be any that keep to these rules, and one draw needn't show every extreme that they name: No owner is named by more than 8 nodes of one device; some owner is named by exactly 8 nodes of one device; owners are unevenly loaded. `a_window`: pixel intensities. `b_section`: pixel intensities.
All inputs are finite; a program needn't handle non-finite values.
Results may differ from the reference program's by a relative error of at most 0.0057.
Values may be sent and summed in bfloat16 or wider, within the bound.
No kernel may reach another device: no remote copies, remote signals or barrier semaphores. Data moves between devices by JAX's collectives and lax.ppermute only.
A program may use at most 128 MiB of HBM per device.

```python
import math
import jax
import jax.numpy as jnp
import numpy as np
from jax import lax

PATCH = 160
STRIDE = 8
NODE_ROWS = 10
NODE_COLS = 16
TILE_ROWS = 1024
TILE_COLS = 1024
RELAX = 2
NODES = 160
CAP = 8
MESH_ROWS = 40
MESH_COLS = 128
WIN_ROWS = 320
WIN_COLS = 1024
SEC_ROWS = 4096
SEC_COLS = 8192
N_ROW = 4
N_COL = 8
DEVICES = 32


def image_scales(key, height, breadth):
    key_rows, key_cols = jax.random.split(key)
    row_scale = jnp.exp(jax.random.uniform(key_rows, (height, 1), jnp.float32, 0.0, 1.1513))
    col_scale = jnp.exp(jax.random.uniform(key_cols, (1, breadth), jnp.float32, 0.0, 1.1513))
    return row_scale * col_scale


def draw_a_window(key, part):
    key = jax.random.fold_in(key, 11)
    key_base, key_scale = jax.random.split(key)
    base = jnp.clip(jax.random.normal(key_base, (WIN_ROWS, WIN_COLS), jnp.float32), -6.0, 6.0)
    return (base * image_scales(key_scale, WIN_ROWS, WIN_COLS)).astype(jnp.bfloat16)


def draw_b_section(key, part):
    key = jax.random.fold_in(key, 23)
    key_base, key_scale = jax.random.split(key)
    base = jnp.clip(jax.random.normal(key_base, (SEC_ROWS, SEC_COLS), jnp.float32), -6.0, 6.0)
    return (base * image_scales(key_scale, SEC_ROWS, SEC_COLS)).astype(jnp.bfloat16)


def set_ends(array, own_key, low, high):
    dims = array.shape
    index_at = [jax.random.randint(jax.random.fold_in(own_key, axis), (), 0, dims[axis]) for axis in range(len(dims))]
    array = array.at[tuple(index_at)].set(low)
    longest = dims.index(max(dims))
    index_at[longest] = (index_at[longest] + 1) % dims[longest]
    return array.at[tuple(index_at)].set(high)


def shared_out(key, own, number, rows, number_of, top, reach, lean):
    order = jax.random.permutation(key, number_of)
    packed, ordinary = portions_of(number_of, rows * top, reach, lean, True), portions_of(number_of, rows * top, reach, lean, False)
    places = jnp.arange(number_of)

    def named(lengths, rotation):
        used = int((lengths > 0).sum())
        fixed = max(1, used // 4)
        moved = fixed + (places - fixed + rotation * (used - fixed)) % max(1, number_of - fixed)
        return jnp.zeros((number_of,), jnp.int32).at[order[jnp.where(places < fixed, places, moved)]].set(jnp.asarray(lengths, jnp.int32))

    lengths = jnp.where(number % 4 == 0, named(packed, number // 4), named(ordinary, number - number // 4 - 1))
    mixed = jax.random.permutation(jax.random.fold_in(own, 3), number_of)
    donor, sink = mixed[0:number_of // 2 * 2:2], mixed[1:number_of // 2 * 2:2]
    slack = jnp.minimum(lengths[donor] - 1, reach - lengths[sink]) // 2
    slack = jnp.where((donor == order[0]) | (sink == order[0]) | (lengths[sink] == 0), 0, jnp.maximum(slack, 0))
    moved = jax.random.randint(jax.random.fold_in(own, 4), (number_of // 2,), 0, 1 << 20) % (slack + 1)
    lengths = lengths.at[donor].add(-moved).at[sink].add(moved)
    items = jnp.searchsorted(jnp.cumsum(lengths), jnp.arange(rows * top), side="right").astype(jnp.int32)
    listing = items.reshape(top, rows).T
    listing = listing[jax.random.permutation(jax.random.fold_in(own, 1), rows)]
    rotation = jax.random.randint(jax.random.fold_in(own, 2), (rows, 1), 0, top)
    return jnp.take_along_axis(listing, (jnp.arange(top)[None, :] + rotation) % top, axis=1)


def portions_of(count, total, most, slope, full):
    loads = [(1 << 20) // math.isqrt(grade ** slope) + 1 for grade in range(1, count + 1)]
    largest = most if full else min(most, max(-(-total // count), total * loads[0] // sum(loads)))
    least = 1 if total - largest >= count - 1 else 0
    counts, spare = [largest] + [least] * (count - 1), total - largest - least * (count - 1)
    while spare > 0:
        candidates = [i for i in range(1, count) if counts[i] < largest] or [i for i in range(1, count) if counts[i] < most]
        pool, left = sum([loads[i] for i in candidates]), spare
        for i in candidates:
            more = min(most - counts[i], max(1, left * loads[i] // pool), spare)
            counts[i] = counts[i] + more
            spare = spare - more
    return np.array(counts)


def setup_inputs(seed: int = 0) -> dict:
    streams_of = jax.random.split(jax.random.key(seed), 7)
    a_window = draw_a_window(jax.random.fold_in(streams_of[6], 71), 0)
    b_section = draw_b_section(jax.random.fold_in(streams_of[6], 71), 0)
    owners_keys = jax.random.split(jax.random.fold_in(streams_of[2], 1), N_ROW * N_COL * NODE_ROWS * NODE_COLS // NODES)
    owners_turns = jax.random.permutation(jax.random.fold_in(streams_of[2], 3), N_ROW * N_COL * NODE_ROWS * NODE_COLS // NODES)
    owners = jax.vmap(lambda own, number: shared_out(jax.random.fold_in(streams_of[2], 2), own, number, NODES, DEVICES, 1, CAP, 2))(owners_keys, owners_turns).reshape((N_ROW, N_COL, NODE_ROWS, NODE_COLS, 1))
    pos_rows = set_ends(jax.random.randint(streams_of[3], (MESH_ROWS, MESH_COLS), PATCH // 2, TILE_ROWS - PATCH // 2 + 1), jax.random.fold_in(streams_of[3], 1), PATCH // 2, (TILE_ROWS - PATCH // 2 + 1) - 1).astype(jnp.int32)
    pos_cols = set_ends(jax.random.randint(streams_of[4], (MESH_ROWS, MESH_COLS), PATCH // 2, TILE_COLS - PATCH // 2 + 1), jax.random.fold_in(streams_of[4], 1), PATCH // 2, (TILE_COLS - PATCH // 2 + 1) - 1).astype(jnp.int32)
    peaks = set_ends(jax.random.randint(streams_of[5], (2, MESH_ROWS, MESH_COLS), -4, 5), jax.random.fold_in(streams_of[5], 1), -4, 4).astype(jnp.int32)
    return dict(a_window=a_window, b_section=b_section, owners=owners, pos_rows=pos_rows, pos_cols=pos_cols, peaks=peaks)


sharpness = 80.0
epsilon = 1e-06
stiffness = 0.24
centre_reach = 2

def dft_tables(extent):
    indices = jnp.arange(extent, dtype=jnp.int32)
    product = indices[:, None] * indices[None, :] % extent
    angles = product.astype(jnp.float32) * (2.0 * math.pi / extent)
    return (jnp.cos(angles).astype(jnp.bfloat16), jnp.sin(angles).astype(jnp.bfloat16))

def batched(left_fourier_table, stacked_pairs):
    return jnp.einsum('dr,xre->xde', left_fourier_table.astype(jnp.float32), stacked_pairs.astype(jnp.float32))

def spectrum(patch_stack, right_table, left_fourier_table):
    shift_magnitude, extent = (patch_stack.shape[0], patch_stack.shape[1])
    halves = jnp.dot(patch_stack.reshape(shift_magnitude * extent, extent), right_table, preferred_element_type=jnp.float32)
    halves = halves.astype(jnp.bfloat16).reshape(shift_magnitude, extent, 2 * extent)
    real_part = halves[:, :, :extent]
    imag_part = halves[:, :, extent:]
    stacked_pairs = jnp.concatenate([halves, jnp.concatenate([imag_part, -real_part], axis=2)], axis=1)
    return batched(left_fourier_table, stacked_pairs)

def correlate(first, second, peak_rows, peak_cols):
    shift_magnitude, extent = (first.shape[0], first.shape[1])
    cosine, sine = dft_tables(extent)
    right_table = jnp.concatenate([cosine, -sine], axis=1)
    left_fourier_table = jnp.concatenate([cosine, sine], axis=1)
    back_table = jnp.concatenate([cosine, -sine], axis=0)
    spec_first = spectrum(first, right_table, left_fourier_table)
    spec_second = spectrum(second, right_table, left_fourier_table)
    first_real = spec_first[:, :, :extent]
    first_spectrum_imaginary = spec_first[:, :, extent:]
    second_real = spec_second[:, :, :extent]
    second_imag = spec_second[:, :, extent:]
    cross_real = first_real * second_real + first_spectrum_imaginary * second_imag
    cross_imag = first_real * second_imag - first_spectrum_imaginary * second_real
    cross = jnp.concatenate([cross_real, cross_imag], axis=2).astype(jnp.bfloat16)
    cross_real_b = cross[:, :, :extent]
    cross_imag_b = cross[:, :, extent:]
    stacked_pairs = jnp.concatenate([cross, jnp.concatenate([-cross_imag_b, cross_real_b], axis=2)], axis=1)
    inverse_half = batched(left_fourier_table, stacked_pairs).astype(jnp.bfloat16)
    correlation = jnp.dot(inverse_half.reshape(shift_magnitude * extent, 2 * extent), back_table, preferred_element_type=jnp.float32)
    correlation = correlation.reshape(shift_magnitude, extent, extent)
    energy_first = lax.optimization_barrier(jnp.mean(jnp.square(first.astype(jnp.float32)), axis=(1, 2)))
    energy_second = lax.optimization_barrier(jnp.mean(jnp.square(second.astype(jnp.float32)), axis=(1, 2)))
    scaling = float(extent * extent * extent * extent) * jnp.sqrt(energy_first + epsilon) * jnp.sqrt(energy_second + epsilon)
    score = correlation / scaling[:, None, None]
    positions = jnp.arange(extent, dtype=jnp.int32)
    shift_rows = (positions[None, :] - peak_rows[:, None] + extent // 2) % extent - extent // 2
    shift_cols = (positions[None, :] - peak_cols[:, None] + extent // 2) % extent - extent // 2
    near = (jnp.abs(shift_rows) <= centre_reach)[:, :, None] & (jnp.abs(shift_cols) <= centre_reach)[:, None, :]
    weights = jnp.where(near, jnp.exp(sharpness * score), 0.0)
    total = lax.optimization_barrier(jnp.sum(weights, axis=(1, 2)))
    moment_rows = lax.optimization_barrier(jnp.sum(weights * shift_rows[:, :, None].astype(jnp.float32), axis=(1, 2)))
    moment_cols = lax.optimization_barrier(jnp.sum(weights * shift_cols[:, None, :].astype(jnp.float32), axis=(1, 2)))
    flow_rows = peak_rows.astype(jnp.float32) + moment_rows / total
    flow_cols = peak_cols.astype(jnp.float32) + moment_cols / total
    runner = lax.optimization_barrier(jnp.max(jnp.where(near, -2.0, score), axis=(1, 2)))
    return (flow_rows, flow_cols, runner)

def neighbours(padded_image):
    return padded_image[:, 2:, 1:-1] + padded_image[:, :-2, 1:-1] + padded_image[:, 1:-1, 2:] + padded_image[:, 1:-1, :-2]

def reference(a_window, b_section, owners, pos_rows, pos_cols, peaks):
    half_patch = PATCH // 2
    owner_grid = jnp.transpose(owners[..., 0], (0, 2, 1, 3)).reshape(MESH_ROWS, MESH_COLS).astype(jnp.int32)
    b_top = (owner_grid // N_COL * TILE_ROWS + pos_rows - half_patch).astype(jnp.int32)
    b_left = (owner_grid % N_COL * TILE_COLS + pos_cols - half_patch).astype(jnp.int32)
    centre_rows = jnp.arange(MESH_ROWS, dtype=jnp.int32) * STRIDE + STRIDE // 2
    centre_cols = jnp.arange(MESH_COLS, dtype=jnp.int32) * STRIDE + STRIDE // 2
    a_top = jnp.broadcast_to(centre_rows[:, None], (MESH_ROWS, MESH_COLS))
    a_left = jnp.broadcast_to(centre_cols[None, :], (MESH_ROWS, MESH_COLS))
    padded_image = jnp.pad(a_window, half_patch)
    total_nodes = MESH_ROWS * MESH_COLS
    block_size = math.gcd(total_nodes, 64)

    def flatten(grid):
        return grid.reshape(total_nodes // block_size, block_size).astype(jnp.int32)

    def per_block(items):
        a_rows, a_cols, b_rows, second_section_columns, peak_rows, peak_cols = items
        first = jax.vmap(lambda corner_row, corner_col: lax.dynamic_slice(padded_image, (corner_row, corner_col), (PATCH, PATCH)))(a_rows, a_cols)
        second = jax.vmap(lambda corner_row, corner_col: lax.dynamic_slice(b_section, (corner_row, corner_col), (PATCH, PATCH)))(b_rows, second_section_columns)
        return correlate(first, second, peak_rows, peak_cols)
    flow_rows, flow_cols, runner = lax.map(per_block, (flatten(a_top), flatten(a_left), flatten(b_top), flatten(b_left), flatten(peaks[0]), flatten(peaks[1])))
    field = jnp.stack([flow_rows.reshape(MESH_ROWS, MESH_COLS), flow_cols.reshape(MESH_ROWS, MESH_COLS)])
    for relax_step in range(RELAX):
        padded_field = jnp.pad(field, ((0, 0), (1, 1), (1, 1)))
        field = field + stiffness * (neighbours(padded_field) - 4.0 * field)
    return (field, runner.reshape(MESH_ROWS, MESH_COLS))
```

```python
import functools
import math

import jax
import jax.numpy as jnp
import numpy as np
from jax import lax
from jax.experimental import pallas as pl
from jax.experimental.pallas import tpu as pltpu
from jax.sharding import PartitionSpec as P

PATCH = 160
STRIDE = 8
RELAX = 2
WIDE = 256
HALF_LANES = 128
FREQS = PATCH // 2 + 1
GROUPS = 11
PAIRED = 16 * GROUPS
BIG = 3.0e38

sharpness = 80.0
epsilon = 1e-06
stiffness = 0.24
centre_reach = 2


def dft_tables():
    steps = np.arange(PATCH)
    angles = 2.0 * math.pi * ((steps[:, None] * steps[None, :FREQS]) % PATCH) / PATCH
    return (
        np.cos(angles).astype(jnp.bfloat16).astype(np.float32),
        np.sin(angles).astype(jnp.bfloat16).astype(np.float32),
    )


def kernel_tables():
    cosine, sine = dft_tables()
    weights = np.full((FREQS,), 2.0, np.float32)
    weights[0] = weights[-1] = 1.0
    across = np.zeros((WIDE, WIDE), np.float32)
    across[:PATCH, :FREQS] = cosine
    across[:PATCH, HALF_LANES : HALF_LANES + FREQS] = sine
    back_across = np.zeros((WIDE, WIDE), np.float32)
    back_across[:FREQS, :PATCH] = 0.5 * (cosine * weights).T
    back_across[HALF_LANES : HALF_LANES + FREQS, :PATCH] = 0.5 * (sine * weights).T
    down = np.zeros((PAIRED, PATCH), np.float32)
    back_down = np.zeros((PATCH, PAIRED), np.float32)
    for freq in range(FREQS):
        row = 16 * (freq // 8) + freq % 8
        down[row] = cosine[:, freq]
        down[row + 8] = sine[:, freq]
        back_down[:, row] = cosine[:, freq] * weights[freq]
        back_down[:, row + 8] = sine[:, freq] * weights[freq]
    caps = np.full((2 * PATCH, HALF_LANES), BIG, np.float32)
    for row in range(2 * PATCH):
        if row % PATCH <= 2 * centre_reach:
            caps[row] = -BIG
    return (
        jnp.asarray(across, jnp.bfloat16),
        jnp.asarray(down, jnp.bfloat16),
        jnp.asarray(back_down, jnp.bfloat16),
        jnp.asarray(back_across, jnp.bfloat16),
        jnp.asarray(caps, jnp.float32),
    )


B_BLOCK, B_ROW, B_ROW_REST, B_COL_REST = 0, 1, 2, 3
A_BLOCK, A_ROW, A_ROW_REST, A_COL_REST = 4, 5, 6, 7
NEAR_ROW, NEAR_COL = 8, 9
FIELDS = 10
STAGES = 6


def correlate_kernel(
    capacity,
    count_ref,
    items_ref,
    a_ref,
    b_ref,
    across_ref,
    down_ref,
    back_down_ref,
    back_across_ref,
    caps_ref,
    out_ref,
    *scratch,
):
    patches, halves, crosses, inverses, corrs, maxima = (
        scratch[0:2],
        scratch[2:4],
        scratch[4:6],
        scratch[6:8],
        scratch[8:12],
        scratch[12:14],
    )
    energies, scales, totals, row_moments, col_moments, runners = scratch[14:20]
    count = count_ref[0]

    def at(step, stage):
        return jnp.clip(step - stage, 0, capacity - 1)

    def extract(source, block, row, row_rest, col_rest, target, base):
        lanes = lax.broadcasted_iota(jnp.int32, (PATCH, WIDE), 1)
        low = source[block, pl.ds(row, PATCH), :]
        high = source[block + 1, pl.ds(row, PATCH), :]
        body = jnp.where(lanes >= col_rest, low, high)
        low = source[block, pl.ds(row + PATCH, 16), :]
        high = source[block + 1, pl.ds(row + PATCH, 16), :]
        tail = jnp.where(lanes[:16] >= col_rest, low, high)
        rows = lax.broadcasted_iota(jnp.int32, (16, WIDE), 0)
        head = jnp.where(rows >= row_rest, body[:16], tail)
        target[base : base + 16, :] = head
        target[base + 16 : base + PATCH, :] = body[16:]
        head = head.astype(jnp.float32)
        body = body[16:].astype(jnp.float32)
        total = jnp.sum((head * head).reshape(2, 8, WIDE), axis=0) + jnp.sum(
            (body * body).reshape(PATCH // 8 - 2, 8, WIDE), axis=0
        )
        return total[:, :HALF_LANES] + total[:, HALF_LANES:]

    def stage_patch(step, now):
        item = at(step, 0)
        slot = item % 8
        for which, source, base, fields in (
            (0, a_ref, 0, (A_BLOCK, A_ROW, A_ROW_REST, A_COL_REST)),
            (1, b_ref, PATCH, (B_BLOCK, B_ROW, B_ROW_REST, B_COL_REST)),
        ):
            block, row, row_rest, col_rest = (items_ref[field, item] for field in fields)
            energies[slot, which] = extract(
                source, block, pl.multiple_of(row, 16), row_rest, col_rest, patches[now], base
            )

    def stage_half(step, was, now):
        item = at(step, 1)
        slot = item % 8
        half = jnp.dot(patches[was][...], across_ref[...], preferred_element_type=jnp.float32)
        halves[now][...] = half.astype(jnp.bfloat16)
        mean_a = jnp.sum(energies[slot, 0], keepdims=True) * (1.0 / (PATCH * PATCH))
        mean_b = jnp.sum(energies[slot, 1], keepdims=True) * (1.0 / (PATCH * PATCH))
        scale = 1.0 / (
            float(PATCH**4) * jnp.sqrt(mean_a + epsilon) * jnp.sqrt(mean_b + epsilon)
        )
        scales[slot] = jnp.broadcast_to(scale, (8, HALF_LANES))

    def stage_cross(step, was, now):
        down = down_ref[...]
        spec_a = jnp.dot(down, halves[was][:PATCH, :], preferred_element_type=jnp.float32)
        spec_b = jnp.dot(down, halves[was][PATCH:, :], preferred_element_type=jnp.float32)

        def sides(spec, group):
            cc = spec[16 * group : 16 * group + 8, :HALF_LANES]
            cs = spec[16 * group : 16 * group + 8, HALF_LANES:]
            sc = spec[16 * group + 8 : 16 * group + 16, :HALF_LANES]
            ss = spec[16 * group + 8 : 16 * group + 16, HALF_LANES:]
            return cc - ss, sc + cs, cc + ss, sc - cs

        for group in range(GROUPS):
            a_pr, a_pi, a_mr, a_mi = sides(spec_a, group)
            b_pr, b_pi, b_mr, b_mi = sides(spec_b, group)
            pr = a_pr * b_pr + a_pi * b_pi
            pi = a_pr * b_pi - a_pi * b_pr
            mr = a_mr * b_mr + a_mi * b_mi
            mi = a_mr * b_mi - a_mi * b_mr
            upper = jnp.concatenate([pr + mr, pi - mi], axis=1)
            lower = jnp.concatenate([pi + mi, mr - pr], axis=1)
            crosses[now][16 * group : 16 * group + 16, :] = jnp.concatenate(
                [upper, lower], axis=0
            ).astype(jnp.bfloat16)

    def stage_inverse(step, was, now):
        inverse = jnp.dot(
            back_down_ref[...], crosses[was][...], preferred_element_type=jnp.float32
        )
        inverses[now][...] = inverse.astype(jnp.bfloat16)

    def stage_correlation(step, was, now):
        item = at(step, 4)
        corr = jnp.dot(
            inverses[was][...], back_across_ref[...], preferred_element_type=jnp.float32
        )
        for part in range(2):
            side = corr[:, part * HALF_LANES : (part + 1) * HALF_LANES]
            corrs[2 * now + part][:PATCH, :] = side
            corrs[2 * now + part][PATCH:, :] = side[:8]
        caps = caps_ref[pl.ds(PATCH - items_ref[NEAR_ROW, item], PATCH), :]
        left = jnp.max(
            jnp.minimum(corr[:, :HALF_LANES], caps).reshape(PATCH // 8, 8, HALF_LANES), axis=0
        )
        right = jnp.max(
            jnp.minimum(corr[:, HALF_LANES:], caps).reshape(PATCH // 8, 8, HALF_LANES), axis=0
        )
        lanes = lax.broadcasted_iota(jnp.int32, (8, HALF_LANES), 1)
        maxima[now][...] = jnp.maximum(
            left, jnp.where(lanes < PATCH - HALF_LANES, right, -BIG)
        )

    def stage_near(step, was):
        item = at(step, 5)
        scale = scales[item % 8]
        near_row = items_ref[NEAR_ROW, item]
        near_col = items_ref[NEAR_COL, item]
        rows = lax.broadcasted_iota(jnp.int32, (8, HALF_LANES), 0)
        lanes = lax.broadcasted_iota(jnp.int32, (8, HALF_LANES), 1)
        shift_rows = (rows - centre_reach).astype(jnp.float32)
        row_near = rows <= 2 * centre_reach
        total, row_moment, col_moment = 0.0, 0.0, 0.0
        best = maxima[was][...]
        for part in range(2):
            values = corrs[2 * was + part][pl.ds(near_row, 8), :]
            place = lanes + part * HALF_LANES
            shift = place - near_col
            shift = jnp.where(shift >= PATCH // 2, shift - PATCH, shift)
            shift = jnp.where(shift < -(PATCH // 2), shift + PATCH, shift)
            inside = row_near & (place < PATCH)
            close = jnp.abs(shift) <= centre_reach
            weight = jnp.where(
                inside & close, jnp.exp(sharpness * (values * scale)), 0.0
            )
            total = total + weight
            row_moment = row_moment + weight * shift_rows
            col_moment = col_moment + weight * shift.astype(jnp.float32)
            best = jnp.maximum(
                best, jnp.where(inside & jnp.logical_not(close), values, -BIG)
            )
        totals[pl.ds(item, 1), :] = jnp.sum(total, axis=0, keepdims=True)
        row_moments[pl.ds(item, 1), :] = jnp.sum(row_moment, axis=0, keepdims=True)
        col_moments[pl.ds(item, 1), :] = jnp.sum(col_moment, axis=0, keepdims=True)
        runners[pl.ds(item, 1), :] = jnp.max(best * scale, axis=0, keepdims=True)

    @pl.loop(0, (count + STAGES) // 2)
    def _(pair):
        for now in range(2):
            step = 2 * pair + now
            stage_near(step, 1 - now)
            stage_correlation(step, 1 - now, now)
            stage_inverse(step, 1 - now, now)
            stage_cross(step, 1 - now, now)
            stage_half(step, 1 - now, now)
            stage_patch(step, now)

    lanes = lax.broadcasted_iota(jnp.int32, (capacity, HALF_LANES), 1)
    used = lax.broadcasted_iota(jnp.int32, (capacity, HALF_LANES), 0) < count
    total = jnp.sum(totals[...], axis=1, keepdims=True)
    rows = jnp.sum(row_moments[...], axis=1, keepdims=True) / total
    cols = jnp.sum(col_moments[...], axis=1, keepdims=True) / total
    best = jnp.maximum(jnp.max(runners[...], axis=1, keepdims=True), -2.0)
    result = jnp.where(lanes == 0, rows, jnp.where(lanes == 1, cols, best))
    out_ref[...] = jnp.where(used & (lanes < 3), result, 0.0)


def correlate(count, items, a_blocks, b_blocks):
    capacity = items.shape[1]
    pair = lambda rows, dtype: [pltpu.VMEM((rows, WIDE), dtype)] * 2
    vmem = pl.BlockSpec(memory_space=pltpu.VMEM)
    smem = pl.BlockSpec(memory_space=pltpu.SMEM)
    rows = pltpu.VMEM((capacity, HALF_LANES), jnp.float32)
    return pl.pallas_call(
        functools.partial(correlate_kernel, capacity),
        out_shape=jax.ShapeDtypeStruct((capacity, HALF_LANES), jnp.float32),
        in_specs=[smem, smem] + [vmem] * 7,
        out_specs=vmem,
        scratch_shapes=pair(2 * PATCH, jnp.bfloat16)
        + pair(2 * PATCH, jnp.bfloat16)
        + pair(PAIRED, jnp.bfloat16)
        + pair(PATCH, jnp.bfloat16)
        + [pltpu.VMEM((PATCH + 8, HALF_LANES), jnp.float32)] * 4
        + [pltpu.VMEM((8, HALF_LANES), jnp.float32)] * 2
        + [
            pltpu.VMEM((8, 2, 8, HALF_LANES), jnp.float32),
            pltpu.VMEM((8, 8, HALF_LANES), jnp.float32),
        ]
        + [rows] * 4,
        compiler_params=pltpu.CompilerParams(vmem_limit_bytes=40 * 1024 * 1024),
    )(count, items, a_blocks, b_blocks, *kernel_tables())


def column_blocks(image, front, rows, blocks):
    height, breadth = image.shape
    top = rows[0]
    image = jnp.pad(
        image,
        ((top, rows[1]), (front * PATCH, (blocks - front) * PATCH - breadth)),
    )
    image = image.reshape(height + sum(rows), blocks, PATCH).transpose(1, 0, 2)
    return jnp.pad(image, ((0, 0), (0, 0), (0, WIDE - PATCH)))


def per_device(a_window, b_section, owners, pos_rows, pos_cols, peaks):
    node_rows, node_cols = pos_rows.shape
    nodes = node_rows * node_cols
    n_row, n_col = lax.axis_size("row"), lax.axis_size("col")
    devices = n_row * n_col
    me_row, me_col = lax.axis_index("row"), lax.axis_index("col")
    me = me_row * n_col + me_col
    share = max(2, (nodes * 8 // 5 + devices - 1) // devices)
    capacity = share * devices
    half_patch = PATCH // 2
    tile_rows, tile_cols = b_section.shape
    a_rows, a_cols = a_window.shape

    b_blocks = column_blocks(b_section, 0, (0, 16), -(-tile_cols // PATCH))

    fields = jnp.stack(
        [
            owners.reshape(nodes),
            pos_rows.reshape(nodes) // 16,
            pos_rows.reshape(nodes) % 16,
            pos_cols.reshape(nodes) // 16,
            pos_cols.reshape(nodes) % 16,
            peaks[0].reshape(nodes),
            peaks[1].reshape(nodes),
            jnp.zeros((nodes,), jnp.int32),
        ]
    ).astype(jnp.bfloat16)
    fields = jnp.pad(fields, ((0, 0), (0, WIDE - nodes))).reshape(16, HALF_LANES)
    sent = jnp.concatenate([a_window, fields], axis=0)
    everyone = lax.all_gather(sent, ("row", "col"))

    window = everyone[:, :a_rows].reshape(n_row, n_col, a_rows, a_cols)
    window = window.transpose(0, 2, 1, 3).reshape(n_row * a_rows, n_col * a_cols)
    a_count = (n_col * a_cols + 76) // PATCH + 2
    a_blocks = column_blocks(window, 1, (half_patch, half_patch), a_count)

    known = everyone[:, a_rows:].reshape(devices, 8, WIDE)[:, :, :nodes]
    mine = (known[:, 0] == me.astype(jnp.bfloat16)).astype(jnp.float32)
    within = jnp.dot(
        mine, jnp.triu(jnp.ones((nodes, nodes), jnp.float32), 1)
    )
    loads = jnp.sum(mine, axis=1)
    before = jnp.sum(
        jnp.where(jnp.tril(jnp.ones((devices, devices), bool), -1), loads[None, :], 0.0), axis=1
    )
    count = jnp.sum(loads).astype(jnp.int32).reshape(1)
    slots = jnp.where(mine > 0, before[:, None] + within, -1.0).astype(jnp.int32)
    slots = slots.reshape(devices * nodes)
    chosen = (
        slots[None, :] == jnp.arange(capacity, dtype=jnp.int32)[:, None]
    ).astype(jnp.bfloat16)
    device_of = jnp.broadcast_to(jnp.arange(devices)[:, None], (devices, nodes))
    node_of = jnp.broadcast_to(jnp.arange(nodes)[None, :], (devices, nodes))
    listed = jnp.concatenate(
        [
            known.transpose(1, 0, 2)[:7],
            device_of[None].astype(jnp.bfloat16),
            node_of[None].astype(jnp.bfloat16),
        ],
        axis=0,
    ).reshape(9, devices * nodes)
    taken = lax.dot_general(
        listed, chosen, (((1,), (1,)), ((), ())), preferred_element_type=jnp.float32
    ).astype(jnp.int32)
    valid = jnp.arange(capacity) < count[0]
    b_top = jnp.where(valid, taken[1] * 16 + taken[2] - half_patch, 0)
    b_left = jnp.where(valid, taken[3] * 16 + taken[4] - half_patch, 0)
    a_top = (taken[7] // n_col * node_rows + taken[8] // node_cols) * STRIDE + STRIDE // 2
    a_left = (
        (taken[7] % n_col * node_cols + taken[8] % node_cols) * STRIDE
        + STRIDE // 2
        + half_patch
    )
    near_row = (taken[5] + b_top % 16 - a_top % 16 - centre_reach + 2 * PATCH) % PATCH
    near_col = (taken[6] + b_left % PATCH - a_left % PATCH + 2 * PATCH) % PATCH
    items = jnp.stack(
        [
            b_left // PATCH,
            b_top // 16 * 16,
            b_top % 16,
            b_left % PATCH,
            a_left // PATCH,
            a_top // 16 * 16,
            a_top % 16,
            a_left % PATCH,
            near_row,
            near_col,
        ]
    )
    result = correlate(count, items, a_blocks, b_blocks)[:, :3]

    spread = lax.dot_general(
        result,
        chosen.astype(jnp.float32),
        (((0,), (0,)), ((), ())),
        precision=lax.Precision.HIGHEST,
    )
    spread = lax.psum(spread, ("row", "col"))
    spread = spread.reshape(3, n_row, n_col, node_rows, node_cols)
    runner = lax.dynamic_slice(
        spread, (2, me_row, me_col, 0, 0), (1, 1, 1, node_rows, node_cols)
    ).reshape(node_rows, node_cols)
    offsets = known[:, 5:7].astype(jnp.float32).transpose(1, 0, 2)
    field = spread[:2] + offsets.reshape(2, n_row, n_col, node_rows, node_cols)
    height, breadth = n_row * node_rows, n_col * node_cols
    field = field.transpose(0, 1, 3, 2, 4).reshape(2, height, breadth)
    field = jnp.pad(field, ((0, 0), (RELAX, RELAX), (RELAX, RELAX)))
    field = lax.dynamic_slice(
        field,
        (0, me_row * node_rows, me_col * node_cols),
        (2, node_rows + 2 * RELAX, node_cols + 2 * RELAX),
    )
    for step in range(RELAX):
        reach = RELAX - 1 - step
        centre = field[:, 1:-1, 1:-1]
        around = (
            field[:, 2:, 1:-1] + field[:, :-2, 1:-1] + field[:, 1:-1, 2:] + field[:, 1:-1, :-2]
        )
        field = centre + stiffness * (around - 4.0 * centre)
        rows = me_row * node_rows - reach + jnp.arange(node_rows + 2 * reach)
        cols = me_col * node_cols - reach + jnp.arange(node_cols + 2 * reach)
        inside = ((rows >= 0) & (rows < height))[:, None] & ((cols >= 0) & (cols < breadth))[None]
        field = jnp.where(inside[None], field, 0.0)
    return (field, runner)


def solution(mesh):
    placed = (
        P("row", "col"),
        P("row", "col"),
        P("row", "col", None, None, None),
        P("row", "col"),
        P("row", "col"),
        P(None, "row", "col"),
    )
    return jax.shard_map(
        per_device,
        mesh=mesh,
        in_specs=placed,
        out_specs=(P(None, "row", "col"), P("row", "col")),
        check_vma=False,
    )
```

```python
import functools
import math

import jax
import jax.numpy as jnp
import numpy as np
from jax import lax
from jax.experimental import pallas as pl
from jax.experimental.pallas import tpu as pltpu
from jax.sharding import PartitionSpec as P

PATCH = 160
STRIDE = 8
RELAX = 2
WIDE = 256
HALF_LANES = 128
FREQS = PATCH // 2 + 1
GROUPS = 11
PAIRED = 16 * GROUPS
BIG = 3.0e38

sharpness = 80.0
epsilon = 1e-06
stiffness = 0.24
centre_reach = 2


def dft_tables():
    steps = np.arange(PATCH)
    angles = 2.0 * math.pi * ((steps[:, None] * steps[None, :FREQS]) % PATCH) / PATCH
    return (
        np.cos(angles).astype(jnp.bfloat16).astype(np.float32),
        np.sin(angles).astype(jnp.bfloat16).astype(np.float32),
    )


def kernel_tables():
    cosine, sine = dft_tables()
    weights = np.full((FREQS,), 2.0, np.float32)
    weights[0] = weights[-1] = 1.0
    across = np.zeros((WIDE, WIDE), np.float32)
    across[:PATCH, :FREQS] = cosine
    across[:PATCH, HALF_LANES : HALF_LANES + FREQS] = sine
    back_across = np.zeros((WIDE, WIDE), np.float32)
    back_across[:FREQS, :PATCH] = 0.5 * (cosine * weights).T
    back_across[HALF_LANES : HALF_LANES + FREQS, :PATCH] = 0.5 * (sine * weights).T
    down = np.zeros((PAIRED, PATCH), np.float32)
    back_down = np.zeros((PATCH, PAIRED), np.float32)
    for freq in range(FREQS):
        row = 16 * (freq // 8) + freq % 8
        down[row] = cosine[:, freq]
        down[row + 8] = sine[:, freq]
        back_down[:, row] = cosine[:, freq] * weights[freq]
        back_down[:, row + 8] = sine[:, freq] * weights[freq]
    caps = np.full((2 * PATCH, HALF_LANES), BIG, np.float32)
    for row in range(2 * PATCH):
        if row % PATCH <= 2 * centre_reach:
            caps[row] = -BIG
    return (
        jnp.asarray(across, jnp.bfloat16),
        jnp.asarray(down, jnp.bfloat16),
        jnp.asarray(back_down, jnp.bfloat16),
        jnp.asarray(back_across, jnp.bfloat16),
        jnp.asarray(caps, jnp.float32),
    )


B_BLOCK, B_ROW, B_ROW_REST, B_COL_REST = 0, 1, 2, 3
A_BLOCK, A_ROW, A_ROW_REST, A_COL_REST = 4, 5, 6, 7
NEAR_ROW, NEAR_COL = 8, 9
FIELDS = 10
STAGES = 6


def cut(strip, start):
    if start >= strip.shape[1]:
        return jnp.zeros((strip.shape[0], WIDE), strip.dtype)
    piece = strip[:, start : min(start + PATCH, strip.shape[1])]
    gap = jnp.zeros((strip.shape[0], WIDE - piece.shape[1]), strip.dtype)
    return jnp.concatenate([piece, gap], axis=1)


def correlate_kernel(
    capacity,
    grid,
    count_ref,
    items_ref,
    everyone_ref,
    tile_ref,
    across_ref,
    down_ref,
    back_down_ref,
    back_across_ref,
    caps_ref,
    out_ref,
    *scratch,
):
    patches, halves, crosses, inverses, corrs, maxima = (
        scratch[0:2],
        scratch[2:4],
        scratch[4:6],
        scratch[6:8],
        scratch[8:12],
        scratch[12:14],
    )
    energies, scales, totals, row_moments, col_moments, runners, a_ref, b_ref = scratch[14:22]
    count = count_ref[0]
    n_row, n_col, a_rows = grid

    height = tile_ref.shape[0]

    @pl.loop(0, height // 128)
    def _(chunk):
        place = pl.ds(pl.multiple_of(chunk * 128, 128), 128)
        strip = tile_ref[place, :]
        for block in range(b_ref.shape[0]):
            b_ref[block, place, :] = cut(strip, block * PATCH)

    b_ref[:, height:, :] = jnp.zeros((b_ref.shape[0], 16, WIDE), jnp.bfloat16)
    a_ref[0] = jnp.zeros(a_ref.shape[1:], jnp.bfloat16)
    rim = jnp.zeros((a_ref.shape[0], PATCH // 2, WIDE), jnp.bfloat16)
    a_ref[:, : PATCH // 2, :] = rim
    a_ref[:, a_ref.shape[1] - PATCH // 2 :, :] = rim

    @pl.loop(0, n_row)
    def _(row):
        strip = jnp.concatenate(
            [everyone_ref[row * n_col + col, :a_rows, :] for col in range(n_col)], axis=1
        )
        place = pl.ds(pl.multiple_of(PATCH // 2 + row * a_rows, 16), a_rows)
        for block in range(1, a_ref.shape[0]):
            a_ref[block, place, :] = cut(strip, (block - 1) * PATCH)

    def at(step, stage):
        return jnp.clip(step - stage, 0, capacity - 1)

    def extract(source, block, row, row_rest, col_rest, target, base):
        lanes = lax.broadcasted_iota(jnp.int32, (PATCH, WIDE), 1)
        low = source[block, pl.ds(row, PATCH), :]
        high = source[block + 1, pl.ds(row, PATCH), :]
        body = jnp.where(lanes >= col_rest, low, high)
        low = source[block, pl.ds(row + PATCH, 16), :]
        high = source[block + 1, pl.ds(row + PATCH, 16), :]
        tail = jnp.where(lanes[:16] >= col_rest, low, high)
        rows = lax.broadcasted_iota(jnp.int32, (16, WIDE), 0)
        head = jnp.where(rows >= row_rest, body[:16], tail)
        target[base : base + 16, :] = head
        target[base + 16 : base + PATCH, :] = body[16:]
        head = head.astype(jnp.float32)
        body = body[16:].astype(jnp.float32)
        total = jnp.sum((head * head).reshape(2, 8, WIDE), axis=0) + jnp.sum(
            (body * body).reshape(PATCH // 8 - 2, 8, WIDE), axis=0
        )
        return total[:, :HALF_LANES] + total[:, HALF_LANES:]

    def stage_patch(step, now):
        item = at(step, 0)
        slot = item % 8
        for which, source, base, fields in (
            (0, a_ref, 0, (A_BLOCK, A_ROW, A_ROW_REST, A_COL_REST)),
            (1, b_ref, PATCH, (B_BLOCK, B_ROW, B_ROW_REST, B_COL_REST)),
        ):
            block, row, row_rest, col_rest = (items_ref[field, item] for field in fields)
            energies[slot, which] = extract(
                source, block, pl.multiple_of(row, 16), row_rest, col_rest, patches[now], base
            )

    def stage_half(step, was, now):
        item = at(step, 1)
        slot = item % 8
        half = jnp.dot(patches[was][...], across_ref[...], preferred_element_type=jnp.float32)
        halves[now][...] = half.astype(jnp.bfloat16)
        mean_a = jnp.sum(energies[slot, 0], keepdims=True) * (1.0 / (PATCH * PATCH))
        mean_b = jnp.sum(energies[slot, 1], keepdims=True) * (1.0 / (PATCH * PATCH))
        scale = 1.0 / (
            float(PATCH**4) * jnp.sqrt(mean_a + epsilon) * jnp.sqrt(mean_b + epsilon)
        )
        scales[slot] = jnp.broadcast_to(scale, (8, HALF_LANES))

    def stage_cross(step, was, now):
        down = down_ref[...]
        spec_a = jnp.dot(down, halves[was][:PATCH, :], preferred_element_type=jnp.float32)
        spec_b = jnp.dot(down, halves[was][PATCH:, :], preferred_element_type=jnp.float32)

        def sides(spec, group):
            cc = spec[16 * group : 16 * group + 8, :HALF_LANES]
            cs = spec[16 * group : 16 * group + 8, HALF_LANES:]
            sc = spec[16 * group + 8 : 16 * group + 16, :HALF_LANES]
            ss = spec[16 * group + 8 : 16 * group + 16, HALF_LANES:]
            return cc - ss, sc + cs, cc + ss, sc - cs

        for group in range(GROUPS):
            a_pr, a_pi, a_mr, a_mi = sides(spec_a, group)
            b_pr, b_pi, b_mr, b_mi = sides(spec_b, group)
            pr = a_pr * b_pr + a_pi * b_pi
            pi = a_pr * b_pi - a_pi * b_pr
            mr = a_mr * b_mr + a_mi * b_mi
            mi = a_mr * b_mi - a_mi * b_mr
            upper = jnp.concatenate([pr + mr, pi - mi], axis=1)
            lower = jnp.concatenate([pi + mi, mr - pr], axis=1)
            crosses[now][16 * group : 16 * group + 16, :] = jnp.concatenate(
                [upper, lower], axis=0
            ).astype(jnp.bfloat16)

    def stage_inverse(step, was, now):
        inverse = jnp.dot(
            back_down_ref[...], crosses[was][...], preferred_element_type=jnp.float32
        )
        inverses[now][...] = inverse.astype(jnp.bfloat16)

    def stage_correlation(step, was, now):
        item = at(step, 4)
        corr = jnp.dot(
            inverses[was][...], back_across_ref[...], preferred_element_type=jnp.float32
        )
        for part in range(2):
            side = corr[:, part * HALF_LANES : (part + 1) * HALF_LANES]
            corrs[2 * now + part][:PATCH, :] = side
            corrs[2 * now + part][PATCH:, :] = side[:8]
        caps = caps_ref[pl.ds(PATCH - items_ref[NEAR_ROW, item], PATCH), :]
        left = jnp.max(
            jnp.minimum(corr[:, :HALF_LANES], caps).reshape(PATCH // 8, 8, HALF_LANES), axis=0
        )
        right = jnp.max(
            jnp.minimum(corr[:, HALF_LANES:], caps).reshape(PATCH // 8, 8, HALF_LANES), axis=0
        )
        lanes = lax.broadcasted_iota(jnp.int32, (8, HALF_LANES), 1)
        maxima[now][...] = jnp.maximum(
            left, jnp.where(lanes < PATCH - HALF_LANES, right, -BIG)
        )

    def stage_near(step, was):
        item = at(step, 5)
        scale = scales[item % 8]
        near_row = items_ref[NEAR_ROW, item]
        near_col = items_ref[NEAR_COL, item]
        rows = lax.broadcasted_iota(jnp.int32, (8, HALF_LANES), 0)
        lanes = lax.broadcasted_iota(jnp.int32, (8, HALF_LANES), 1)
        shift_rows = (rows - centre_reach).astype(jnp.float32)
        row_near = rows <= 2 * centre_reach
        total, row_moment, col_moment = 0.0, 0.0, 0.0
        best = maxima[was][...]
        for part in range(2):
            values = corrs[2 * was + part][pl.ds(near_row, 8), :]
            place = lanes + part * HALF_LANES
            shift = place - near_col
            shift = jnp.where(shift >= PATCH // 2, shift - PATCH, shift)
            shift = jnp.where(shift < -(PATCH // 2), shift + PATCH, shift)
            inside = row_near & (place < PATCH)
            close = jnp.abs(shift) <= centre_reach
            weight = jnp.where(
                inside & close, jnp.exp(sharpness * (values * scale)), 0.0
            )
            total = total + weight
            row_moment = row_moment + weight * shift_rows
            col_moment = col_moment + weight * shift.astype(jnp.float32)
            best = jnp.maximum(
                best, jnp.where(inside & jnp.logical_not(close), values, -BIG)
            )
        totals[pl.ds(item, 1), :] = jnp.sum(total, axis=0, keepdims=True)
        row_moments[pl.ds(item, 1), :] = jnp.sum(row_moment, axis=0, keepdims=True)
        col_moments[pl.ds(item, 1), :] = jnp.sum(col_moment, axis=0, keepdims=True)
        runners[pl.ds(item, 1), :] = jnp.max(best * scale, axis=0, keepdims=True)

    @pl.loop(0, (count + STAGES) // 2)
    def _(pair):
        for now in range(2):
            step = 2 * pair + now
            stage_near(step, 1 - now)
            stage_correlation(step, 1 - now, now)
            stage_inverse(step, 1 - now, now)
            stage_cross(step, 1 - now, now)
            stage_half(step, 1 - now, now)
            stage_patch(step, now)

    lanes = lax.broadcasted_iota(jnp.int32, (capacity, HALF_LANES), 1)
    used = lax.broadcasted_iota(jnp.int32, (capacity, HALF_LANES), 0) < count
    total = jnp.sum(totals[...], axis=1, keepdims=True)
    rows = jnp.sum(row_moments[...], axis=1, keepdims=True) / total
    cols = jnp.sum(col_moments[...], axis=1, keepdims=True) / total
    best = jnp.maximum(jnp.max(runners[...], axis=1, keepdims=True), -2.0)
    result = jnp.where(lanes == 0, rows, jnp.where(lanes == 1, cols, best))
    out_ref[...] = jnp.where(used & (lanes < 3), result, 0.0)


def correlate(count, items, everyone, tile, grid):
    capacity = items.shape[1]
    n_row, n_col, a_rows = grid
    a_blocks = (n_col * everyone.shape[2] + 76) // PATCH + 2
    b_blocks = -(-tile.shape[1] // PATCH)
    pair = lambda rows, dtype: [pltpu.VMEM((rows, WIDE), dtype)] * 2
    vmem = pl.BlockSpec(memory_space=pltpu.VMEM)
    smem = pl.BlockSpec(memory_space=pltpu.SMEM)
    rows = pltpu.VMEM((capacity, HALF_LANES), jnp.float32)
    return pl.pallas_call(
        functools.partial(correlate_kernel, capacity, grid),
        out_shape=jax.ShapeDtypeStruct((capacity, HALF_LANES), jnp.float32),
        in_specs=[smem, smem] + [vmem] * 7,
        out_specs=vmem,
        scratch_shapes=pair(2 * PATCH, jnp.bfloat16)
        + pair(2 * PATCH, jnp.bfloat16)
        + pair(PAIRED, jnp.bfloat16)
        + pair(PATCH, jnp.bfloat16)
        + [pltpu.VMEM((PATCH + 8, HALF_LANES), jnp.float32)] * 4
        + [pltpu.VMEM((8, HALF_LANES), jnp.float32)] * 2
        + [
            pltpu.VMEM((8, 2, 8, HALF_LANES), jnp.float32),
            pltpu.VMEM((8, 8, HALF_LANES), jnp.float32),
        ]
        + [rows] * 4
        + [
            pltpu.VMEM((a_blocks, n_row * a_rows + PATCH, WIDE), jnp.bfloat16),
            pltpu.VMEM((b_blocks, tile.shape[0] + 16, WIDE), jnp.bfloat16),
        ],
        compiler_params=pltpu.CompilerParams(vmem_limit_bytes=40 * 1024 * 1024),
    )(count, items, everyone, tile, *kernel_tables())


def per_device(a_window, b_section, owners, pos_rows, pos_cols, peaks):
    node_rows, node_cols = pos_rows.shape
    nodes = node_rows * node_cols
    n_row, n_col = lax.axis_size("row"), lax.axis_size("col")
    devices = n_row * n_col
    me_row, me_col = lax.axis_index("row"), lax.axis_index("col")
    me = me_row * n_col + me_col
    share = max(2, (nodes * 8 // 5 + devices - 1) // devices)
    capacity = share * devices
    half_patch = PATCH // 2
    a_rows, a_cols = a_window.shape

    fields = jnp.stack(
        [
            owners.reshape(nodes),
            pos_rows.reshape(nodes) // 16,
            pos_rows.reshape(nodes) % 16,
            pos_cols.reshape(nodes) // 16,
            pos_cols.reshape(nodes) % 16,
            peaks[0].reshape(nodes),
            peaks[1].reshape(nodes),
            jnp.zeros((nodes,), jnp.int32),
        ]
    ).astype(jnp.bfloat16)
    fields = jnp.pad(fields, ((0, 0), (0, WIDE - nodes))).reshape(16, HALF_LANES)
    sent = jnp.concatenate([a_window, fields], axis=0)
    everyone = lax.all_gather(lax.all_gather(sent, "col"), "row")
    everyone = everyone.reshape(devices, a_rows + 16, a_cols)

    known = everyone[:, a_rows:].reshape(devices, 8, WIDE)[:, :, :nodes]
    mine = (known[:, 0] == me.astype(jnp.bfloat16)).astype(jnp.float32)
    within = jnp.dot(
        mine, jnp.triu(jnp.ones((nodes, nodes), jnp.float32), 1)
    )
    loads = jnp.sum(mine, axis=1)
    before = jnp.sum(
        jnp.where(jnp.tril(jnp.ones((devices, devices), bool), -1), loads[None, :], 0.0), axis=1
    )
    count = jnp.sum(loads).astype(jnp.int32).reshape(1)
    slots = jnp.where(mine > 0, before[:, None] + within, -1.0).astype(jnp.int32)
    slots = slots.reshape(devices * nodes)
    chosen = (
        slots[None, :] == jnp.arange(capacity, dtype=jnp.int32)[:, None]
    ).astype(jnp.bfloat16)
    device_of = jnp.broadcast_to(jnp.arange(devices)[:, None], (devices, nodes))
    node_of = jnp.broadcast_to(jnp.arange(nodes)[None, :], (devices, nodes))
    listed = jnp.concatenate(
        [
            known.transpose(1, 0, 2)[:7],
            device_of[None].astype(jnp.bfloat16),
            node_of[None].astype(jnp.bfloat16),
        ],
        axis=0,
    ).reshape(9, devices * nodes)
    taken = lax.dot_general(
        listed, chosen, (((1,), (1,)), ((), ())), preferred_element_type=jnp.float32
    ).astype(jnp.int32)
    valid = jnp.arange(capacity) < count[0]
    b_top = jnp.where(valid, taken[1] * 16 + taken[2] - half_patch, 0)
    b_left = jnp.where(valid, taken[3] * 16 + taken[4] - half_patch, 0)
    a_top = (taken[7] // n_col * node_rows + taken[8] // node_cols) * STRIDE + STRIDE // 2
    a_left = (
        (taken[7] % n_col * node_cols + taken[8] % node_cols) * STRIDE
        + STRIDE // 2
        + half_patch
    )
    near_row = (taken[5] + b_top % 16 - a_top % 16 - centre_reach + 2 * PATCH) % PATCH
    near_col = (taken[6] + b_left % PATCH - a_left % PATCH + 2 * PATCH) % PATCH
    items = jnp.stack(
        [
            b_left // PATCH,
            b_top // 16 * 16,
            b_top % 16,
            b_left % PATCH,
            a_left // PATCH,
            a_top // 16 * 16,
            a_top % 16,
            a_left % PATCH,
            near_row,
            near_col,
        ]
    )
    result = correlate(count, items, everyone, b_section, (n_row, n_col, a_rows))[:, :3]

    height, breadth = n_row * node_rows, n_col * node_cols
    tall, broad = node_rows + 2 * RELAX, node_cols + 2 * RELAX
    lanes = -(-tall * broad // HALF_LANES) * HALF_LANES
    shape = (devices, lanes)
    device = lax.broadcasted_iota(jnp.int32, shape, 0)
    place = lax.broadcasted_iota(jnp.int32, shape, 1)
    row = device // n_col * node_rows + place // broad - RELAX
    col = device % n_col * node_cols + place % broad - RELAX
    real = (row >= 0) & (row < height) & (col >= 0) & (col < breadth) & (place < tall * broad)
    wanted = jnp.where(real, row * breadth + col, -1).reshape(devices * lanes)
    node = (taken[7] // n_col * node_rows + taken[8] // node_cols) * breadth + (
        taken[7] % n_col * node_cols + taken[8] % node_cols
    )
    node = jnp.where(valid, node, -2)
    spread = lax.dot_general(
        result,
        (node[:, None] == wanted[None, :]).astype(jnp.float32),
        (((0,), (0,)), ((), ())),
        precision=lax.Precision.HIGHEST,
    )
    spread = spread.reshape(3, devices, lanes).transpose(1, 0, 2)
    spread = lax.all_to_all(spread, ("row", "col"), split_axis=0, concat_axis=0, tiled=True)
    spread = jnp.sum(spread, axis=0)[:, : tall * broad].reshape(3, tall, broad)
    runner = spread[2, RELAX:-RELAX, RELAX:-RELAX]
    offsets = known[:, 5:7].astype(jnp.float32).reshape(n_row, n_col, 2, node_rows, node_cols)
    offsets = offsets.transpose(2, 0, 3, 1, 4).reshape(2, height, breadth)
    offsets = jnp.pad(offsets, ((0, 0), (RELAX, RELAX), (RELAX, RELAX)))
    field = spread[:2] + lax.dynamic_slice(
        offsets, (0, me_row * node_rows, me_col * node_cols), (2, tall, broad)
    )
    for step in range(RELAX):
        reach = RELAX - 1 - step
        centre = field[:, 1:-1, 1:-1]
        around = (
            field[:, 2:, 1:-1] + field[:, :-2, 1:-1] + field[:, 1:-1, 2:] + field[:, 1:-1, :-2]
        )
        field = centre + stiffness * (around - 4.0 * centre)
        rows = me_row * node_rows - reach + jnp.arange(node_rows + 2 * reach)
        cols = me_col * node_cols - reach + jnp.arange(node_cols + 2 * reach)
        inside = ((rows >= 0) & (rows < height))[:, None] & ((cols >= 0) & (cols < breadth))[None]
        field = jnp.where(inside[None], field, 0.0)
    return (field, runner)


def solution(mesh):
    placed = (
        P("row", "col"),
        P("row", "col"),
        P("row", "col", None, None, None),
        P("row", "col"),
        P("row", "col"),
        P(None, "row", "col"),
    )
    return jax.shard_map(
        per_device,
        mesh=mesh,
        in_specs=placed,
        out_specs=(P(None, "row", "col"), P("row", "col")),
        check_vma=False,
    )
```

```python
import functools
import math

import jax
import jax.numpy as jnp
import numpy as np
from jax import lax
from jax.experimental import pallas as pl
from jax.experimental.pallas import tpu as pltpu
from jax.sharding import PartitionSpec as P

PATCH = 160
STRIDE = 8
RELAX = 2
WIDE = 256
HALF_LANES = 128
FREQS = PATCH // 2 + 1
GROUPS = 11
PAIRED = 16 * GROUPS
BIG = 3.0e38

sharpness = 80.0
epsilon = 1e-06
stiffness = 0.24
centre_reach = 2


def dft_tables():
    steps = np.arange(PATCH)
    angles = 2.0 * math.pi * ((steps[:, None] * steps[None, :FREQS]) % PATCH) / PATCH
    return (
        np.cos(angles).astype(jnp.bfloat16).astype(np.float32),
        np.sin(angles).astype(jnp.bfloat16).astype(np.float32),
    )


def kernel_tables():
    cosine, sine = dft_tables()
    weights = np.full((FREQS,), 2.0, np.float32)
    weights[0] = weights[-1] = 1.0
    across = np.zeros((WIDE, WIDE), np.float32)
    across[:PATCH, :FREQS] = cosine
    across[:PATCH, HALF_LANES : HALF_LANES + FREQS] = sine
    back_across = np.zeros((WIDE, WIDE), np.float32)
    back_across[:FREQS, :PATCH] = 0.5 * (cosine * weights).T
    back_across[HALF_LANES : HALF_LANES + FREQS, :PATCH] = 0.5 * (sine * weights).T
    down = np.zeros((PAIRED, PATCH), np.float32)
    back_down = np.zeros((PATCH, PAIRED), np.float32)
    for freq in range(FREQS):
        row = 16 * (freq // 8) + freq % 8
        down[row] = cosine[:, freq]
        down[row + 8] = sine[:, freq]
        back_down[:, row] = cosine[:, freq] * weights[freq]
        back_down[:, row + 8] = sine[:, freq] * weights[freq]
    caps = np.full((2 * PATCH, HALF_LANES), BIG, np.float32)
    for row in range(2 * PATCH):
        if row % PATCH <= 2 * centre_reach:
            caps[row] = -BIG
    return (
        jnp.asarray(across, jnp.bfloat16),
        jnp.asarray(down, jnp.bfloat16),
        jnp.asarray(back_down, jnp.bfloat16),
        jnp.asarray(back_across, jnp.bfloat16),
        jnp.asarray(caps, jnp.float32),
    )


B_BLOCK, B_ROW, B_ROW_REST, B_COL_REST = 0, 1, 2, 3
A_BLOCK, A_ROW, A_ROW_REST, A_COL_REST = 4, 5, 6, 7
NEAR_ROW, NEAR_COL = 8, 9
FIELDS = 10
BATCH = 4
RING = 16


def cut(strip, start):
    if start >= strip.shape[1]:
        return jnp.zeros((strip.shape[0], WIDE), strip.dtype)
    piece = strip[:, start : min(start + PATCH, strip.shape[1])]
    gap = jnp.zeros((strip.shape[0], WIDE - piece.shape[1]), strip.dtype)
    return jnp.concatenate([piece, gap], axis=1)


def correlate_kernel(
    capacity,
    grid,
    count_ref,
    items_ref,
    everyone_ref,
    tile_ref,
    across_ref,
    down_ref,
    back_down_ref,
    back_across_ref,
    caps_ref,
    out_ref,
    *scratch,
):
    patches, halves, crosses, inverses = scratch[:4]
    corrs = scratch[4:6]
    energies, totals, row_moments, col_moments, runners, a_ref, b_ref = scratch[6:]
    count = count_ref[0]
    n_row, n_col, a_rows = grid

    height = tile_ref.shape[0]

    @pl.loop(0, height // 128)
    def _(chunk):
        place = pl.ds(pl.multiple_of(chunk * 128, 128), 128)
        strip = tile_ref[place, :]
        for block in range(b_ref.shape[0]):
            b_ref[block, place, :] = cut(strip, block * PATCH)

    b_ref[:, height:, :] = jnp.zeros((b_ref.shape[0], 16, WIDE), jnp.bfloat16)
    a_ref[0] = jnp.zeros(a_ref.shape[1:], jnp.bfloat16)
    rim = jnp.zeros((a_ref.shape[0], PATCH // 2, WIDE), jnp.bfloat16)
    a_ref[:, : PATCH // 2, :] = rim
    a_ref[:, a_ref.shape[1] - PATCH // 2 :, :] = rim

    @pl.loop(0, n_row)
    def _(row):
        strip = jnp.concatenate(
            [everyone_ref[row * n_col + col, :a_rows, :] for col in range(n_col)], axis=1
        )
        place = pl.ds(pl.multiple_of(PATCH // 2 + row * a_rows, 16), a_rows)
        for block in range(1, a_ref.shape[0]):
            a_ref[block, place, :] = cut(strip, (block - 1) * PATCH)

    def at(step, stage, part):
        return jnp.clip(BATCH * (step - stage) + part, 0, capacity - 1)

    def extract(source, block, row, row_rest, col_rest, base):
        lanes = lax.broadcasted_iota(jnp.int32, (16, WIDE), 1) >= col_rest
        rows = lax.broadcasted_iota(jnp.int32, (16, WIDE), 0) >= row_rest

        def group(place):
            here = pl.ds(pl.multiple_of(row + 16 * place, 16), 16)
            return jnp.where(lanes, source[block, here, :], source[block + 1, here, :])

        total = jnp.zeros((8, WIDE), jnp.float32)
        for place in range(PATCH // 16):
            values = group(place)
            if place == 0:
                values = jnp.where(rows, values, group(PATCH // 16))
            patches[base + 16 * place : base + 16 * place + 16, :] = values
            values = values.astype(jnp.float32)
            values = values * values
            total = total + (values[:8] + values[8:])
        return total[:, :HALF_LANES] + total[:, HALF_LANES:]

    def stage_half(step):
        for part in range(BATCH):
            item = at(step, 0, part)
            for which, source, fields in (
                (0, a_ref, (A_BLOCK, A_ROW, A_ROW_REST, A_COL_REST)),
                (1, b_ref, (B_BLOCK, B_ROW, B_ROW_REST, B_COL_REST)),
            ):
                block, row, row_rest, col_rest = (items_ref[field, item] for field in fields)
                energies[item % RING, which] = extract(
                    source, block, row, row_rest, col_rest, (2 * part + which) * PATCH
                )
        half = jnp.dot(patches[...], across_ref[...], preferred_element_type=jnp.float32)
        halves[...] = half.astype(jnp.bfloat16)

    def sides(spec, group):
        cc = spec[16 * group : 16 * group + 8, :HALF_LANES]
        cs = spec[16 * group : 16 * group + 8, HALF_LANES:]
        sc = spec[16 * group + 8 : 16 * group + 16, :HALF_LANES]
        ss = spec[16 * group + 8 : 16 * group + 16, HALF_LANES:]
        return cc - ss, sc + cs, cc + ss, sc - cs

    def stage_inverse():
        down = down_ref[...]
        for part in range(BATCH):
            base = 2 * part * PATCH
            spec_a = jnp.dot(
                down, halves[base : base + PATCH, :], preferred_element_type=jnp.float32
            )
            base = base + PATCH
            spec_b = jnp.dot(
                down, halves[base : base + PATCH, :], preferred_element_type=jnp.float32
            )
            for group in range(GROUPS):
                a_pr, a_pi, a_mr, a_mi = sides(spec_a, group)
                b_pr, b_pi, b_mr, b_mi = sides(spec_b, group)
                pr = a_pr * b_pr + a_pi * b_pi
                pi = a_pr * b_pi - a_pi * b_pr
                mr = a_mr * b_mr + a_mi * b_mi
                mi = a_mr * b_mi - a_mi * b_mr
                upper = jnp.concatenate([pr + mr, pi - mi], axis=1)
                lower = jnp.concatenate([pi + mi, mr - pr], axis=1)
                crosses[part, 16 * group : 16 * group + 16, :] = jnp.concatenate(
                    [upper, lower], axis=0
                ).astype(jnp.bfloat16)
        for part in range(BATCH):
            inverse = jnp.dot(
                back_down_ref[...], crosses[part], preferred_element_type=jnp.float32
            )
            inverses[PATCH * part : PATCH * (part + 1), :] = inverse.astype(jnp.bfloat16)

    def stage_score(step):
        corr_all = jnp.dot(
            inverses[...], back_across_ref[...], preferred_element_type=jnp.float32
        )
        rows = lax.broadcasted_iota(jnp.int32, (8, HALF_LANES), 0)
        lanes = lax.broadcasted_iota(jnp.int32, (8, HALF_LANES), 1)
        shift_rows = (rows - centre_reach).astype(jnp.float32)
        row_near = rows <= 2 * centre_reach
        for part in range(BATCH):
            item = at(step, 2, part)
            near_row = items_ref[NEAR_ROW, item]
            near_col = items_ref[NEAR_COL, item]
            ring = item % RING
            mean_a = jnp.sum(energies[ring, 0], keepdims=True) * (1.0 / (PATCH * PATCH))
            mean_b = jnp.sum(energies[ring, 1], keepdims=True) * (1.0 / (PATCH * PATCH))
            scale = 1.0 / (
                float(PATCH**4) * jnp.sqrt(mean_a + epsilon) * jnp.sqrt(mean_b + epsilon)
            )
            caps = caps_ref[pl.ds(PATCH - near_row, PATCH), :]
            total, row_moment, col_moment = 0.0, 0.0, 0.0
            best = None
            for half in range(2):
                corr = corr_all[
                    PATCH * part : PATCH * (part + 1),
                    half * HALF_LANES : (half + 1) * HALF_LANES,
                ]
                corrs[half][part, :PATCH, :] = corr
                corrs[half][part, PATCH:, :] = corr[:8]
                far = jnp.max(
                    jnp.minimum(corr, caps).reshape(PATCH // 8, 8, HALF_LANES), axis=0
                )
                if half == 0:
                    best = far
                else:
                    far = jnp.where(lanes < PATCH - HALF_LANES, far, -BIG)
                    best = jnp.maximum(best, far)
            for half in range(2):
                values = corrs[half][part, pl.ds(near_row, 8), :]
                place = lanes + half * HALF_LANES
                shift = place - near_col
                shift = jnp.where(shift >= PATCH // 2, shift - PATCH, shift)
                shift = jnp.where(shift < -(PATCH // 2), shift + PATCH, shift)
                inside = row_near & (place < PATCH)
                close = jnp.abs(shift) <= centre_reach
                weight = jnp.where(
                    inside & close, jnp.exp(sharpness * (values * scale)), 0.0
                )
                total = total + weight
                row_moment = row_moment + weight * shift_rows
                col_moment = col_moment + weight * shift.astype(jnp.float32)
                best = jnp.maximum(
                    best, jnp.where(inside & jnp.logical_not(close), values, -BIG)
                )
            totals[pl.ds(item, 1), :] = jnp.sum(total, axis=0, keepdims=True)
            row_moments[pl.ds(item, 1), :] = jnp.sum(row_moment, axis=0, keepdims=True)
            col_moments[pl.ds(item, 1), :] = jnp.sum(col_moment, axis=0, keepdims=True)
            runners[pl.ds(item, 1), :] = jnp.max(best * scale, axis=0, keepdims=True)

    @pl.loop(0, (count + BATCH - 1) // BATCH + 2)
    def _(step):
        stage_score(step)
        stage_inverse()
        stage_half(step)

    lanes = lax.broadcasted_iota(jnp.int32, (capacity, HALF_LANES), 1)
    used = lax.broadcasted_iota(jnp.int32, (capacity, HALF_LANES), 0) < count
    total = jnp.sum(totals[...], axis=1, keepdims=True)
    rows = jnp.sum(row_moments[...], axis=1, keepdims=True) / total
    cols = jnp.sum(col_moments[...], axis=1, keepdims=True) / total
    best = jnp.maximum(jnp.max(runners[...], axis=1, keepdims=True), -2.0)
    result = jnp.where(lanes == 0, rows, jnp.where(lanes == 1, cols, best))
    out_ref[...] = jnp.where(used & (lanes < 3), result, 0.0)


def correlate(count, items, everyone, tile, grid):
    capacity = items.shape[1]
    n_row, n_col, a_rows = grid
    a_blocks = (n_col * everyone.shape[2] + 76) // PATCH + 2
    b_blocks = -(-tile.shape[1] // PATCH)
    vmem = pl.BlockSpec(memory_space=pltpu.VMEM)
    smem = pl.BlockSpec(memory_space=pltpu.SMEM)
    rows = pltpu.VMEM((capacity, HALF_LANES), jnp.float32)
    return pl.pallas_call(
        functools.partial(correlate_kernel, capacity, grid),
        out_shape=jax.ShapeDtypeStruct((capacity, HALF_LANES), jnp.float32),
        in_specs=[smem, smem] + [vmem] * 7,
        out_specs=vmem,
        scratch_shapes=[
            pltpu.VMEM((2 * BATCH * PATCH, WIDE), jnp.bfloat16),
            pltpu.VMEM((2 * BATCH * PATCH, WIDE), jnp.bfloat16),
            pltpu.VMEM((BATCH, PAIRED, WIDE), jnp.bfloat16),
            pltpu.VMEM((BATCH * PATCH, WIDE), jnp.bfloat16),
            pltpu.VMEM((BATCH, PATCH + 8, HALF_LANES), jnp.float32),
            pltpu.VMEM((BATCH, PATCH + 8, HALF_LANES), jnp.float32),
            pltpu.VMEM((RING, 2, 8, HALF_LANES), jnp.float32),
        ]
        + [rows] * 4
        + [
            pltpu.VMEM((a_blocks, n_row * a_rows + PATCH, WIDE), jnp.bfloat16),
            pltpu.VMEM((b_blocks, tile.shape[0] + 16, WIDE), jnp.bfloat16),
        ],
        compiler_params=pltpu.CompilerParams(vmem_limit_bytes=40 * 1024 * 1024),
    )(count, items, everyone, tile, *kernel_tables())


def per_device(a_window, b_section, owners, pos_rows, pos_cols, peaks):
    node_rows, node_cols = pos_rows.shape
    nodes = node_rows * node_cols
    n_row, n_col = lax.axis_size("row"), lax.axis_size("col")
    devices = n_row * n_col
    me_row, me_col = lax.axis_index("row"), lax.axis_index("col")
    me = me_row * n_col + me_col
    share = max(2, (nodes * 8 // 5 + devices - 1) // devices)
    capacity = share * devices
    half_patch = PATCH // 2
    a_rows, a_cols = a_window.shape

    fields = jnp.stack(
        [
            owners.reshape(nodes),
            pos_rows.reshape(nodes) // 16,
            pos_rows.reshape(nodes) % 16,
            pos_cols.reshape(nodes) // 16,
            pos_cols.reshape(nodes) % 16,
            peaks[0].reshape(nodes),
            peaks[1].reshape(nodes),
            jnp.zeros((nodes,), jnp.int32),
        ]
    ).astype(jnp.bfloat16)
    fields = jnp.pad(fields, ((0, 0), (0, WIDE - nodes))).reshape(16, HALF_LANES)
    sent = jnp.concatenate([a_window, fields], axis=0)
    sent = jnp.broadcast_to(sent[None], (n_col,) + sent.shape)
    sent = lax.all_to_all(sent, "col", split_axis=0, concat_axis=0, tiled=True)
    everyone = lax.all_gather(sent, "row")
    everyone = everyone.reshape(devices, a_rows + 16, a_cols)

    known = everyone[:, a_rows:].reshape(devices, 8, WIDE)[:, :, :nodes]
    mine = (known[:, 0] == me.astype(jnp.bfloat16)).astype(jnp.float32)
    within = jnp.dot(
        mine, jnp.triu(jnp.ones((nodes, nodes), jnp.float32), 1)
    )
    loads = jnp.sum(mine, axis=1)
    before = jnp.sum(
        jnp.where(jnp.tril(jnp.ones((devices, devices), bool), -1), loads[None, :], 0.0), axis=1
    )
    count = jnp.sum(loads).astype(jnp.int32).reshape(1)
    slots = jnp.where(mine > 0, before[:, None] + within, -1.0).astype(jnp.int32)
    slots = slots.reshape(devices * nodes)
    chosen = (
        slots[None, :] == jnp.arange(capacity, dtype=jnp.int32)[:, None]
    ).astype(jnp.bfloat16)
    device_of = jnp.broadcast_to(jnp.arange(devices)[:, None], (devices, nodes))
    node_of = jnp.broadcast_to(jnp.arange(nodes)[None, :], (devices, nodes))
    listed = jnp.concatenate(
        [
            known.transpose(1, 0, 2)[:7],
            device_of[None].astype(jnp.bfloat16),
            node_of[None].astype(jnp.bfloat16),
        ],
        axis=0,
    ).reshape(9, devices * nodes)
    taken = lax.dot_general(
        listed, chosen, (((1,), (1,)), ((), ())), preferred_element_type=jnp.float32
    ).astype(jnp.int32)
    valid = jnp.arange(capacity) < count[0]
    b_top = jnp.where(valid, taken[1] * 16 + taken[2] - half_patch, 0)
    b_left = jnp.where(valid, taken[3] * 16 + taken[4] - half_patch, 0)
    a_top = (taken[7] // n_col * node_rows + taken[8] // node_cols) * STRIDE + STRIDE // 2
    a_left = (
        (taken[7] % n_col * node_cols + taken[8] % node_cols) * STRIDE
        + STRIDE // 2
        + half_patch
    )
    near_row = (taken[5] + b_top % 16 - a_top % 16 - centre_reach + 2 * PATCH) % PATCH
    near_col = (taken[6] + b_left % PATCH - a_left % PATCH + 2 * PATCH) % PATCH
    items = jnp.stack(
        [
            b_left // PATCH,
            b_top // 16 * 16,
            b_top % 16,
            b_left % PATCH,
            a_left // PATCH,
            a_top // 16 * 16,
            a_top % 16,
            a_left % PATCH,
            near_row,
            near_col,
        ]
    )
    result = correlate(count, items, everyone, b_section, (n_row, n_col, a_rows))[:, :3]

    height, breadth = n_row * node_rows, n_col * node_cols
    tall, broad = node_rows + 2 * RELAX, node_cols + 2 * RELAX
    lanes = -(-tall * broad // HALF_LANES) * HALF_LANES
    shape = (devices, lanes)
    device = lax.broadcasted_iota(jnp.int32, shape, 0)
    place = lax.broadcasted_iota(jnp.int32, shape, 1)
    row = device // n_col * node_rows + place // broad - RELAX
    col = device % n_col * node_cols + place % broad - RELAX
    real = (row >= 0) & (row < height) & (col >= 0) & (col < breadth) & (place < tall * broad)
    wanted = jnp.where(real, row * breadth + col, -1).reshape(devices * lanes)
    node = (taken[7] // n_col * node_rows + taken[8] // node_cols) * breadth + (
        taken[7] % n_col * node_cols + taken[8] % node_cols
    )
    node = jnp.where(valid, node, -2)
    spread = lax.dot_general(
        result,
        (node[:, None] == wanted[None, :]).astype(jnp.float32),
        (((0,), (0,)), ((), ())),
        precision=lax.Precision.HIGHEST,
    )
    spread = spread.reshape(3, devices, lanes).transpose(1, 0, 2)
    spread = lax.all_to_all(spread, ("row", "col"), split_axis=0, concat_axis=0, tiled=True)
    spread = jnp.sum(spread, axis=0)[:, : tall * broad].reshape(3, tall, broad)
    runner = spread[2, RELAX:-RELAX, RELAX:-RELAX]
    offsets = known[:, 5:7].astype(jnp.float32).reshape(n_row, n_col, 2, node_rows, node_cols)
    offsets = offsets.transpose(2, 0, 3, 1, 4).reshape(2, height, breadth)
    offsets = jnp.pad(offsets, ((0, 0), (RELAX, RELAX), (RELAX, RELAX)))
    field = spread[:2] + lax.dynamic_slice(
        offsets, (0, me_row * node_rows, me_col * node_cols), (2, tall, broad)
    )
    for step in range(RELAX):
        reach = RELAX - 1 - step
        centre = field[:, 1:-1, 1:-1]
        around = (
            field[:, 2:, 1:-1] + field[:, :-2, 1:-1] + field[:, 1:-1, 2:] + field[:, 1:-1, :-2]
        )
        field = centre + stiffness * (around - 4.0 * centre)
        rows = me_row * node_rows - reach + jnp.arange(node_rows + 2 * reach)
        cols = me_col * node_cols - reach + jnp.arange(node_cols + 2 * reach)
        inside = ((rows >= 0) & (rows < height))[:, None] & ((cols >= 0) & (cols < breadth))[None]
        field = jnp.where(inside[None], field, 0.0)
    return (field, runner)


def solution(mesh):
    placed = (
        P("row", "col"),
        P("row", "col"),
        P("row", "col", None, None, None),
        P("row", "col"),
        P("row", "col"),
        P(None, "row", "col"),
    )
    return jax.shard_map(
        per_device,
        mesh=mesh,
        in_specs=placed,
        out_specs=(P(None, "row", "col"), P("row", "col")),
        check_vma=False,
    )
```

```python
import functools
import math

import jax
import jax.numpy as jnp
import numpy as np
from jax import lax
from jax.experimental import pallas as pl
from jax.experimental.pallas import tpu as pltpu
from jax.sharding import PartitionSpec as P

PATCH = 160
NODE_LANES = 16
STRIDE = 8
RELAX = 2
WIDE = 256
HALF_LANES = 128
FREQS = PATCH // 2 + 1
GROUPS = 11
PAIRED = 16 * GROUPS
BIG = 3.0e38

sharpness = 80.0
epsilon = 1e-06
stiffness = 0.24
centre_reach = 2


def dft_tables():
    steps = np.arange(PATCH)
    angles = 2.0 * math.pi * ((steps[:, None] * steps[None, :FREQS]) % PATCH) / PATCH
    return (
        np.cos(angles).astype(jnp.bfloat16).astype(np.float32),
        np.sin(angles).astype(jnp.bfloat16).astype(np.float32),
    )


def kernel_tables():
    cosine, sine = dft_tables()
    weights = np.full((FREQS,), 2.0, np.float32)
    weights[0] = weights[-1] = 1.0
    across = np.zeros((WIDE, WIDE), np.float32)
    across[:PATCH, :FREQS] = cosine
    across[:PATCH, HALF_LANES : HALF_LANES + FREQS] = sine
    back_across = np.zeros((WIDE, WIDE), np.float32)
    back_across[:FREQS, :PATCH] = 0.5 * (cosine * weights).T
    back_across[HALF_LANES : HALF_LANES + FREQS, :PATCH] = 0.5 * (sine * weights).T
    down = np.zeros((PAIRED, PATCH), np.float32)
    back_down = np.zeros((PATCH, PAIRED), np.float32)
    for freq in range(FREQS):
        row = 16 * (freq // 8) + freq % 8
        down[row] = cosine[:, freq]
        down[row + 8] = sine[:, freq]
        back_down[:, row] = cosine[:, freq] * weights[freq]
        back_down[:, row + 8] = sine[:, freq] * weights[freq]
    caps = np.full((2 * PATCH, HALF_LANES), BIG, np.float32)
    for row in range(2 * PATCH):
        if row % PATCH <= 2 * centre_reach:
            caps[row] = -BIG
    return (
        jnp.asarray(across, jnp.bfloat16),
        jnp.asarray(down, jnp.bfloat16),
        jnp.asarray(back_down, jnp.bfloat16),
        jnp.asarray(back_across, jnp.bfloat16),
        jnp.asarray(caps, jnp.float32),
    )


def listing_tables():
    lane = np.arange(HALF_LANES)
    group, place = lane // NODE_LANES, lane % NODE_LANES
    repeat = (lane[:, None] < NODE_LANES) & (place[None] == lane[:, None])
    earlier = (group[:, None] == group[None]) & (place[:, None] < place[None])
    first = np.broadcast_to(lane[:, None] < NODE_LANES, (HALF_LANES, HALF_LANES))
    below = lane[None] < lane[:, None]
    counting = np.concatenate([repeat, earlier, first, below, below.T, first.T], axis=1)
    fields = np.zeros((2 * HALF_LANES, HALF_LANES), np.float32)
    fields[lane, group] = 1.0
    fields[HALF_LANES, MESH_ROW] = 1.0
    return (
        jnp.asarray(counting, jnp.bfloat16),
        jnp.asarray(fields, jnp.bfloat16),
        jnp.asarray(fields.T[:16], jnp.bfloat16),
    )


OWNER, ROW_HIGH, ROW_LOW, COL_HIGH, COL_LOW, PEAK_ROW, PEAK_COL, MESH_COL, MESH_ROW = range(9)
B_BLOCK, B_ROW, B_ROW_REST, B_COL_REST = 0, 1, 2, 3
A_BLOCK, A_ROW, A_ROW_REST, A_COL_REST = 4, 5, 6, 7
NEAR_ROW, NEAR_COL = 8, 9
FIELDS = 10
BATCH = 4
RING = 16


def cut(strip, start):
    if start >= strip.shape[1]:
        return jnp.zeros((strip.shape[0], WIDE), strip.dtype)
    piece = strip[:, start : min(start + PATCH, strip.shape[1])]
    gap = jnp.zeros((strip.shape[0], WIDE - piece.shape[1]), strip.dtype)
    return jnp.concatenate([piece, gap], axis=1)


def correlate_kernel(
    capacity,
    grid,
    everyone_ref,
    tile_ref,
    across_ref,
    down_ref,
    back_down_ref,
    back_across_ref,
    caps_ref,
    counting_ref,
    fields_ref,
    fields_turned_ref,
    out_ref,
    *scratch,
):
    patches, halves, crosses, inverses = scratch[:4]
    corrs = scratch[4:6]
    energies, totals, row_moments, col_moments, runners, a_ref, b_ref = scratch[6:13]
    columns_ref, listed_ref, items_ref, semaphore = scratch[13:]
    n_row, n_col, a_rows, node_rows = grid
    count = list_nodes(
        capacity,
        grid,
        everyone_ref,
        counting_ref,
        fields_ref,
        fields_turned_ref,
        columns_ref,
        listed_ref,
    )
    to_scalars = pltpu.make_async_copy(listed_ref, items_ref, semaphore)
    to_scalars.start()

    height = tile_ref.shape[0]

    @pl.loop(0, height // 128)
    def _(chunk):
        place = pl.ds(pl.multiple_of(chunk * 128, 128), 128)
        strip = tile_ref[place, :]
        for block in range(b_ref.shape[0]):
            b_ref[block, place, :] = cut(strip, block * PATCH)

    b_ref[:, height:, :] = jnp.zeros((b_ref.shape[0], 16, WIDE), jnp.bfloat16)
    a_ref[0] = jnp.zeros(a_ref.shape[1:], jnp.bfloat16)
    rim = jnp.zeros((a_ref.shape[0], PATCH // 2, WIDE), jnp.bfloat16)
    a_ref[:, : PATCH // 2, :] = rim
    a_ref[:, a_ref.shape[1] - PATCH // 2 :, :] = rim

    @pl.loop(0, n_row)
    def _(row):
        strip = jnp.concatenate(
            [everyone_ref[row * n_col + col, :a_rows, :] for col in range(n_col)], axis=1
        )
        place = pl.ds(pl.multiple_of(PATCH // 2 + row * a_rows, 16), a_rows)
        for block in range(1, a_ref.shape[0]):
            a_ref[block, place, :] = cut(strip, (block - 1) * PATCH)

    def at(step, stage, part):
        return jnp.clip(BATCH * (step - stage) + part, 0, capacity - 1)

    def extract(source, block, row, row_rest, col_rest, base):
        lanes = lax.broadcasted_iota(jnp.int32, (16, WIDE), 1) >= col_rest
        rows = lax.broadcasted_iota(jnp.int32, (16, WIDE), 0) >= row_rest

        def group(place):
            here = pl.ds(pl.multiple_of(row + 16 * place, 16), 16)
            return jnp.where(lanes, source[block, here, :], source[block + 1, here, :])

        total = jnp.zeros((8, WIDE), jnp.float32)
        for place in range(PATCH // 16):
            values = group(place)
            if place == 0:
                values = jnp.where(rows, values, group(PATCH // 16))
            patches[base + 16 * place : base + 16 * place + 16, :] = values
            values = values.astype(jnp.float32)
            values = values * values
            total = total + (values[:8] + values[8:])
        return total[:, :HALF_LANES] + total[:, HALF_LANES:]

    def stage_half(step):
        for part in range(BATCH):
            item = at(step, 0, part)
            for which, source, fields in (
                (0, a_ref, (A_BLOCK, A_ROW, A_ROW_REST, A_COL_REST)),
                (1, b_ref, (B_BLOCK, B_ROW, B_ROW_REST, B_COL_REST)),
            ):
                block, row, row_rest, col_rest = (items_ref[field, item] for field in fields)
                energies[item % RING, which] = extract(
                    source, block, row, row_rest, col_rest, (2 * part + which) * PATCH
                )
        half = jnp.dot(patches[...], across_ref[...], preferred_element_type=jnp.float32)
        halves[...] = half.astype(jnp.bfloat16)

    def sides(spec, group):
        cc = spec[16 * group : 16 * group + 8, :HALF_LANES]
        cs = spec[16 * group : 16 * group + 8, HALF_LANES:]
        sc = spec[16 * group + 8 : 16 * group + 16, :HALF_LANES]
        ss = spec[16 * group + 8 : 16 * group + 16, HALF_LANES:]
        return cc - ss, sc + cs, cc + ss, sc - cs

    def stage_inverse():
        down = down_ref[...]
        for part in range(BATCH):
            base = 2 * part * PATCH
            spec_a = jnp.dot(
                down, halves[base : base + PATCH, :], preferred_element_type=jnp.float32
            )
            base = base + PATCH
            spec_b = jnp.dot(
                down, halves[base : base + PATCH, :], preferred_element_type=jnp.float32
            )
            for group in range(GROUPS):
                a_pr, a_pi, a_mr, a_mi = sides(spec_a, group)
                b_pr, b_pi, b_mr, b_mi = sides(spec_b, group)
                pr = a_pr * b_pr + a_pi * b_pi
                pi = a_pr * b_pi - a_pi * b_pr
                mr = a_mr * b_mr + a_mi * b_mi
                mi = a_mr * b_mi - a_mi * b_mr
                upper = jnp.concatenate([pr + mr, pi - mi], axis=1)
                lower = jnp.concatenate([pi + mi, mr - pr], axis=1)
                crosses[part, 16 * group : 16 * group + 16, :] = jnp.concatenate(
                    [upper, lower], axis=0
                ).astype(jnp.bfloat16)
        for part in range(BATCH):
            inverse = jnp.dot(
                back_down_ref[...], crosses[part], preferred_element_type=jnp.float32
            )
            inverses[PATCH * part : PATCH * (part + 1), :] = inverse.astype(jnp.bfloat16)

    def stage_score(step):
        corr_all = jnp.dot(
            inverses[...], back_across_ref[...], preferred_element_type=jnp.float32
        )
        rows = lax.broadcasted_iota(jnp.int32, (8, HALF_LANES), 0)
        lanes = lax.broadcasted_iota(jnp.int32, (8, HALF_LANES), 1)
        shift_rows = (rows - centre_reach).astype(jnp.float32)
        row_near = rows <= 2 * centre_reach
        for part in range(BATCH):
            item = at(step, 2, part)
            near_row = items_ref[NEAR_ROW, item]
            near_col = items_ref[NEAR_COL, item]
            ring = item % RING
            mean_a = jnp.sum(energies[ring, 0], keepdims=True) * (1.0 / (PATCH * PATCH))
            mean_b = jnp.sum(energies[ring, 1], keepdims=True) * (1.0 / (PATCH * PATCH))
            scale = 1.0 / (
                float(PATCH**4) * jnp.sqrt(mean_a + epsilon) * jnp.sqrt(mean_b + epsilon)
            )
            caps = caps_ref[pl.ds(PATCH - near_row, PATCH), :]
            total, row_moment, col_moment = 0.0, 0.0, 0.0
            best = None
            for half in range(2):
                corr = corr_all[
                    PATCH * part : PATCH * (part + 1),
                    half * HALF_LANES : (half + 1) * HALF_LANES,
                ]
                corrs[half][part, :PATCH, :] = corr
                corrs[half][part, PATCH:, :] = corr[:8]
                far = jnp.max(
                    jnp.minimum(corr, caps).reshape(PATCH // 8, 8, HALF_LANES), axis=0
                )
                if half == 0:
                    best = far
                else:
                    far = jnp.where(lanes < PATCH - HALF_LANES, far, -BIG)
                    best = jnp.maximum(best, far)
            for half in range(2):
                values = corrs[half][part, pl.ds(near_row, 8), :]
                place = lanes + half * HALF_LANES
                shift = place - near_col
                shift = jnp.where(shift >= PATCH // 2, shift - PATCH, shift)
                shift = jnp.where(shift < -(PATCH // 2), shift + PATCH, shift)
                inside = row_near & (place < PATCH)
                close = jnp.abs(shift) <= centre_reach
                weight = jnp.where(
                    inside & close, jnp.exp(sharpness * (values * scale)), 0.0
                )
                total = total + weight
                row_moment = row_moment + weight * shift_rows
                col_moment = col_moment + weight * shift.astype(jnp.float32)
                best = jnp.maximum(
                    best, jnp.where(inside & jnp.logical_not(close), values, -BIG)
                )
            totals[pl.ds(item, 1), :] = jnp.sum(total, axis=0, keepdims=True)
            row_moments[pl.ds(item, 1), :] = jnp.sum(row_moment, axis=0, keepdims=True)
            col_moments[pl.ds(item, 1), :] = jnp.sum(col_moment, axis=0, keepdims=True)
            runners[pl.ds(item, 1), :] = jnp.max(best * scale, axis=0, keepdims=True)

    to_scalars.wait()

    @pl.loop(0, (count + BATCH - 1) // BATCH + 2)
    def _(step):
        stage_score(step)
        stage_inverse()
        stage_half(step)

    used = lax.broadcasted_iota(jnp.int32, (capacity, 1), 0) < count
    total = jnp.sum(totals[...], axis=1, keepdims=True)
    peak_row = columns_ref[:, PEAK_ROW : PEAK_ROW + 1]
    peak_col = columns_ref[:, PEAK_COL : PEAK_COL + 1]
    results = (
        peak_row + jnp.sum(row_moments[...], axis=1, keepdims=True) / total,
        peak_col + jnp.sum(col_moments[...], axis=1, keepdims=True) / total,
        jnp.maximum(jnp.max(runners[...], axis=1, keepdims=True), -2.0),
    )
    lanes = lax.broadcasted_iota(jnp.int32, (capacity, HALF_LANES), 1)
    terms = jnp.zeros((capacity, HALF_LANES), jnp.float32)
    for value, rest in enumerate(results):
        rest = jnp.where(used, rest, 0.0)
        for term in range(3):
            here = rest.astype(jnp.bfloat16).astype(jnp.float32)
            terms = jnp.where(lanes == 8 * term + value, here, terms)
            rest = rest - here
    square = (32, HALF_LANES)
    pick = lax.broadcasted_iota(jnp.int32, square, 0) == lax.broadcasted_iota(jnp.int32, square, 1)
    terms = lax.dot_general(
        jnp.where(pick, 1.0, 0.0).astype(jnp.bfloat16),
        terms.astype(jnp.bfloat16),
        (((1,), (1,)), ((), ())),
        preferred_element_type=jnp.float32,
    ).astype(jnp.bfloat16)

    height, breadth = n_row * node_rows, n_col * NODE_LANES
    tall, broad = node_rows + 2 * RELAX, NODE_LANES + 2 * RELAX
    width = out_ref.shape[2]
    node = columns_ref[:, MESH_ROW : MESH_ROW + 1] * float(breadth)
    node = node + columns_ref[:, MESH_COL : MESH_COL + 1]
    node = jnp.where(used, node, -2.0)
    place = lax.broadcasted_iota(jnp.int32, (8, width), 1).astype(jnp.float32)
    local_row = jnp.floor((place + 0.5) * (1.0 / broad))
    local_col = place - local_row * broad

    @pl.loop(0, n_row * n_col)
    def _(device):
        row = local_row + ((device // n_col) * node_rows - RELAX).astype(jnp.float32)
        col = local_col + ((device % n_col) * NODE_LANES - RELAX).astype(jnp.float32)
        real = (row >= 0) & (row < height) & (col >= 0) & (col < breadth) & (local_row < tall)
        wanted = jnp.where(real, row * float(breadth) + col, -1.0)[:1]
        chosen = jnp.where(node == wanted, 1.0, 0.0).astype(jnp.bfloat16)
        sent = jnp.dot(terms, chosen, preferred_element_type=jnp.float32)
        sent = sent[0:8] + sent[8:16] + sent[16:24]
        out_ref[device] = sent[:3]


def list_nodes(
    capacity,
    grid,
    everyone_ref,
    counting_ref,
    fields_ref,
    fields_turned_ref,
    columns_ref,
    listed_ref,
):
    n_row, n_col, a_rows, node_rows = grid
    me = (lax.axis_index("row") * n_col + lax.axis_index("col")).astype(jnp.float32)
    exact = functools.partial(lax.dot_general, preferred_element_type=jnp.float32)
    plain = (((1,), (0,)), ((), ()))
    turned = (((1,), (1,)), ((), ()))

    def table(index, many=1):
        return counting_ref[:, index * HALF_LANES : (index + many) * HALF_LANES]

    slot = lax.broadcasted_iota(jnp.int32, (capacity, HALF_LANES), 0).astype(jnp.float32)
    before = jnp.zeros((1, HALF_LANES), jnp.float32)
    found = jnp.zeros((capacity, 3 * HALF_LANES), jnp.float32)
    for block in range(n_row * n_col // 8):
        records = everyone_ref[8 * block : 8 * block + 8, a_rows : a_rows + 16, :]
        records = records.reshape(HALF_LANES, HALF_LANES)
        mine = exact(records, table(0), plain) == me
        ones = jnp.where(mine, 1.0, 0.0).astype(jnp.bfloat16)
        counts = exact(ones, table(1, 2), plain)
        within, loads = counts[:, :HALF_LANES], counts[:, HALF_LANES:]
        base = exact(table(3), loads.astype(jnp.bfloat16), plain) + before
        slots = jnp.where(mine, within + base, -1.0)
        row_loads = exact(table(5)[:16], ones, turned)
        row_base = exact(row_loads.astype(jnp.bfloat16), table(4), plain)[:1] + before
        holds = (slot >= row_base) & (slot < row_base + row_loads[:1])
        local = lax.broadcasted_iota(jnp.int32, (HALF_LANES, HALF_LANES), 0) % 16
        mesh_row = (local + 8 * block // n_col * node_rows).astype(jnp.float32)
        found = found + exact(
            jnp.where(holds, 1.0, 0.0).astype(jnp.bfloat16),
            jnp.concatenate(
                [records, slots.astype(jnp.bfloat16), mesh_row.astype(jnp.bfloat16)], axis=1
            ),
            plain,
        )
        before = before + jnp.sum(loads, axis=0, keepdims=True)

    same = found[:, HALF_LANES : 2 * HALF_LANES] == slot
    taken = jnp.concatenate(
        [jnp.where(same, found[:, :HALF_LANES], 0.0), found[:, 2 * HALF_LANES :]], axis=1
    ).astype(jnp.bfloat16)
    columns_ref[...] = exact(taken, fields_ref[...], plain)
    rows = exact(fields_turned_ref[...], taken, turned)

    def field(index):
        return rows[index : index + 1, :]

    def divide(value, by):
        whole = jnp.floor((value + 0.5) * (1.0 / by))
        return whole, value - whole * by

    half = float(PATCH // 2)
    b_top = jnp.maximum(16.0 * field(ROW_HIGH) + field(ROW_LOW) - half, 0.0)
    b_left = jnp.maximum(16.0 * field(COL_HIGH) + field(COL_LOW) - half, 0.0)
    a_top = STRIDE * field(MESH_ROW) + STRIDE // 2
    a_left = STRIDE * field(MESH_COL) + (STRIDE // 2 + half)
    b_group, b_row_rest = divide(b_top, 16)
    b_block, b_col_rest = divide(b_left, PATCH)
    a_group, a_row_rest = divide(a_top, 16)
    a_block, a_col_rest = divide(a_left, PATCH)
    near_row = divide(field(PEAK_ROW) + b_row_rest - a_row_rest - centre_reach, PATCH)[1]
    near_col = divide(field(PEAK_COL) + b_col_rest - a_col_rest, PATCH)[1]
    for index, value in (
        (B_BLOCK, b_block),
        (B_ROW, 16.0 * b_group),
        (B_ROW_REST, b_row_rest),
        (B_COL_REST, b_col_rest),
        (A_BLOCK, a_block),
        (A_ROW, 16.0 * a_group),
        (A_ROW_REST, a_row_rest),
        (A_COL_REST, a_col_rest),
        (NEAR_ROW, near_row),
        (NEAR_COL, near_col),
    ):
        listed_ref[index : index + 1, :] = value.astype(jnp.int32)
    listed_ref[FIELDS:, :] = jnp.zeros((16 - FIELDS, capacity), jnp.int32)
    return jnp.max(before).astype(jnp.int32)


def correlate(capacity, everyone, tile, grid):
    n_row, n_col, a_rows, node_rows = grid
    tall, broad = node_rows + 2 * RELAX, NODE_LANES + 2 * RELAX
    width = -(-tall * broad // HALF_LANES) * HALF_LANES
    a_blocks = (n_col * everyone.shape[2] + 76) // PATCH + 2
    b_blocks = -(-tile.shape[1] // PATCH)
    vmem = pl.BlockSpec(memory_space=pltpu.VMEM)
    rows = pltpu.VMEM((capacity, HALF_LANES), jnp.float32)
    return pl.pallas_call(
        functools.partial(correlate_kernel, capacity, grid),
        out_shape=jax.ShapeDtypeStruct((n_row * n_col, 3, width), jnp.float32),
        in_specs=[vmem] * 10,
        out_specs=vmem,
        scratch_shapes=[
            pltpu.VMEM((2 * BATCH * PATCH, WIDE), jnp.bfloat16),
            pltpu.VMEM((2 * BATCH * PATCH, WIDE), jnp.bfloat16),
            pltpu.VMEM((BATCH, PAIRED, WIDE), jnp.bfloat16),
            pltpu.VMEM((BATCH * PATCH, WIDE), jnp.bfloat16),
            pltpu.VMEM((BATCH, PATCH + 8, HALF_LANES), jnp.float32),
            pltpu.VMEM((BATCH, PATCH + 8, HALF_LANES), jnp.float32),
            pltpu.VMEM((RING, 2, 8, HALF_LANES), jnp.float32),
        ]
        + [rows] * 4
        + [
            pltpu.VMEM((a_blocks, n_row * a_rows + PATCH, WIDE), jnp.bfloat16),
            pltpu.VMEM((b_blocks, tile.shape[0] + 16, WIDE), jnp.bfloat16),
            rows,
            pltpu.VMEM((16, capacity), jnp.int32),
            pltpu.SMEM((16, capacity), jnp.int32),
            pltpu.SemaphoreType.DMA,
        ],
        compiler_params=pltpu.CompilerParams(vmem_limit_bytes=40 * 1024 * 1024),
    )(everyone, tile, *kernel_tables(), *listing_tables())


def per_device(a_window, b_section, owners, pos_rows, pos_cols, peaks):
    node_rows, node_cols = pos_rows.shape
    nodes = node_rows * node_cols
    n_row, n_col = lax.axis_size("row"), lax.axis_size("col")
    devices = n_row * n_col
    me_row, me_col = lax.axis_index("row"), lax.axis_index("col")
    share = max(2, (nodes * 8 // 5 + devices - 1) // devices)
    a_rows, a_cols = a_window.shape
    height, breadth = n_row * node_rows, n_col * node_cols

    mesh_col = me_col * node_cols + lax.broadcasted_iota(jnp.int32, pos_rows.shape, 1)
    records = jnp.concatenate(
        [
            owners.reshape(node_rows, node_cols),
            pos_rows // 16,
            pos_rows % 16,
            pos_cols // 16,
            pos_cols % 16,
            peaks[0],
            peaks[1],
            mesh_col,
        ],
        axis=1,
    ).astype(jnp.bfloat16)
    records = jnp.pad(records, ((0, 16 - node_rows), (0, 0)), constant_values=-1)
    sent = jnp.concatenate([a_window, records], axis=0)
    sent = jnp.broadcast_to(sent[None], (n_col,) + sent.shape)
    sent = lax.all_to_all(sent, "col", split_axis=0, concat_axis=0, tiled=True)
    everyone = lax.all_gather(sent, "row").reshape(devices, a_rows + 16, a_cols)

    grid = (n_row, n_col, a_rows, node_rows)
    spread = correlate(share * devices, everyone, b_section, grid)
    spread = lax.all_to_all(spread, ("row", "col"), split_axis=0, concat_axis=0, tiled=True)
    tall, broad = node_rows + 2 * RELAX, node_cols + 2 * RELAX
    spread = jnp.sum(spread, axis=0)[:, : tall * broad].reshape(3, tall, broad)
    runner = spread[2, RELAX:-RELAX, RELAX:-RELAX]
    field = spread[:2]
    for step in range(RELAX):
        reach = RELAX - 1 - step
        centre = field[:, 1:-1, 1:-1]
        around = (
            field[:, 2:, 1:-1] + field[:, :-2, 1:-1] + field[:, 1:-1, 2:] + field[:, 1:-1, :-2]
        )
        field = centre + stiffness * (around - 4.0 * centre)
        rows = me_row * node_rows - reach + jnp.arange(node_rows + 2 * reach)
        cols = me_col * node_cols - reach + jnp.arange(node_cols + 2 * reach)
        inside = ((rows >= 0) & (rows < height))[:, None] & ((cols >= 0) & (cols < breadth))[None]
        field = jnp.where(inside[None], field, 0.0)
    return (field, runner)


def solution(mesh):
    placed = (
        P("row", "col"),
        P("row", "col"),
        P("row", "col", None, None, None),
        P("row", "col"),
        P("row", "col"),
        P(None, "row", "col"),
    )
    return jax.shard_map(
        per_device,
        mesh=mesh,
        in_specs=placed,
        out_specs=(P(None, "row", "col"), P("row", "col")),
        check_vma=False,
    )
```

```python
import functools
import math

import jax
import jax.numpy as jnp
import numpy as np
from jax import lax
from jax.experimental import pallas as pl
from jax.experimental.pallas import tpu as pltpu
from jax.sharding import PartitionSpec as P

PATCH = 160
NODE_LANES = 16
SPREAD_LANES = 32
SPREAD_ROWS = 16
STRIDE = 8
RELAX = 2
WIDE = 256
HALF_LANES = 128
FREQS = PATCH // 2 + 1
GROUPS = 11
PAIRED = 16 * GROUPS
BIG = 3.0e38

sharpness = 80.0
epsilon = 1e-06
stiffness = 0.24
centre_reach = 2


def dft_tables():
    steps = np.arange(PATCH)
    angles = 2.0 * math.pi * ((steps[:, None] * steps[None, :FREQS]) % PATCH) / PATCH
    return (
        np.cos(angles).astype(jnp.bfloat16).astype(np.float32),
        np.sin(angles).astype(jnp.bfloat16).astype(np.float32),
    )


def kernel_tables():
    cosine, sine = dft_tables()
    weights = np.full((FREQS,), 2.0, np.float32)
    weights[0] = weights[-1] = 1.0
    across = np.zeros((WIDE, WIDE), np.float32)
    across[:PATCH, :FREQS] = cosine
    across[:PATCH, HALF_LANES : HALF_LANES + FREQS] = sine
    back_across = np.zeros((WIDE, WIDE), np.float32)
    back_across[:FREQS, :PATCH] = 0.5 * (cosine * weights).T
    back_across[HALF_LANES : HALF_LANES + FREQS, :PATCH] = 0.5 * (sine * weights).T
    down = np.zeros((PAIRED, PATCH), np.float32)
    back_down = np.zeros((PATCH, PAIRED), np.float32)
    for freq in range(FREQS):
        row = 16 * (freq // 8) + freq % 8
        down[row] = cosine[:, freq]
        down[row + 8] = sine[:, freq]
        back_down[:, row] = cosine[:, freq] * weights[freq]
        back_down[:, row + 8] = sine[:, freq] * weights[freq]
    return across, down, back_down, back_across


def listing_tables():
    lane = np.arange(HALF_LANES)
    group, place = lane // NODE_LANES, lane % NODE_LANES
    repeat = (lane[:, None] < NODE_LANES) & (place[None] == lane[:, None])
    earlier = (group[:, None] == group[None]) & (place[:, None] < place[None])
    first = np.broadcast_to(lane[:, None] < NODE_LANES, (HALF_LANES, HALF_LANES))
    below = lane[None] < lane[:, None]
    fields = np.zeros((2 * HALF_LANES, HALF_LANES), np.float32)
    fields[lane, group] = 1.0
    fields[HALF_LANES, MESH_ROW] = 1.0
    return repeat, np.concatenate([earlier, first], axis=1), below, below.T, first.T[:16], fields, (
        fields.T[:16]
    )


def all_tables():
    names = ("across", "down", "back_down", "back_across", "repeat", "within")
    names += ("below", "above", "count", "fields", "turned")
    places, parts, start = {}, [], 0
    for name, part in zip(names, kernel_tables() + listing_tables()):
        rows, lanes = part.shape
        places[name] = (start, rows, lanes)
        rows_up = -(-rows // 16) * 16
        parts.append(np.zeros((rows_up, WIDE), np.float32))
        parts[-1][:rows, :lanes] = part
        start += rows_up
    return jnp.asarray(np.concatenate(parts), jnp.bfloat16), places


OWNER, ROW_HIGH, ROW_LOW, COL_HIGH, COL_LOW, PEAK_ROW, PEAK_COL, MESH_COL, MESH_ROW = range(9)
B_BLOCK, B_ROW, B_ROW_REST, B_COL_REST = 0, 1, 2, 3
A_BLOCK, A_ROW, A_ROW_REST, A_COL_REST = 4, 5, 6, 7
NEAR_ROW, NEAR_COL = 8, 9
FIELDS = 10
BATCH = 4
RING = 16


def cut(strip, start):
    if start >= strip.shape[1]:
        return jnp.zeros((strip.shape[0], WIDE), strip.dtype)
    piece = strip[:, start : min(start + PATCH, strip.shape[1])]
    gap = jnp.zeros((strip.shape[0], WIDE - piece.shape[1]), strip.dtype)
    return jnp.concatenate([piece, gap], axis=1)


def correlate_kernel(
    capacity,
    grid,
    places,
    everyone_ref,
    tile_ref,
    tables_ref,
    out_ref,
    *scratch,
):
    patches, halves, crosses, inverses = scratch[:4]
    corrs = scratch[4:6]
    energies, totals, row_moments, col_moments, runners, a_ref, b_ref = scratch[6:13]
    columns_ref, listed_ref, items_ref, semaphore, caps_ref, rows_ref = scratch[13:]

    def table(name):
        start, rows, lanes = places[name]
        return tables_ref[start : start + rows, :lanes]

    n_row, n_col, a_rows, node_rows = grid
    count = list_nodes(
        capacity,
        grid,
        everyone_ref,
        table,
        columns_ref,
        rows_ref,
        listed_ref,
    )
    caps_row = lax.broadcasted_iota(jnp.int32, caps_ref.shape, 0) % PATCH
    caps_ref[...] = jnp.where(caps_row <= 2 * centre_reach, -BIG, BIG)
    to_scalars = pltpu.make_async_copy(listed_ref, items_ref, semaphore)
    to_scalars.start()

    height = tile_ref.shape[0]

    @pl.loop(0, height // 128)
    def _(chunk):
        place = pl.ds(pl.multiple_of(chunk * 128, 128), 128)
        strip = tile_ref[place, :]
        for block in range(b_ref.shape[0]):
            b_ref[block, place, :] = cut(strip, block * PATCH)

    b_ref[:, height:, :] = jnp.zeros((b_ref.shape[0], 16, WIDE), jnp.bfloat16)
    a_ref[0] = jnp.zeros(a_ref.shape[1:], jnp.bfloat16)
    rim = jnp.zeros((a_ref.shape[0], PATCH // 2, WIDE), jnp.bfloat16)
    a_ref[:, : PATCH // 2, :] = rim
    a_ref[:, a_ref.shape[1] - PATCH // 2 :, :] = rim

    @pl.loop(0, n_row)
    def _(row):
        strip = jnp.concatenate(
            [everyone_ref[row * n_col + col, :a_rows, :] for col in range(n_col)], axis=1
        )
        place = pl.ds(pl.multiple_of(PATCH // 2 + row * a_rows, 16), a_rows)
        for block in range(1, a_ref.shape[0]):
            a_ref[block, place, :] = cut(strip, (block - 1) * PATCH)

    def at(step, stage, part):
        return jnp.clip(BATCH * (step - stage) + part, 0, capacity - 1)

    def extract(source, block, row, row_rest, col_rest, base):
        lanes = lax.broadcasted_iota(jnp.int32, (16, WIDE), 1) >= col_rest
        rows = lax.broadcasted_iota(jnp.int32, (16, WIDE), 0) >= row_rest

        def group(place):
            here = pl.ds(pl.multiple_of(row + 16 * place, 16), 16)
            return jnp.where(lanes, source[block, here, :], source[block + 1, here, :])

        total = jnp.zeros((8, WIDE), jnp.float32)
        for place in range(PATCH // 16):
            values = group(place)
            if place == 0:
                values = jnp.where(rows, values, group(PATCH // 16))
            patches[base + 16 * place : base + 16 * place + 16, :] = values
            values = values.astype(jnp.float32)
            values = values * values
            total = total + (values[:8] + values[8:])
        return total[:, :HALF_LANES] + total[:, HALF_LANES:]

    def stage_half(step):
        for part in range(BATCH):
            item = at(step, 0, part)
            for which, source, fields in (
                (0, a_ref, (A_BLOCK, A_ROW, A_ROW_REST, A_COL_REST)),
                (1, b_ref, (B_BLOCK, B_ROW, B_ROW_REST, B_COL_REST)),
            ):
                block, row, row_rest, col_rest = (items_ref[field, item] for field in fields)
                energies[item % RING, which] = extract(
                    source, block, row, row_rest, col_rest, (2 * part + which) * PATCH
                )
        half = jnp.dot(patches[...], table("across"), preferred_element_type=jnp.float32)
        halves[...] = half.astype(jnp.bfloat16)

    def sides(spec, group):
        cc = spec[16 * group : 16 * group + 8, :HALF_LANES]
        cs = spec[16 * group : 16 * group + 8, HALF_LANES:]
        sc = spec[16 * group + 8 : 16 * group + 16, :HALF_LANES]
        ss = spec[16 * group + 8 : 16 * group + 16, HALF_LANES:]
        return cc - ss, sc + cs, cc + ss, sc - cs

    def stage_inverse():
        down = table("down")
        for part in range(BATCH):
            base = 2 * part * PATCH
            spec_a = jnp.dot(
                down, halves[base : base + PATCH, :], preferred_element_type=jnp.float32
            )
            base = base + PATCH
            spec_b = jnp.dot(
                down, halves[base : base + PATCH, :], preferred_element_type=jnp.float32
            )
            for group in range(GROUPS):
                a_pr, a_pi, a_mr, a_mi = sides(spec_a, group)
                b_pr, b_pi, b_mr, b_mi = sides(spec_b, group)
                pr = a_pr * b_pr + a_pi * b_pi
                pi = a_pr * b_pi - a_pi * b_pr
                mr = a_mr * b_mr + a_mi * b_mi
                mi = a_mr * b_mi - a_mi * b_mr
                upper = jnp.concatenate([pr + mr, pi - mi], axis=1)
                lower = jnp.concatenate([pi + mi, mr - pr], axis=1)
                crosses[part, 16 * group : 16 * group + 16, :] = jnp.concatenate(
                    [upper, lower], axis=0
                ).astype(jnp.bfloat16)
        for part in range(BATCH):
            inverse = jnp.dot(
                table("back_down"), crosses[part], preferred_element_type=jnp.float32
            )
            inverses[PATCH * part : PATCH * (part + 1), :] = inverse.astype(jnp.bfloat16)

    def stage_score(step):
        corr_all = jnp.dot(
            inverses[...], table("back_across"), preferred_element_type=jnp.float32
        )
        rows = lax.broadcasted_iota(jnp.int32, (8, HALF_LANES), 0)
        lanes = lax.broadcasted_iota(jnp.int32, (8, HALF_LANES), 1)
        shift_rows = (rows - centre_reach).astype(jnp.float32)
        row_near = rows <= 2 * centre_reach
        for part in range(BATCH):
            item = at(step, 2, part)
            near_row = items_ref[NEAR_ROW, item]
            near_col = items_ref[NEAR_COL, item]
            ring = item % RING
            mean_a = jnp.sum(energies[ring, 0], keepdims=True) * (1.0 / (PATCH * PATCH))
            mean_b = jnp.sum(energies[ring, 1], keepdims=True) * (1.0 / (PATCH * PATCH))
            scale = 1.0 / (
                float(PATCH**4) * jnp.sqrt(mean_a + epsilon) * jnp.sqrt(mean_b + epsilon)
            )
            caps = caps_ref[pl.ds(PATCH - near_row, PATCH), :]
            total, row_moment, col_moment = 0.0, 0.0, 0.0
            best = None
            for half in range(2):
                corr = corr_all[
                    PATCH * part : PATCH * (part + 1),
                    half * HALF_LANES : (half + 1) * HALF_LANES,
                ]
                corrs[half][part, :PATCH, :] = corr
                corrs[half][part, PATCH:, :] = corr[:8]
                far = jnp.max(
                    jnp.minimum(corr, caps).reshape(PATCH // 8, 8, HALF_LANES), axis=0
                )
                if half == 0:
                    best = far
                else:
                    far = jnp.where(lanes < PATCH - HALF_LANES, far, -BIG)
                    best = jnp.maximum(best, far)
            for half in range(2):
                values = corrs[half][part, pl.ds(near_row, 8), :]
                place = lanes + half * HALF_LANES
                shift = place - near_col
                shift = jnp.where(shift >= PATCH // 2, shift - PATCH, shift)
                shift = jnp.where(shift < -(PATCH // 2), shift + PATCH, shift)
                inside = row_near & (place < PATCH)
                close = jnp.abs(shift) <= centre_reach
                weight = jnp.where(
                    inside & close, jnp.exp(sharpness * (values * scale)), 0.0
                )
                total = total + weight
                row_moment = row_moment + weight * shift_rows
                col_moment = col_moment + weight * shift.astype(jnp.float32)
                best = jnp.maximum(
                    best, jnp.where(inside & jnp.logical_not(close), values, -BIG)
                )
            totals[pl.ds(item, 1), :] = jnp.sum(total, axis=0, keepdims=True)
            row_moments[pl.ds(item, 1), :] = jnp.sum(row_moment, axis=0, keepdims=True)
            col_moments[pl.ds(item, 1), :] = jnp.sum(col_moment, axis=0, keepdims=True)
            runners[pl.ds(item, 1), :] = jnp.max(best * scale, axis=0, keepdims=True)

    to_scalars.wait()

    @pl.loop(0, (count + BATCH - 1) // BATCH + 2)
    def _(step):
        stage_score(step)
        stage_inverse()
        stage_half(step)

    used = lax.broadcasted_iota(jnp.int32, (capacity, 1), 0) < count
    total = jnp.sum(totals[...], axis=1, keepdims=True)
    peak_row = columns_ref[:, PEAK_ROW : PEAK_ROW + 1]
    peak_col = columns_ref[:, PEAK_COL : PEAK_COL + 1]
    results = (
        peak_row + jnp.sum(row_moments[...], axis=1, keepdims=True) / total,
        peak_col + jnp.sum(col_moments[...], axis=1, keepdims=True) / total,
        jnp.maximum(jnp.max(runners[...], axis=1, keepdims=True), -2.0),
    )
    lanes = lax.broadcasted_iota(jnp.int32, (capacity, HALF_LANES), 1)
    terms = [jnp.zeros((capacity, HALF_LANES), jnp.float32)] * 3
    for value, rest in enumerate(results):
        rest = jnp.where(used, rest, 0.0)
        for term in range(3):
            here = rest.astype(jnp.bfloat16).astype(jnp.float32)
            terms[term] = jnp.where(lanes // SPREAD_LANES == value, here, terms[term])
            rest = rest - here
    slot_row = rows_ref[MESH_ROW : MESH_ROW + 1, :]
    slot_col = columns_ref[:, MESH_COL : MESH_COL + 1]
    offset = (lanes % SPREAD_LANES - RELAX).astype(jnp.float32)
    shape = (n_row * SPREAD_ROWS, capacity)
    place = lax.broadcasted_iota(jnp.int32, shape, 0)
    row = place // SPREAD_ROWS * node_rows + place % SPREAD_ROWS - RELAX
    rows_picked = jnp.where(slot_row == row.astype(jnp.float32), 1.0, 0.0).astype(jnp.bfloat16)
    for col in range(n_col):
        here = slot_col == offset + float(col * NODE_LANES)
        sent = sum(
            jnp.dot(
                rows_picked,
                jnp.where(here, term, 0.0).astype(jnp.bfloat16),
                preferred_element_type=jnp.float32,
            )
            for term in terms
        )
        for row in range(n_row):
            out_ref[row * n_col + col] = sent[SPREAD_ROWS * row : SPREAD_ROWS * (row + 1)]


def list_nodes(
    capacity,
    grid,
    everyone_ref,
    table,
    columns_ref,
    rows_ref,
    listed_ref,
):
    n_row, n_col, a_rows, node_rows = grid
    me = (lax.axis_index("row") * n_col + lax.axis_index("col")).astype(jnp.float32)
    exact = functools.partial(lax.dot_general, preferred_element_type=jnp.float32)
    plain = (((1,), (0,)), ((), ()))
    turned = (((1,), (1,)), ((), ()))

    slot = lax.broadcasted_iota(jnp.int32, (capacity, HALF_LANES), 0).astype(jnp.float32)
    before = jnp.zeros((1, HALF_LANES), jnp.float32)
    found = jnp.zeros((capacity, 3 * HALF_LANES), jnp.float32)
    for block in range(n_row * n_col // 8):
        records = everyone_ref[8 * block : 8 * block + 8, a_rows : a_rows + 16, :]
        records = records.reshape(HALF_LANES, HALF_LANES)
        mine = exact(records, table("repeat"), plain) == me
        ones = jnp.where(mine, 1.0, 0.0).astype(jnp.bfloat16)
        counts = exact(ones, table("within"), plain)
        within, loads = counts[:, :HALF_LANES], counts[:, HALF_LANES:]
        base = exact(table("below"), loads.astype(jnp.bfloat16), plain) + before
        slots = jnp.where(mine, within + base, -1.0)
        row_loads = exact(table("count"), ones, turned)
        row_base = exact(row_loads.astype(jnp.bfloat16), table("above"), plain)[:1] + before
        holds = (slot >= row_base) & (slot < row_base + row_loads[:1])
        local = lax.broadcasted_iota(jnp.int32, (HALF_LANES, HALF_LANES), 0) % 16
        mesh_row = (local + 8 * block // n_col * node_rows).astype(jnp.float32)
        found = found + exact(
            jnp.where(holds, 1.0, 0.0).astype(jnp.bfloat16),
            jnp.concatenate(
                [records, slots.astype(jnp.bfloat16), mesh_row.astype(jnp.bfloat16)], axis=1
            ),
            plain,
        )
        before = before + jnp.sum(loads, axis=0, keepdims=True)

    same = found[:, HALF_LANES : 2 * HALF_LANES] == slot
    taken = jnp.concatenate(
        [jnp.where(same, found[:, :HALF_LANES], 0.0), found[:, 2 * HALF_LANES :]], axis=1
    ).astype(jnp.bfloat16)
    columns_ref[...] = exact(taken, table("fields"), plain)
    rows = exact(table("turned"), taken, turned)
    rows_ref[...] = rows

    def field(index):
        return rows[index : index + 1, :]

    def divide(value, by):
        whole = jnp.floor((value + 0.5) * (1.0 / by))
        return whole, value - whole * by

    half = float(PATCH // 2)
    b_top = jnp.maximum(16.0 * field(ROW_HIGH) + field(ROW_LOW) - half, 0.0)
    b_left = jnp.maximum(16.0 * field(COL_HIGH) + field(COL_LOW) - half, 0.0)
    a_top = STRIDE * field(MESH_ROW) + STRIDE // 2
    a_left = STRIDE * field(MESH_COL) + (STRIDE // 2 + half)
    b_group, b_row_rest = divide(b_top, 16)
    b_block, b_col_rest = divide(b_left, PATCH)
    a_group, a_row_rest = divide(a_top, 16)
    a_block, a_col_rest = divide(a_left, PATCH)
    near_row = divide(field(PEAK_ROW) + b_row_rest - a_row_rest - centre_reach, PATCH)[1]
    near_col = divide(field(PEAK_COL) + b_col_rest - a_col_rest, PATCH)[1]
    for index, value in (
        (B_BLOCK, b_block),
        (B_ROW, 16.0 * b_group),
        (B_ROW_REST, b_row_rest),
        (B_COL_REST, b_col_rest),
        (A_BLOCK, a_block),
        (A_ROW, 16.0 * a_group),
        (A_ROW_REST, a_row_rest),
        (A_COL_REST, a_col_rest),
        (NEAR_ROW, near_row),
        (NEAR_COL, near_col),
    ):
        listed_ref[index : index + 1, :] = value.astype(jnp.int32)
    listed_ref[FIELDS:, :] = jnp.zeros((16 - FIELDS, capacity), jnp.int32)
    return jnp.max(before).astype(jnp.int32)


def correlate(capacity, everyone, tile, grid):
    n_row, n_col, a_rows, node_rows = grid
    tables, places = all_tables()
    a_blocks = (n_col * everyone.shape[2] + 76) // PATCH + 2
    b_blocks = -(-tile.shape[1] // PATCH)
    vmem = pl.BlockSpec(memory_space=pltpu.VMEM)
    rows = pltpu.VMEM((capacity, HALF_LANES), jnp.float32)
    return pl.pallas_call(
        functools.partial(correlate_kernel, capacity, grid, places),
        out_shape=jax.ShapeDtypeStruct(
            (n_row * n_col, SPREAD_ROWS, HALF_LANES), jnp.float32
        ),
        in_specs=[vmem] * 3,
        out_specs=vmem,
        scratch_shapes=[
            pltpu.VMEM((2 * BATCH * PATCH, WIDE), jnp.bfloat16),
            pltpu.VMEM((2 * BATCH * PATCH, WIDE), jnp.bfloat16),
            pltpu.VMEM((BATCH, PAIRED, WIDE), jnp.bfloat16),
            pltpu.VMEM((BATCH * PATCH, WIDE), jnp.bfloat16),
            pltpu.VMEM((BATCH, PATCH + 8, HALF_LANES), jnp.float32),
            pltpu.VMEM((BATCH, PATCH + 8, HALF_LANES), jnp.float32),
            pltpu.VMEM((RING, 2, 8, HALF_LANES), jnp.float32),
        ]
        + [rows] * 4
        + [
            pltpu.VMEM((a_blocks, n_row * a_rows + PATCH, WIDE), jnp.bfloat16),
            pltpu.VMEM((b_blocks, tile.shape[0] + 16, WIDE), jnp.bfloat16),
            rows,
            pltpu.VMEM((16, capacity), jnp.int32),
            pltpu.SMEM((16, capacity), jnp.int32),
            pltpu.SemaphoreType.DMA,
            pltpu.VMEM((2 * PATCH, HALF_LANES), jnp.float32),
            pltpu.VMEM((16, capacity), jnp.float32),
        ],
        compiler_params=pltpu.CompilerParams(vmem_limit_bytes=40 * 1024 * 1024),
    )(everyone, tile, tables)


def per_device(a_window, b_section, owners, pos_rows, pos_cols, peaks):
    node_rows, node_cols = pos_rows.shape
    nodes = node_rows * node_cols
    n_row, n_col = lax.axis_size("row"), lax.axis_size("col")
    devices = n_row * n_col
    me_row, me_col = lax.axis_index("row"), lax.axis_index("col")
    share = max(2, (nodes * 8 // 5 + devices - 1) // devices)
    a_rows, a_cols = a_window.shape
    height, breadth = n_row * node_rows, n_col * node_cols

    mesh_col = me_col * node_cols + lax.broadcasted_iota(jnp.int32, pos_rows.shape, 1)
    records = jnp.concatenate(
        [
            owners.reshape(node_rows, node_cols),
            pos_rows // 16,
            pos_rows % 16,
            pos_cols // 16,
            pos_cols % 16,
            peaks[0],
            peaks[1],
            mesh_col,
        ],
        axis=1,
    ).astype(jnp.bfloat16)
    records = jnp.pad(records, ((0, 16 - node_rows), (0, 0)), constant_values=-1)
    sent = jnp.concatenate([a_window, records], axis=0)
    sent = jnp.broadcast_to(sent[None], (n_col,) + sent.shape)
    sent = lax.all_to_all(sent, "col", split_axis=0, concat_axis=0, tiled=True)
    everyone = lax.all_gather(sent, "row").reshape(devices, a_rows + 16, a_cols)

    grid = (n_row, n_col, a_rows, node_rows)
    spread = correlate(share * devices, everyone, b_section, grid)
    spread = lax.all_to_all(spread, ("row", "col"), split_axis=0, concat_axis=0, tiled=True)
    tall, broad = node_rows + 2 * RELAX, node_cols + 2 * RELAX
    spread = jnp.sum(spread, axis=0)[:tall]
    spread = [spread[:, SPREAD_LANES * value :][:, :broad] for value in range(3)]
    runner = spread[2][RELAX:-RELAX, RELAX:-RELAX]
    field = jnp.stack(spread[:2])
    for step in range(RELAX):
        reach = RELAX - 1 - step
        centre = field[:, 1:-1, 1:-1]
        around = (
            field[:, 2:, 1:-1] + field[:, :-2, 1:-1] + field[:, 1:-1, 2:] + field[:, 1:-1, :-2]
        )
        field = centre + stiffness * (around - 4.0 * centre)
        rows = me_row * node_rows - reach + jnp.arange(node_rows + 2 * reach)
        cols = me_col * node_cols - reach + jnp.arange(node_cols + 2 * reach)
        inside = ((rows >= 0) & (rows < height))[:, None] & ((cols >= 0) & (cols < breadth))[None]
        field = jnp.where(inside[None], field, 0.0)
    return (field, runner)


def solution(mesh):
    placed = (
        P("row", "col"),
        P("row", "col"),
        P("row", "col", None, None, None),
        P("row", "col"),
        P("row", "col"),
        P(None, "row", "col"),
    )
    return jax.shard_map(
        per_device,
        mesh=mesh,
        in_specs=placed,
        out_specs=(P(None, "row", "col"), P("row", "col")),
        check_vma=False,
    )
```

```python
import functools
import math

import jax
import jax.numpy as jnp
import numpy as np
from jax import lax
from jax.experimental import pallas as pl
from jax.experimental.pallas import tpu as pltpu
from jax.sharding import PartitionSpec as P

PATCH = 160
NODE_LANES = 16
SPREAD_LANES = 20
SPREAD_ROWS = 16
STRIDE = 8
RELAX = 2
WIDE = 256
HALF_LANES = 128
FREQS = PATCH // 2 + 1
GROUPS = 11
PAIRED = 16 * GROUPS
BIG = 3.0e38

sharpness = 80.0
epsilon = 1e-06
stiffness = 0.24
centre_reach = 2


def dft_tables():
    steps = np.arange(PATCH)
    angles = 2.0 * math.pi * ((steps[:, None] * steps[None, :FREQS]) % PATCH) / PATCH
    return (
        np.cos(angles).astype(jnp.bfloat16).astype(np.float32),
        np.sin(angles).astype(jnp.bfloat16).astype(np.float32),
    )


def kernel_tables():
    cosine, sine = dft_tables()
    weights = np.full((FREQS,), 2.0, np.float32)
    weights[0] = weights[-1] = 1.0
    across = np.zeros((WIDE, WIDE), np.float32)
    across[:PATCH, :FREQS] = cosine
    across[:PATCH, HALF_LANES : HALF_LANES + FREQS] = sine
    back_across = np.zeros((WIDE, WIDE), np.float32)
    back_across[:FREQS, :PATCH] = 0.5 * (cosine * weights).T
    back_across[HALF_LANES : HALF_LANES + FREQS, :PATCH] = 0.5 * (sine * weights).T
    down = np.zeros((PAIRED, PATCH), np.float32)
    back_down = np.zeros((PATCH, PAIRED), np.float32)
    for freq in range(FREQS):
        row = 16 * (freq // 8) + freq % 8
        down[row] = cosine[:, freq]
        down[row + 8] = sine[:, freq]
        back_down[:, row] = cosine[:, freq] * weights[freq]
        back_down[:, row + 8] = sine[:, freq] * weights[freq]
    return across, down, back_down, back_across


def listing_tables():
    lane = np.arange(HALF_LANES)
    group, place = lane // NODE_LANES, lane % NODE_LANES
    repeat = (lane[:, None] < NODE_LANES) & (place[None] == lane[:, None])
    earlier = (group[:, None] == group[None]) & (place[:, None] < place[None])
    first = np.broadcast_to(lane[:, None] < NODE_LANES, (HALF_LANES, HALF_LANES))
    below = lane[None] < lane[:, None]
    fields = np.zeros((2 * HALF_LANES, HALF_LANES), np.float32)
    fields[lane, group] = 1.0
    fields[HALF_LANES, MESH_ROW] = 1.0
    return repeat, np.concatenate([earlier, first], axis=1), below, below.T, first.T[:16], fields, (
        fields.T[:16]
    )


def all_tables():
    names = ("across", "down", "back_down", "back_across", "repeat", "within")
    names += ("below", "above", "count", "fields", "turned")
    places, parts, start = {}, [], 0
    for name, part in zip(names, kernel_tables() + listing_tables()):
        rows, lanes = part.shape
        places[name] = (start, rows, lanes)
        rows_up = -(-rows // 16) * 16
        parts.append(np.zeros((rows_up, WIDE), np.float32))
        parts[-1][:rows, :lanes] = part
        start += rows_up
    return jnp.asarray(np.concatenate(parts), jnp.bfloat16), places


OWNER, ROW_HIGH, ROW_LOW, COL_HIGH, COL_LOW, PEAK_ROW, PEAK_COL, MESH_COL, MESH_ROW = range(9)
B_BLOCK, B_ROW, B_ROW_REST, B_COL_REST = 0, 1, 2, 3
A_BLOCK, A_ROW, A_ROW_REST, A_COL_REST = 4, 5, 6, 7
NEAR_ROW, NEAR_COL = 8, 9
FIELDS = 10
BATCH = 6
RING = 32
TRIO = 3
SECOND = FREQS
THIRD = 2 * FREQS - HALF_LANES


def cut(strip, start):
    if start >= strip.shape[1]:
        return jnp.zeros((strip.shape[0], WIDE), strip.dtype)
    piece = strip[:, start : min(start + PATCH, strip.shape[1])]
    gap = jnp.zeros((strip.shape[0], WIDE - piece.shape[1]), strip.dtype)
    return jnp.concatenate([piece, gap], axis=1)


def correlate_kernel(
    capacity,
    grid,
    places,
    everyone_ref,
    blocks_ref,
    tables_ref,
    out_ref,
    *scratch,
):
    patches, halves, crosses, inverses = scratch[:4]
    corrs = scratch[4:6]
    energies, totals, row_moments, col_moments, runners, a_ref, b_ref = scratch[6:13]
    columns_ref, listed_ref, items_ref, semaphores, caps_ref, rows_ref = scratch[13:]
    to_blocks = pltpu.make_async_copy(blocks_ref, b_ref, semaphores.at[0])
    to_blocks.start()

    def table(name):
        start, rows, lanes = places[name]
        return tables_ref[start : start + rows, :lanes]

    n_row, n_col, a_rows, node_rows = grid
    count = list_nodes(
        capacity,
        grid,
        everyone_ref,
        table,
        columns_ref,
        rows_ref,
        listed_ref,
    )
    caps_row = lax.broadcasted_iota(jnp.int32, caps_ref.shape, 0) % PATCH
    caps_ref[...] = jnp.where(caps_row <= 2 * centre_reach, -BIG, BIG)
    to_scalars = pltpu.make_async_copy(listed_ref, items_ref, semaphores.at[1])
    to_scalars.start()

    a_ref[0] = jnp.zeros(a_ref.shape[1:], jnp.bfloat16)
    rim = jnp.zeros((a_ref.shape[0], PATCH // 2, WIDE), jnp.bfloat16)
    a_ref[:, : PATCH // 2, :] = rim
    a_ref[:, a_ref.shape[1] - PATCH // 2 :, :] = rim

    @pl.loop(0, n_row)
    def _(row):
        strip = jnp.concatenate(
            [everyone_ref[row * n_col + col, :a_rows, :] for col in range(n_col)], axis=1
        )
        place = pl.ds(pl.multiple_of(PATCH // 2 + row * a_rows, 16), a_rows)
        for block in range(1, a_ref.shape[0]):
            a_ref[block, place, :] = cut(strip, (block - 1) * PATCH)

    def at(step, stage, part):
        return jnp.clip(BATCH * (step - stage) + part, 0, capacity - 1)

    def extract(source, block, row, row_rest, col_rest, base):
        lanes = lax.broadcasted_iota(jnp.int32, (16, WIDE), 1) >= col_rest
        rows = lax.broadcasted_iota(jnp.int32, (16, WIDE), 0) >= row_rest

        def group(place):
            here = pl.ds(pl.multiple_of(row + 16 * place, 16), 16)
            return jnp.where(lanes, source[block, here, :], source[block + 1, here, :])

        total = jnp.zeros((8, WIDE), jnp.float32)
        for place in range(PATCH // 16):
            values = group(place)
            if place == 0:
                values = jnp.where(rows, values, group(PATCH // 16))
            patches[base + 16 * place : base + 16 * place + 16, :] = values
            values = values.astype(jnp.float32)
            values = values * values
            total = total + (values[:8] + values[8:])
        return total[:, :HALF_LANES] + total[:, HALF_LANES:]

    def patch_base(part, which):
        trio, place = divmod(part, TRIO)
        return ((2 * trio + which) * TRIO + place) * PATCH

    def stage_half(step):
        for part in range(BATCH):
            item = at(step, 0, part)
            for which, source, fields in (
                (0, a_ref, (A_BLOCK, A_ROW, A_ROW_REST, A_COL_REST)),
                (1, b_ref, (B_BLOCK, B_ROW, B_ROW_REST, B_COL_REST)),
            ):
                block, row, row_rest, col_rest = (items_ref[field, item] for field in fields)
                energies[item % RING, which] = extract(
                    source, block, row, row_rest, col_rest, patch_base(part, which)
                )
        half = jnp.dot(patches[...], table("across"), preferred_element_type=jnp.float32)
        lanes = lax.broadcasted_iota(jnp.int32, (PATCH, HALF_LANES), 1)
        for trio in range(BATCH // TRIO):
            for which in range(2):
                for side in (slice(0, HALF_LANES), slice(HALF_LANES, WIDE)):
                    first, second, third = (
                        half[base : base + PATCH, side]
                        for base in (patch_base(TRIO * trio + n, which) for n in range(TRIO))
                    )
                    second = pltpu.roll(second, SECOND, axis=1)
                    third = pltpu.roll(third, THIRD, axis=1)
                    halves[trio, which, 0, :, side] = jnp.where(
                        lanes < SECOND, first, second
                    ).astype(jnp.bfloat16)
                    halves[trio, which, 1, :, side] = jnp.where(
                        lanes < THIRD, second, third
                    ).astype(jnp.bfloat16)

    def sides(spec, group):
        cc = spec[16 * group : 16 * group + 8, :HALF_LANES]
        cs = spec[16 * group : 16 * group + 8, HALF_LANES:]
        sc = spec[16 * group + 8 : 16 * group + 16, :HALF_LANES]
        ss = spec[16 * group + 8 : 16 * group + 16, HALF_LANES:]
        return cc - ss, sc + cs, cc + ss, sc - cs

    def stage_inverse():
        down = table("down")
        for pair in range(2 * (BATCH // TRIO)):
            trio, tile = divmod(pair, 2)
            spec_a = jnp.dot(down, halves[trio, 0, tile], preferred_element_type=jnp.float32)
            spec_b = jnp.dot(down, halves[trio, 1, tile], preferred_element_type=jnp.float32)
            for group in range(GROUPS):
                a_pr, a_pi, a_mr, a_mi = sides(spec_a, group)
                b_pr, b_pi, b_mr, b_mi = sides(spec_b, group)
                pr = a_pr * b_pr + a_pi * b_pi
                pi = a_pr * b_pi - a_pi * b_pr
                mr = a_mr * b_mr + a_mi * b_mi
                mi = a_mr * b_mi - a_mi * b_mr
                upper = jnp.concatenate([pr + mr, pi - mi], axis=1)
                lower = jnp.concatenate([pi + mi, mr - pr], axis=1)
                crosses[pair, 16 * group : 16 * group + 16, :] = jnp.concatenate(
                    [upper, lower], axis=0
                ).astype(jnp.bfloat16)
        lanes = lax.broadcasted_iota(jnp.int32, (PATCH, HALF_LANES), 1)
        for trio in range(BATCH // TRIO):
            low, high = (
                jnp.dot(
                    table("back_down"), crosses[2 * trio + tile], preferred_element_type=jnp.float32
                )
                for tile in range(2)
            )
            for side in (slice(0, HALF_LANES), slice(HALF_LANES, WIDE)):
                first = low[:, side]
                second = jnp.where(lanes >= SECOND, first, high[:, side])
                second = pltpu.roll(second, HALF_LANES - SECOND, axis=1)
                third = pltpu.roll(high[:, side], HALF_LANES - THIRD, axis=1)
                for place, inverse in enumerate((first, second, third)):
                    base = (TRIO * trio + place) * PATCH
                    inverses[base : base + PATCH, side] = inverse.astype(jnp.bfloat16)

    def stage_score(step):
        corr_all = jnp.dot(
            inverses[...], table("back_across"), preferred_element_type=jnp.float32
        )
        rows = lax.broadcasted_iota(jnp.int32, (8, HALF_LANES), 0)
        lanes = lax.broadcasted_iota(jnp.int32, (8, HALF_LANES), 1)
        shift_rows = (rows - centre_reach).astype(jnp.float32)
        row_near = rows <= 2 * centre_reach
        for part in range(BATCH):
            item = at(step, 2, part)
            near_row = items_ref[NEAR_ROW, item]
            near_col = items_ref[NEAR_COL, item]
            ring = item % RING
            mean_a = jnp.sum(energies[ring, 0], keepdims=True) * (1.0 / (PATCH * PATCH))
            mean_b = jnp.sum(energies[ring, 1], keepdims=True) * (1.0 / (PATCH * PATCH))
            scale = 1.0 / (
                float(PATCH**4) * jnp.sqrt(mean_a + epsilon) * jnp.sqrt(mean_b + epsilon)
            )
            caps = caps_ref[pl.ds(PATCH - near_row, PATCH), :]
            total, row_moment, col_moment = 0.0, 0.0, 0.0
            best = None
            for half in range(2):
                corr = corr_all[
                    PATCH * part : PATCH * (part + 1),
                    half * HALF_LANES : (half + 1) * HALF_LANES,
                ]
                corrs[half][part, :PATCH, :] = corr
                corrs[half][part, PATCH:, :] = corr[:8]
                far = jnp.max(
                    jnp.minimum(corr, caps).reshape(PATCH // 8, 8, HALF_LANES), axis=0
                )
                if half == 0:
                    best = far
                else:
                    far = jnp.where(lanes < PATCH - HALF_LANES, far, -BIG)
                    best = jnp.maximum(best, far)
            for half in range(2):
                values = corrs[half][part, pl.ds(near_row, 8), :]
                place = lanes + half * HALF_LANES
                shift = place - near_col
                shift = jnp.where(shift >= PATCH // 2, shift - PATCH, shift)
                shift = jnp.where(shift < -(PATCH // 2), shift + PATCH, shift)
                inside = row_near & (place < PATCH)
                close = jnp.abs(shift) <= centre_reach
                weight = jnp.where(
                    inside & close, jnp.exp(sharpness * (values * scale)), 0.0
                )
                total = total + weight
                row_moment = row_moment + weight * shift_rows
                col_moment = col_moment + weight * shift.astype(jnp.float32)
                best = jnp.maximum(
                    best, jnp.where(inside & jnp.logical_not(close), values, -BIG)
                )
            totals[pl.ds(item, 1), :] = jnp.sum(total, axis=0, keepdims=True)
            row_moments[pl.ds(item, 1), :] = jnp.sum(row_moment, axis=0, keepdims=True)
            col_moments[pl.ds(item, 1), :] = jnp.sum(col_moment, axis=0, keepdims=True)
            runners[pl.ds(item, 1), :] = jnp.max(best * scale, axis=0, keepdims=True)

    to_scalars.wait()
    to_blocks.wait()

    @pl.loop(0, (count + BATCH - 1) // BATCH + 2)
    def _(step):
        stage_score(step)
        stage_inverse()
        stage_half(step)

    used = lax.broadcasted_iota(jnp.int32, (capacity, 1), 0) < count
    total = jnp.sum(totals[...], axis=1, keepdims=True)
    peak_row = columns_ref[:, PEAK_ROW : PEAK_ROW + 1]
    peak_col = columns_ref[:, PEAK_COL : PEAK_COL + 1]
    results = (
        peak_row + jnp.sum(row_moments[...], axis=1, keepdims=True) / total,
        peak_col + jnp.sum(col_moments[...], axis=1, keepdims=True) / total,
        jnp.maximum(jnp.max(runners[...], axis=1, keepdims=True), -2.0),
    )
    lanes = lax.broadcasted_iota(jnp.int32, (capacity, HALF_LANES), 1)
    terms = [jnp.zeros((capacity, HALF_LANES), jnp.float32)] * 3
    for value, rest in enumerate(results):
        rest = jnp.where(used, rest, 0.0)
        for term in range(3):
            here = rest.astype(jnp.bfloat16).astype(jnp.float32)
            terms[term] = jnp.where(lanes // SPREAD_LANES == value, here, terms[term])
            rest = rest - here
    slot_row = rows_ref[MESH_ROW : MESH_ROW + 1, :]
    slot_col = columns_ref[:, MESH_COL : MESH_COL + 1]
    offset = (lanes % SPREAD_LANES - RELAX).astype(jnp.float32)
    shape = (n_row * SPREAD_ROWS, capacity)
    place = lax.broadcasted_iota(jnp.int32, shape, 0)
    row = place // SPREAD_ROWS * node_rows + place % SPREAD_ROWS - RELAX
    rows_picked = jnp.where(slot_row == row.astype(jnp.float32), 1.0, 0.0).astype(jnp.bfloat16)
    for col in range(n_col):
        here = slot_col == offset + float(col * NODE_LANES)
        sent = sum(
            jnp.dot(
                rows_picked,
                jnp.where(here, term, 0.0).astype(jnp.bfloat16),
                preferred_element_type=jnp.float32,
            )
            for term in terms
        )
        for row in range(n_row):
            block = sent[SPREAD_ROWS * row : SPREAD_ROWS * (row + 1)]
            turned = pltpu.roll(block[8:], HALF_LANES // 2, axis=1)
            out_ref[row * n_col + col] = jnp.where(
                lanes[:8] < HALF_LANES // 2, block[:8], turned
            )


def list_nodes(
    capacity,
    grid,
    everyone_ref,
    table,
    columns_ref,
    rows_ref,
    listed_ref,
):
    n_row, n_col, a_rows, node_rows = grid
    me = (lax.axis_index("row") * n_col + lax.axis_index("col")).astype(jnp.float32)
    exact = functools.partial(lax.dot_general, preferred_element_type=jnp.float32)
    plain = (((1,), (0,)), ((), ()))
    turned = (((1,), (1,)), ((), ()))

    slot = lax.broadcasted_iota(jnp.int32, (capacity, HALF_LANES), 0).astype(jnp.float32)
    before = jnp.zeros((1, HALF_LANES), jnp.float32)
    found = jnp.zeros((capacity, 3 * HALF_LANES), jnp.float32)
    for block in range(n_row * n_col // 8):
        records = everyone_ref[8 * block : 8 * block + 8, a_rows : a_rows + 16, :]
        records = records.reshape(HALF_LANES, HALF_LANES)
        mine = exact(records, table("repeat"), plain) == me
        ones = jnp.where(mine, 1.0, 0.0).astype(jnp.bfloat16)
        counts = exact(ones, table("within"), plain)
        within, loads = counts[:, :HALF_LANES], counts[:, HALF_LANES:]
        base = exact(table("below"), loads.astype(jnp.bfloat16), plain) + before
        slots = jnp.where(mine, within + base, -1.0)
        row_loads = exact(table("count"), ones, turned)
        row_base = exact(row_loads.astype(jnp.bfloat16), table("above"), plain)[:1] + before
        holds = (slot >= row_base) & (slot < row_base + row_loads[:1])
        local = lax.broadcasted_iota(jnp.int32, (HALF_LANES, HALF_LANES), 0) % 16
        mesh_row = (local + 8 * block // n_col * node_rows).astype(jnp.float32)
        found = found + exact(
            jnp.where(holds, 1.0, 0.0).astype(jnp.bfloat16),
            jnp.concatenate(
                [records, slots.astype(jnp.bfloat16), mesh_row.astype(jnp.bfloat16)], axis=1
            ),
            plain,
        )
        before = before + jnp.sum(loads, axis=0, keepdims=True)

    same = found[:, HALF_LANES : 2 * HALF_LANES] == slot
    taken = jnp.concatenate(
        [jnp.where(same, found[:, :HALF_LANES], 0.0), found[:, 2 * HALF_LANES :]], axis=1
    ).astype(jnp.bfloat16)
    columns_ref[...] = exact(taken, table("fields"), plain)
    rows = exact(table("turned"), taken, turned)
    rows_ref[...] = rows

    def field(index):
        return rows[index : index + 1, :]

    def divide(value, by):
        whole = jnp.floor((value + 0.5) * (1.0 / by))
        return whole, value - whole * by

    half = float(PATCH // 2)
    b_top = jnp.maximum(16.0 * field(ROW_HIGH) + field(ROW_LOW) - half, 0.0)
    b_left = jnp.maximum(16.0 * field(COL_HIGH) + field(COL_LOW) - half, 0.0)
    a_top = STRIDE * field(MESH_ROW) + STRIDE // 2
    a_left = STRIDE * field(MESH_COL) + (STRIDE // 2 + half)
    b_group, b_row_rest = divide(b_top, 16)
    b_block, b_col_rest = divide(b_left, PATCH)
    a_group, a_row_rest = divide(a_top, 16)
    a_block, a_col_rest = divide(a_left, PATCH)
    near_row = divide(field(PEAK_ROW) + b_row_rest - a_row_rest - centre_reach, PATCH)[1]
    near_col = divide(field(PEAK_COL) + b_col_rest - a_col_rest, PATCH)[1]
    for index, value in (
        (B_BLOCK, b_block),
        (B_ROW, 16.0 * b_group),
        (B_ROW_REST, b_row_rest),
        (B_COL_REST, b_col_rest),
        (A_BLOCK, a_block),
        (A_ROW, 16.0 * a_group),
        (A_ROW_REST, a_row_rest),
        (A_COL_REST, a_col_rest),
        (NEAR_ROW, near_row),
        (NEAR_COL, near_col),
    ):
        listed_ref[index : index + 1, :] = value.astype(jnp.int32)
    listed_ref[FIELDS:, :] = jnp.zeros((16 - FIELDS, capacity), jnp.int32)
    return jnp.max(before).astype(jnp.int32)


def cut_kernel(tile_ref, out_ref):
    strip = tile_ref[...]
    for block in range(out_ref.shape[0]):
        out_ref[block] = cut(strip, block * PATCH)


def cut_tile(tile):
    rows, cols = tile.shape
    blocks = -(-cols // PATCH)
    return pl.pallas_call(
        cut_kernel,
        grid=(rows // HALF_LANES,),
        out_shape=jax.ShapeDtypeStruct((blocks, rows + 16, WIDE), jnp.bfloat16),
        in_specs=[pl.BlockSpec((HALF_LANES, cols), lambda step: (step, 0))],
        out_specs=pl.BlockSpec((blocks, HALF_LANES, WIDE), lambda step: (0, step, 0)),
        cost_estimate=pl.CostEstimate(
            flops=0, bytes_accessed=2 * rows * (cols + blocks * WIDE), transcendentals=0
        ),
    )(tile)


def correlate(capacity, everyone, blocks, grid):
    n_row, n_col, a_rows, node_rows = grid
    tables, places = all_tables()
    a_blocks = (n_col * everyone.shape[2] + 76) // PATCH + 2
    vmem = pl.BlockSpec(memory_space=pltpu.VMEM)
    rows = pltpu.VMEM((capacity, HALF_LANES), jnp.float32)
    return pl.pallas_call(
        functools.partial(correlate_kernel, capacity, grid, places),
        out_shape=jax.ShapeDtypeStruct(
            (n_row * n_col, SPREAD_ROWS // 2, HALF_LANES), jnp.float32
        ),
        in_specs=[vmem, pl.BlockSpec(memory_space=pl.ANY), vmem],
        out_specs=vmem,
        scratch_shapes=[
            pltpu.VMEM((2 * BATCH * PATCH, WIDE), jnp.bfloat16),
            pltpu.VMEM((BATCH // TRIO, 2, 2, PATCH, WIDE), jnp.bfloat16),
            pltpu.VMEM((BATCH // TRIO * 2, PAIRED, WIDE), jnp.bfloat16),
            pltpu.VMEM((BATCH * PATCH, WIDE), jnp.bfloat16),
            pltpu.VMEM((BATCH, PATCH + 8, HALF_LANES), jnp.float32),
            pltpu.VMEM((BATCH, PATCH + 8, HALF_LANES), jnp.float32),
            pltpu.VMEM((RING, 2, 8, HALF_LANES), jnp.float32),
        ]
        + [rows] * 4
        + [
            pltpu.VMEM((a_blocks, n_row * a_rows + PATCH, WIDE), jnp.bfloat16),
            pltpu.VMEM(blocks.shape, jnp.bfloat16),
            rows,
            pltpu.VMEM((16, capacity), jnp.int32),
            pltpu.SMEM((16, capacity), jnp.int32),
            pltpu.SemaphoreType.DMA((2,)),
            pltpu.VMEM((2 * PATCH, HALF_LANES), jnp.float32),
            pltpu.VMEM((16, capacity), jnp.float32),
        ],
        compiler_params=pltpu.CompilerParams(vmem_limit_bytes=40 * 1024 * 1024),
    )(everyone, blocks, tables)


def per_device(a_window, b_section, owners, pos_rows, pos_cols, peaks):
    node_rows, node_cols = pos_rows.shape
    nodes = node_rows * node_cols
    n_row, n_col = lax.axis_size("row"), lax.axis_size("col")
    devices = n_row * n_col
    me_row, me_col = lax.axis_index("row"), lax.axis_index("col")
    share = max(2, (nodes * 8 // 5 + devices - 1) // devices)
    a_rows, a_cols = a_window.shape
    height, breadth = n_row * node_rows, n_col * node_cols

    mesh_col = me_col * node_cols + lax.broadcasted_iota(jnp.int32, pos_rows.shape, 1)
    records = jnp.concatenate(
        [
            owners.reshape(node_rows, node_cols),
            pos_rows // 16,
            pos_rows % 16,
            pos_cols // 16,
            pos_cols % 16,
            peaks[0],
            peaks[1],
            mesh_col,
        ],
        axis=1,
    ).astype(jnp.bfloat16)
    records = jnp.pad(records, ((0, 16 - node_rows), (0, 0)), constant_values=-1)
    sent = jnp.concatenate([a_window, records], axis=0)
    sent = jnp.broadcast_to(sent[None], (n_col,) + sent.shape)
    sent = lax.all_to_all(sent, "col", split_axis=0, concat_axis=0, tiled=True)
    everyone = lax.all_gather(sent, "row").reshape(devices, a_rows + 16, a_cols)

    grid = (n_row, n_col, a_rows, node_rows)
    spread = correlate(share * devices, everyone, cut_tile(b_section), grid)
    spread = lax.all_to_all(spread, ("row", "col"), split_axis=0, concat_axis=0, tiled=True)
    tall, broad = node_rows + 2 * RELAX, node_cols + 2 * RELAX
    spread = jnp.sum(spread, axis=0)
    half_lanes = HALF_LANES // 2
    spread = jnp.concatenate([spread[:, :half_lanes], spread[:, half_lanes:]], axis=0)[:tall]
    spread = [spread[:, SPREAD_LANES * value :][:, :broad] for value in range(3)]
    runner = spread[2][RELAX:-RELAX, RELAX:-RELAX]
    field = jnp.stack(spread[:2])
    for step in range(RELAX):
        reach = RELAX - 1 - step
        centre = field[:, 1:-1, 1:-1]
        around = (
            field[:, 2:, 1:-1] + field[:, :-2, 1:-1] + field[:, 1:-1, 2:] + field[:, 1:-1, :-2]
        )
        field = centre + stiffness * (around - 4.0 * centre)
        rows = me_row * node_rows - reach + jnp.arange(node_rows + 2 * reach)
        cols = me_col * node_cols - reach + jnp.arange(node_cols + 2 * reach)
        inside = ((rows >= 0) & (rows < height))[:, None] & ((cols >= 0) & (cols < breadth))[None]
        field = jnp.where(inside[None], field, 0.0)
    return (field, runner)


def solution(mesh):
    placed = (
        P("row", "col"),
        P("row", "col"),
        P("row", "col", None, None, None),
        P("row", "col"),
        P("row", "col"),
        P(None, "row", "col"),
    )
    return jax.shard_map(
        per_device,
        mesh=mesh,
        in_specs=placed,
        out_specs=(P(None, "row", "col"), P("row", "col")),
        check_vma=False,
    )
```

```python
import functools
import math

import jax
import jax.numpy as jnp
import numpy as np
from jax import lax
from jax.experimental import pallas as pl
from jax.experimental.pallas import tpu as pltpu
from jax.sharding import PartitionSpec as P

PATCH = 160
NODE_LANES = 16
SPREAD_LANES = 20
SPREAD_ROWS = 16
STRIDE = 8
RELAX = 2
WIDE = 256
HALF_LANES = 128
FREQS = PATCH // 2 + 1
GROUPS = 11
PAIRED = 16 * GROUPS
BIG = 3.0e38

sharpness = 80.0
epsilon = 1e-06
stiffness = 0.24
centre_reach = 2


def dft_tables():
    steps = np.arange(PATCH)
    angles = 2.0 * math.pi * ((steps[:, None] * steps[None, :FREQS]) % PATCH) / PATCH
    return (
        np.cos(angles).astype(jnp.bfloat16).astype(np.float32),
        np.sin(angles).astype(jnp.bfloat16).astype(np.float32),
    )


def kernel_tables():
    cosine, sine = dft_tables()
    weights = np.full((FREQS,), 2.0, np.float32)
    weights[0] = weights[-1] = 1.0
    across = np.zeros((WIDE, WIDE), np.float32)
    across[:PATCH, :FREQS] = cosine
    across[:PATCH, HALF_LANES : HALF_LANES + FREQS] = sine
    back_across = np.zeros((WIDE, WIDE), np.float32)
    back_across[:FREQS, :PATCH] = 0.5 * (cosine * weights).T
    back_across[HALF_LANES : HALF_LANES + FREQS, :PATCH] = 0.5 * (sine * weights).T
    down = np.zeros((PAIRED, PATCH), np.float32)
    back_down = np.zeros((PATCH, PAIRED), np.float32)
    for freq in range(FREQS):
        row = 16 * (freq // 8) + freq % 8
        down[row] = cosine[:, freq]
        down[row + 8] = sine[:, freq]
        back_down[:, row] = cosine[:, freq] * weights[freq]
        back_down[:, row + 8] = sine[:, freq] * weights[freq]
    return across, down, back_down, back_across


def listing_tables():
    lane = np.arange(HALF_LANES)
    group, place = lane // NODE_LANES, lane % NODE_LANES
    repeat = (lane[:, None] < NODE_LANES) & (place[None] == lane[:, None])
    earlier = (group[:, None] == group[None]) & (place[:, None] < place[None])
    first = np.broadcast_to(lane[:, None] < NODE_LANES, (HALF_LANES, HALF_LANES))
    below = lane[None] < lane[:, None]
    fields = np.zeros((2 * HALF_LANES, HALF_LANES), np.float32)
    fields[lane, group] = 1.0
    fields[HALF_LANES, MESH_ROW] = 1.0
    return repeat, np.concatenate([earlier, first], axis=1), below, below.T, first.T[:16], fields, (
        fields.T[:16]
    )


def all_tables():
    names = ("across", "down", "back_down", "back_across", "repeat", "within")
    names += ("below", "above", "count", "fields", "turned")
    places, parts, start = {}, [], 0
    for name, part in zip(names, kernel_tables() + listing_tables()):
        rows, lanes = part.shape
        places[name] = (start, rows, lanes)
        rows_up = -(-rows // 16) * 16
        parts.append(np.zeros((rows_up, WIDE), np.float32))
        parts[-1][:rows, :lanes] = part
        start += rows_up
    return jnp.asarray(np.concatenate(parts), jnp.bfloat16), places


OWNER, ROW_HIGH, ROW_LOW, COL_HIGH, COL_LOW, PEAK_ROW, PEAK_COL, MESH_COL, MESH_ROW = range(9)
B_BLOCK, B_ROW, B_ROW_REST, B_COL_REST = 0, 1, 2, 3
A_BLOCK, A_ROW, A_ROW_REST, A_COL_REST = 4, 5, 6, 7
NEAR_ROW, NEAR_COL = 8, 9
FIELDS = 10
BATCH = 3
RING = 16
TRIO = 3
SECOND = FREQS
THIRD = 2 * FREQS - HALF_LANES


def cut(strip, start):
    if start >= strip.shape[1]:
        return jnp.zeros((strip.shape[0], WIDE), strip.dtype)
    piece = strip[:, start : min(start + PATCH, strip.shape[1])]
    gap = jnp.zeros((strip.shape[0], WIDE - piece.shape[1]), strip.dtype)
    return jnp.concatenate([piece, gap], axis=1)


def correlate_kernel(
    capacity,
    grid,
    places,
    everyone_ref,
    blocks_ref,
    tables_ref,
    out_ref,
    *scratch,
):
    patches, halves, crosses, inverses = scratch[:4]
    corrs = scratch[4:6]
    energies, totals, row_moments, col_moments, runners, a_ref, b_ref = scratch[6:13]
    columns_ref, listed_ref, items_ref, semaphores, caps_ref, rows_ref = scratch[13:]
    to_blocks = pltpu.make_async_copy(blocks_ref, b_ref, semaphores.at[0])
    to_blocks.start()

    def table(name):
        start, rows, lanes = places[name]
        return tables_ref[start : start + rows, :lanes]

    n_row, n_col, a_rows, node_rows = grid
    count = list_nodes(
        capacity,
        grid,
        everyone_ref,
        table,
        columns_ref,
        rows_ref,
        listed_ref,
    )
    caps_row = lax.broadcasted_iota(jnp.int32, caps_ref.shape, 0) % PATCH
    caps_ref[...] = jnp.where(caps_row <= 2 * centre_reach, -BIG, BIG)
    to_scalars = pltpu.make_async_copy(listed_ref, items_ref, semaphores.at[1])
    to_scalars.start()

    a_ref[0] = jnp.zeros(a_ref.shape[1:], jnp.bfloat16)
    rim = jnp.zeros((a_ref.shape[0], PATCH // 2, WIDE), jnp.bfloat16)
    a_ref[:, : PATCH // 2, :] = rim
    a_ref[:, a_ref.shape[1] - PATCH // 2 :, :] = rim

    @pl.loop(0, n_row)
    def _(row):
        strip = jnp.concatenate(
            [everyone_ref[row * n_col + col, :a_rows, :] for col in range(n_col)], axis=1
        )
        place = pl.ds(pl.multiple_of(PATCH // 2 + row * a_rows, 16), a_rows)
        for block in range(1, a_ref.shape[0]):
            a_ref[block, place, :] = cut(strip, (block - 1) * PATCH)

    def at(step, stage, part):
        return jnp.clip(BATCH * (step - stage) + part, 0, capacity - 1)

    def extract(source, block, row, row_rest, col_rest, base):
        lanes = lax.broadcasted_iota(jnp.int32, (16, WIDE), 1) >= col_rest
        rows = lax.broadcasted_iota(jnp.int32, (16, WIDE), 0) >= row_rest

        def group(place):
            here = pl.ds(pl.multiple_of(row + 16 * place, 16), 16)
            return jnp.where(lanes, source[block, here, :], source[block + 1, here, :])

        groups = [group(place) for place in range(PATCH // 16 + 1)]
        groups[0] = jnp.where(rows, groups[0], groups.pop())
        total = jnp.zeros((8, WIDE), jnp.float32)
        for values in groups:
            values = values.astype(jnp.float32)
            values = values * values
            total = total + (values[:8] + values[8:])
        patches[base : base + PATCH, :] = jnp.concatenate(groups, axis=0)
        return total[:, :HALF_LANES] + total[:, HALF_LANES:]

    def patch_base(part, which):
        trio, place = divmod(part, TRIO)
        return ((2 * trio + which) * TRIO + place) * PATCH

    def stage_half(step):
        for part in range(BATCH):
            item = at(step, 0, part)
            for which, source, fields in (
                (0, a_ref, (A_BLOCK, A_ROW, A_ROW_REST, A_COL_REST)),
                (1, b_ref, (B_BLOCK, B_ROW, B_ROW_REST, B_COL_REST)),
            ):
                block, row, row_rest, col_rest = (items_ref[field, item] for field in fields)
                energies[item % RING, which] = extract(
                    source, block, row, row_rest, col_rest, patch_base(part, which)
                )
        half = jnp.dot(patches[...], table("across"), preferred_element_type=jnp.float32)
        lanes = lax.broadcasted_iota(jnp.int32, (PATCH, HALF_LANES), 1)
        for trio in range(BATCH // TRIO):
            for which in range(2):
                for side in (slice(0, HALF_LANES), slice(HALF_LANES, WIDE)):
                    first, second, third = (
                        half[base : base + PATCH, side]
                        for base in (patch_base(TRIO * trio + n, which) for n in range(TRIO))
                    )
                    second = pltpu.roll(second, SECOND, axis=1)
                    third = pltpu.roll(third, THIRD, axis=1)
                    halves[trio, which, 0, :, side] = jnp.where(
                        lanes < SECOND, first, second
                    ).astype(jnp.bfloat16)
                    halves[trio, which, 1, :, side] = jnp.where(
                        lanes < THIRD, second, third
                    ).astype(jnp.bfloat16)

    def sides(spec, group):
        cc = spec[16 * group : 16 * group + 8, :HALF_LANES]
        cs = spec[16 * group : 16 * group + 8, HALF_LANES:]
        sc = spec[16 * group + 8 : 16 * group + 16, :HALF_LANES]
        ss = spec[16 * group + 8 : 16 * group + 16, HALF_LANES:]
        return cc - ss, sc + cs, cc + ss, sc - cs

    def stage_cross():
        down = table("down")
        for pair in range(2 * (BATCH // TRIO)):
            trio, tile = divmod(pair, 2)
            spec_a = jnp.dot(down, halves[trio, 0, tile], preferred_element_type=jnp.float32)
            spec_b = jnp.dot(down, halves[trio, 1, tile], preferred_element_type=jnp.float32)
            for group in range(GROUPS):
                a_pr, a_pi, a_mr, a_mi = sides(spec_a, group)
                b_pr, b_pi, b_mr, b_mi = sides(spec_b, group)
                pr = a_pr * b_pr + a_pi * b_pi
                pi = a_pr * b_pi - a_pi * b_pr
                mr = a_mr * b_mr + a_mi * b_mi
                mi = a_mr * b_mi - a_mi * b_mr
                upper = jnp.concatenate([pr + mr, pi - mi], axis=1)
                lower = jnp.concatenate([pi + mi, mr - pr], axis=1)
                crosses[pair, 16 * group : 16 * group + 16, :] = jnp.concatenate(
                    [upper, lower], axis=0
                ).astype(jnp.bfloat16)

    def stage_inverse():
        lanes = lax.broadcasted_iota(jnp.int32, (PATCH, HALF_LANES), 1)
        for trio in range(BATCH // TRIO):
            low, high = (
                jnp.dot(
                    table("back_down"), crosses[2 * trio + tile], preferred_element_type=jnp.float32
                )
                for tile in range(2)
            )
            for side in (slice(0, HALF_LANES), slice(HALF_LANES, WIDE)):
                first = low[:, side]
                second = jnp.where(lanes >= SECOND, first, high[:, side])
                second = pltpu.roll(second, HALF_LANES - SECOND, axis=1)
                third = pltpu.roll(high[:, side], HALF_LANES - THIRD, axis=1)
                for place, inverse in enumerate((first, second, third)):
                    base = (TRIO * trio + place) * PATCH
                    inverses[base : base + PATCH, side] = inverse.astype(jnp.bfloat16)

    def stage_score(step):
        corr_all = jnp.dot(
            inverses[...], table("back_across"), preferred_element_type=jnp.float32
        )
        rows = lax.broadcasted_iota(jnp.int32, (8, HALF_LANES), 0)
        lanes = lax.broadcasted_iota(jnp.int32, (8, HALF_LANES), 1)
        shift_rows = (rows - centre_reach).astype(jnp.float32)
        row_near = rows <= 2 * centre_reach
        for part in range(BATCH):
            item = at(step, 3, part)
            near_row = items_ref[NEAR_ROW, item]
            near_col = items_ref[NEAR_COL, item]
            ring = item % RING
            mean_a = jnp.sum(energies[ring, 0], keepdims=True) * (1.0 / (PATCH * PATCH))
            mean_b = jnp.sum(energies[ring, 1], keepdims=True) * (1.0 / (PATCH * PATCH))
            scale = 1.0 / (
                float(PATCH**4) * jnp.sqrt(mean_a + epsilon) * jnp.sqrt(mean_b + epsilon)
            )
            caps = caps_ref[pl.ds(PATCH - near_row, PATCH), :]
            total, row_moment, col_moment = 0.0, 0.0, 0.0
            best = None
            for half in range(2):
                corr = corr_all[
                    PATCH * part : PATCH * (part + 1),
                    half * HALF_LANES : (half + 1) * HALF_LANES,
                ]
                corrs[half][part, :PATCH, :] = corr
                corrs[half][part, PATCH:, :] = corr[:8]
                far = jnp.max(
                    jnp.minimum(corr, caps).reshape(PATCH // 8, 8, HALF_LANES), axis=0
                )
                if half == 0:
                    best = far
                else:
                    far = jnp.where(lanes < PATCH - HALF_LANES, far, -BIG)
                    best = jnp.maximum(best, far)
            for half in range(2):
                values = corrs[half][part, pl.ds(near_row, 8), :]
                place = lanes + half * HALF_LANES
                shift = place - near_col
                shift = jnp.where(shift >= PATCH // 2, shift - PATCH, shift)
                shift = jnp.where(shift < -(PATCH // 2), shift + PATCH, shift)
                inside = row_near & (place < PATCH)
                close = jnp.abs(shift) <= centre_reach
                weight = jnp.where(
                    inside & close, jnp.exp(sharpness * (values * scale)), 0.0
                )
                total = total + weight
                row_moment = row_moment + weight * shift_rows
                col_moment = col_moment + weight * shift.astype(jnp.float32)
                best = jnp.maximum(
                    best, jnp.where(inside & jnp.logical_not(close), values, -BIG)
                )
            totals[pl.ds(item, 1), :] = jnp.sum(total, axis=0, keepdims=True)
            row_moments[pl.ds(item, 1), :] = jnp.sum(row_moment, axis=0, keepdims=True)
            col_moments[pl.ds(item, 1), :] = jnp.sum(col_moment, axis=0, keepdims=True)
            runners[pl.ds(item, 1), :] = jnp.max(best * scale, axis=0, keepdims=True)

    to_scalars.wait()
    to_blocks.wait()

    @pl.loop(0, ((count + BATCH - 1) // BATCH + 4) // 2)
    def _(pair):
        for step in (2 * pair, 2 * pair + 1):
            stage_score(step)
            stage_inverse()
            stage_cross()
            stage_half(step)

    used = lax.broadcasted_iota(jnp.int32, (capacity, 1), 0) < count
    total = jnp.sum(totals[...], axis=1, keepdims=True)
    peak_row = columns_ref[:, PEAK_ROW : PEAK_ROW + 1]
    peak_col = columns_ref[:, PEAK_COL : PEAK_COL + 1]
    results = (
        peak_row + jnp.sum(row_moments[...], axis=1, keepdims=True) / total,
        peak_col + jnp.sum(col_moments[...], axis=1, keepdims=True) / total,
        jnp.maximum(jnp.max(runners[...], axis=1, keepdims=True), -2.0),
    )
    lanes = lax.broadcasted_iota(jnp.int32, (capacity, HALF_LANES), 1)
    terms = [jnp.zeros((capacity, HALF_LANES), jnp.float32)] * 3
    for value, rest in enumerate(results):
        rest = jnp.where(used, rest, 0.0)
        for term in range(3):
            here = rest.astype(jnp.bfloat16).astype(jnp.float32)
            terms[term] = jnp.where(lanes // SPREAD_LANES == value, here, terms[term])
            rest = rest - here
    slot_row = rows_ref[MESH_ROW : MESH_ROW + 1, :]
    slot_col = columns_ref[:, MESH_COL : MESH_COL + 1]
    offset = (lanes % SPREAD_LANES - RELAX).astype(jnp.float32)
    shape = (n_row * SPREAD_ROWS, capacity)
    place = lax.broadcasted_iota(jnp.int32, shape, 0)
    row = place // SPREAD_ROWS * node_rows + place % SPREAD_ROWS - RELAX
    rows_picked = jnp.where(slot_row == row.astype(jnp.float32), 1.0, 0.0).astype(jnp.bfloat16)
    for col in range(n_col):
        here = slot_col == offset + float(col * NODE_LANES)
        sent = sum(
            jnp.dot(
                rows_picked,
                jnp.where(here, term, 0.0).astype(jnp.bfloat16),
                preferred_element_type=jnp.float32,
            )
            for term in terms
        )
        for row in range(n_row):
            block = sent[SPREAD_ROWS * row : SPREAD_ROWS * (row + 1)]
            turned = pltpu.roll(block[8:], HALF_LANES // 2, axis=1)
            out_ref[row * n_col + col] = jnp.where(
                lanes[:8] < HALF_LANES // 2, block[:8], turned
            )


def list_nodes(
    capacity,
    grid,
    everyone_ref,
    table,
    columns_ref,
    rows_ref,
    listed_ref,
):
    n_row, n_col, a_rows, node_rows = grid
    me = (lax.axis_index("row") * n_col + lax.axis_index("col")).astype(jnp.float32)
    exact = functools.partial(lax.dot_general, preferred_element_type=jnp.float32)
    plain = (((1,), (0,)), ((), ()))
    turned = (((1,), (1,)), ((), ()))

    slot = lax.broadcasted_iota(jnp.int32, (capacity, HALF_LANES), 0).astype(jnp.float32)
    before = jnp.zeros((1, HALF_LANES), jnp.float32)
    found = jnp.zeros((capacity, 3 * HALF_LANES), jnp.float32)
    for block in range(n_row * n_col // 8):
        records = everyone_ref[8 * block : 8 * block + 8, a_rows : a_rows + 16, :]
        records = records.reshape(HALF_LANES, HALF_LANES)
        mine = exact(records, table("repeat"), plain) == me
        ones = jnp.where(mine, 1.0, 0.0).astype(jnp.bfloat16)
        counts = exact(ones, table("within"), plain)
        within, loads = counts[:, :HALF_LANES], counts[:, HALF_LANES:]
        base = exact(table("below"), loads.astype(jnp.bfloat16), plain) + before
        slots = jnp.where(mine, within + base, -1.0)
        row_loads = exact(table("count"), ones, turned)
        row_base = exact(row_loads.astype(jnp.bfloat16), table("above"), plain)[:1] + before
        holds = (slot >= row_base) & (slot < row_base + row_loads[:1])
        local = lax.broadcasted_iota(jnp.int32, (HALF_LANES, HALF_LANES), 0) % 16
        mesh_row = (local + 8 * block // n_col * node_rows).astype(jnp.float32)
        found = found + exact(
            jnp.where(holds, 1.0, 0.0).astype(jnp.bfloat16),
            jnp.concatenate(
                [records, slots.astype(jnp.bfloat16), mesh_row.astype(jnp.bfloat16)], axis=1
            ),
            plain,
        )
        before = before + jnp.sum(loads, axis=0, keepdims=True)

    same = found[:, HALF_LANES : 2 * HALF_LANES] == slot
    taken = jnp.concatenate(
        [jnp.where(same, found[:, :HALF_LANES], 0.0), found[:, 2 * HALF_LANES :]], axis=1
    ).astype(jnp.bfloat16)
    columns_ref[...] = exact(taken, table("fields"), plain)
    rows = exact(table("turned"), taken, turned)
    rows_ref[...] = rows

    def field(index):
        return rows[index : index + 1, :]

    def divide(value, by):
        whole = jnp.floor((value + 0.5) * (1.0 / by))
        return whole, value - whole * by

    half = float(PATCH // 2)
    b_top = jnp.maximum(16.0 * field(ROW_HIGH) + field(ROW_LOW) - half, 0.0)
    b_left = jnp.maximum(16.0 * field(COL_HIGH) + field(COL_LOW) - half, 0.0)
    a_top = STRIDE * field(MESH_ROW) + STRIDE // 2
    a_left = STRIDE * field(MESH_COL) + (STRIDE // 2 + half)
    b_group, b_row_rest = divide(b_top, 16)
    b_block, b_col_rest = divide(b_left, PATCH)
    a_group, a_row_rest = divide(a_top, 16)
    a_block, a_col_rest = divide(a_left, PATCH)
    near_row = divide(field(PEAK_ROW) + b_row_rest - a_row_rest - centre_reach, PATCH)[1]
    near_col = divide(field(PEAK_COL) + b_col_rest - a_col_rest, PATCH)[1]
    for index, value in (
        (B_BLOCK, b_block),
        (B_ROW, 16.0 * b_group),
        (B_ROW_REST, b_row_rest),
        (B_COL_REST, b_col_rest),
        (A_BLOCK, a_block),
        (A_ROW, 16.0 * a_group),
        (A_ROW_REST, a_row_rest),
        (A_COL_REST, a_col_rest),
        (NEAR_ROW, near_row),
        (NEAR_COL, near_col),
    ):
        listed_ref[index : index + 1, :] = value.astype(jnp.int32)
    listed_ref[FIELDS:, :] = jnp.zeros((16 - FIELDS, capacity), jnp.int32)
    return jnp.max(before).astype(jnp.int32)


def cut_kernel(tile_ref, out_ref):
    strip = tile_ref[...]
    for block in range(out_ref.shape[0]):
        out_ref[block] = cut(strip, block * PATCH)


def cut_tile(tile):
    rows, cols = tile.shape
    blocks = -(-cols // PATCH)
    return pl.pallas_call(
        cut_kernel,
        grid=(rows // HALF_LANES,),
        out_shape=jax.ShapeDtypeStruct((blocks, rows + 16, WIDE), jnp.bfloat16),
        in_specs=[pl.BlockSpec((HALF_LANES, cols), lambda step: (step, 0))],
        out_specs=pl.BlockSpec((blocks, HALF_LANES, WIDE), lambda step: (0, step, 0)),
        cost_estimate=pl.CostEstimate(
            flops=0, bytes_accessed=2 * rows * (cols + blocks * WIDE), transcendentals=0
        ),
    )(tile)


def correlate(capacity, everyone, blocks, grid):
    n_row, n_col, a_rows, node_rows = grid
    tables, places = all_tables()
    a_blocks = (n_col * everyone.shape[2] + 76) // PATCH + 2
    vmem = pl.BlockSpec(memory_space=pltpu.VMEM)
    rows = pltpu.VMEM((capacity, HALF_LANES), jnp.float32)
    return pl.pallas_call(
        functools.partial(correlate_kernel, capacity, grid, places),
        out_shape=jax.ShapeDtypeStruct(
            (n_row * n_col, SPREAD_ROWS // 2, HALF_LANES), jnp.float32
        ),
        in_specs=[vmem, pl.BlockSpec(memory_space=pl.ANY), vmem],
        out_specs=vmem,
        scratch_shapes=[
            pltpu.VMEM((2 * BATCH * PATCH, WIDE), jnp.bfloat16),
            pltpu.VMEM((BATCH // TRIO, 2, 2, PATCH, WIDE), jnp.bfloat16),
            pltpu.VMEM((BATCH // TRIO * 2, PAIRED, WIDE), jnp.bfloat16),
            pltpu.VMEM((BATCH * PATCH, WIDE), jnp.bfloat16),
            pltpu.VMEM((BATCH, PATCH + 8, HALF_LANES), jnp.float32),
            pltpu.VMEM((BATCH, PATCH + 8, HALF_LANES), jnp.float32),
            pltpu.VMEM((RING, 2, 8, HALF_LANES), jnp.float32),
        ]
        + [rows] * 4
        + [
            pltpu.VMEM((a_blocks, n_row * a_rows + PATCH, WIDE), jnp.bfloat16),
            pltpu.VMEM(blocks.shape, jnp.bfloat16),
            rows,
            pltpu.VMEM((16, capacity), jnp.int32),
            pltpu.SMEM((16, capacity), jnp.int32),
            pltpu.SemaphoreType.DMA((2,)),
            pltpu.VMEM((2 * PATCH, HALF_LANES), jnp.float32),
            pltpu.VMEM((16, capacity), jnp.float32),
        ],
        compiler_params=pltpu.CompilerParams(vmem_limit_bytes=61 * 1024 * 1024),
    )(everyone, blocks, tables)


def per_device(a_window, b_section, owners, pos_rows, pos_cols, peaks):
    node_rows, node_cols = pos_rows.shape
    nodes = node_rows * node_cols
    n_row, n_col = lax.axis_size("row"), lax.axis_size("col")
    devices = n_row * n_col
    me_row, me_col = lax.axis_index("row"), lax.axis_index("col")
    share = max(2, (nodes * 8 // 5 + devices - 1) // devices)
    a_rows, a_cols = a_window.shape
    height, breadth = n_row * node_rows, n_col * node_cols

    mesh_col = me_col * node_cols + lax.broadcasted_iota(jnp.int32, pos_rows.shape, 1)
    records = jnp.concatenate(
        [
            owners.reshape(node_rows, node_cols),
            pos_rows // 16,
            pos_rows % 16,
            pos_cols // 16,
            pos_cols % 16,
            peaks[0],
            peaks[1],
            mesh_col,
        ],
        axis=1,
    ).astype(jnp.bfloat16)
    records = jnp.pad(records, ((0, 16 - node_rows), (0, 0)), constant_values=-1)
    sent = jnp.concatenate([a_window, records], axis=0)
    sent = jnp.broadcast_to(sent[None], (n_col,) + sent.shape)
    sent = lax.all_to_all(sent, "col", split_axis=0, concat_axis=0, tiled=True)
    everyone = lax.all_gather(sent, "row").reshape(devices, a_rows + 16, a_cols)

    grid = (n_row, n_col, a_rows, node_rows)
    spread = correlate(share * devices, everyone, cut_tile(b_section), grid)
    spread = lax.all_to_all(spread, ("row", "col"), split_axis=0, concat_axis=0, tiled=True)
    tall, broad = node_rows + 2 * RELAX, node_cols + 2 * RELAX
    spread = jnp.sum(spread, axis=0)
    half_lanes = HALF_LANES // 2
    spread = jnp.concatenate([spread[:, :half_lanes], spread[:, half_lanes:]], axis=0)[:tall]
    spread = [spread[:, SPREAD_LANES * value :][:, :broad] for value in range(3)]
    runner = spread[2][RELAX:-RELAX, RELAX:-RELAX]
    field = jnp.stack(spread[:2])
    for step in range(RELAX):
        reach = RELAX - 1 - step
        centre = field[:, 1:-1, 1:-1]
        around = (
            field[:, 2:, 1:-1] + field[:, :-2, 1:-1] + field[:, 1:-1, 2:] + field[:, 1:-1, :-2]
        )
        field = centre + stiffness * (around - 4.0 * centre)
        rows = me_row * node_rows - reach + jnp.arange(node_rows + 2 * reach)
        cols = me_col * node_cols - reach + jnp.arange(node_cols + 2 * reach)
        inside = ((rows >= 0) & (rows < height))[:, None] & ((cols >= 0) & (cols < breadth))[None]
        field = jnp.where(inside[None], field, 0.0)
    return (field, runner)


def solution(mesh):
    placed = (
        P("row", "col"),
        P("row", "col"),
        P("row", "col", None, None, None),
        P("row", "col"),
        P("row", "col"),
        P(None, "row", "col"),
    )
    return jax.shard_map(
        per_device,
        mesh=mesh,
        in_specs=placed,
        out_specs=(P(None, "row", "col"), P("row", "col")),
        check_vma=False,
    )
```

```python
import functools
import math

import jax
import jax.numpy as jnp
import numpy as np
from jax import lax
from jax.experimental import pallas as pl
from jax.experimental.pallas import tpu as pltpu
from jax.sharding import PartitionSpec as P

PATCH = 160
NODE_LANES = 16
SPREAD_LANES = 20
SPREAD_ROWS = 16
STRIDE = 8
RELAX = 2
WIDE = 256
HALF_LANES = 128
FREQS = PATCH // 2 + 1
GROUPS = 11
PAIRED = 16 * GROUPS
BIG = 3.0e38

sharpness = 80.0
epsilon = 1e-06
stiffness = 0.24
centre_reach = 2


def dft_tables():
    steps = np.arange(PATCH)
    angles = 2.0 * math.pi * ((steps[:, None] * steps[None, :FREQS]) % PATCH) / PATCH
    return (
        np.cos(angles).astype(jnp.bfloat16).astype(np.float32),
        np.sin(angles).astype(jnp.bfloat16).astype(np.float32),
    )


def kernel_tables():
    cosine, sine = dft_tables()
    weights = np.full((FREQS,), 2.0, np.float32)
    weights[0] = weights[-1] = 1.0
    across = np.zeros((WIDE, WIDE), np.float32)
    across[:PATCH, :FREQS] = cosine
    across[:PATCH, HALF_LANES : HALF_LANES + FREQS] = sine
    back_across = np.zeros((WIDE, WIDE), np.float32)
    back_across[:FREQS, :PATCH] = 0.5 * (cosine * weights).T
    back_across[HALF_LANES : HALF_LANES + FREQS, :PATCH] = 0.5 * (sine * weights).T
    down = np.zeros((PAIRED, PATCH), np.float32)
    back_down = np.zeros((PATCH, PAIRED), np.float32)
    for freq in range(FREQS):
        row = 16 * (freq // 8) + freq % 8
        down[row] = cosine[:, freq]
        down[row + 8] = sine[:, freq]
        back_down[:, row] = cosine[:, freq] * weights[freq]
        back_down[:, row + 8] = sine[:, freq] * weights[freq]
    return across, down, back_down, back_across


def listing_tables():
    lane = np.arange(HALF_LANES)
    group, place = lane // NODE_LANES, lane % NODE_LANES
    repeat = (lane[:, None] < NODE_LANES) & (place[None] == lane[:, None])
    earlier = (group[:, None] == group[None]) & (place[:, None] < place[None])
    first = np.broadcast_to(lane[:, None] < NODE_LANES, (HALF_LANES, HALF_LANES))
    below = lane[None] < lane[:, None]
    fields = np.zeros((2 * HALF_LANES, HALF_LANES), np.float32)
    fields[lane, group] = 1.0
    fields[HALF_LANES, MESH_ROW] = 1.0
    return repeat, np.concatenate([earlier, first], axis=1), below, below.T, first.T[:16], fields, (
        fields.T[:16]
    )


def all_tables():
    names = ("across", "down", "back_down", "back_across", "repeat", "within")
    names += ("below", "above", "count", "fields", "turned")
    places, parts, start = {}, [], 0
    for name, part in zip(names, kernel_tables() + listing_tables()):
        rows, lanes = part.shape
        places[name] = (start, rows, lanes)
        rows_up = -(-rows // 16) * 16
        parts.append(np.zeros((rows_up, WIDE), np.float32))
        parts[-1][:rows, :lanes] = part
        start += rows_up
    return jnp.asarray(np.concatenate(parts), jnp.bfloat16), places


OWNER, ROW_HIGH, ROW_LOW, COL_HIGH, COL_LOW, PEAK_ROW, PEAK_COL, MESH_COL, MESH_ROW = range(9)
B_BLOCK, B_ROW, B_ROW_REST, B_COL_REST = 0, 1, 2, 3
A_BLOCK, A_ROW, A_ROW_REST, A_COL_REST = 4, 5, 6, 7
NEAR_ROW, NEAR_COL = 8, 9
FIELDS = 10
BATCH = 6
RING = 32
TRIO = 3
ABOVE = 24
BELOW = 32
CAP_ROWS = 64
SECOND = FREQS
THIRD = 2 * FREQS - HALF_LANES


def cut(strip, start):
    if start >= strip.shape[1]:
        return jnp.zeros((strip.shape[0], WIDE), strip.dtype)
    piece = strip[:, start : min(start + PATCH, strip.shape[1])]
    gap = jnp.zeros((strip.shape[0], WIDE - piece.shape[1]), strip.dtype)
    return jnp.concatenate([piece, gap], axis=1)


def correlate_kernel(
    capacity,
    grid,
    places,
    everyone_ref,
    blocks_ref,
    tables_ref,
    out_ref,
    *scratch,
):
    patches, halves, crosses, inverses = scratch[:4]
    corrs = scratch[4:6]
    energies, totals, row_moments, col_moments, runners, a_ref, b_ref = scratch[6:13]
    columns_ref, listed_ref, items_ref, semaphores, caps_ref, rows_ref = scratch[13:]
    to_blocks = pltpu.make_async_copy(blocks_ref, b_ref, semaphores.at[0])
    to_blocks.start()

    def table(name):
        start, rows, lanes = places[name]
        return tables_ref[start : start + rows, :lanes]

    n_row, n_col, a_rows, node_rows = grid
    count = list_nodes(
        capacity,
        grid,
        everyone_ref,
        table,
        columns_ref,
        rows_ref,
        listed_ref,
    )
    caps_row = lax.broadcasted_iota(jnp.int32, caps_ref.shape, 0) - CAP_ROWS
    caps_ref[...] = jnp.where((caps_row >= 0) & (caps_row <= 2 * centre_reach), -BIG, BIG)
    to_scalars = pltpu.make_async_copy(listed_ref, items_ref, semaphores.at[1])
    to_scalars.start()

    a_ref[0] = jnp.zeros(a_ref.shape[1:], jnp.bfloat16)
    rim = jnp.zeros((a_ref.shape[0], PATCH // 2, WIDE), jnp.bfloat16)
    a_ref[:, : PATCH // 2, :] = rim
    a_ref[:, a_ref.shape[1] - PATCH // 2 :, :] = rim

    @pl.loop(0, n_row)
    def _(row):
        strip = jnp.concatenate(
            [everyone_ref[row * n_col + col, :a_rows, :] for col in range(n_col)], axis=1
        )
        place = pl.ds(pl.multiple_of(PATCH // 2 + row * a_rows, 16), a_rows)
        for block in range(1, a_ref.shape[0]):
            a_ref[block, place, :] = cut(strip, (block - 1) * PATCH)

    def at(step, stage, part):
        return jnp.clip(BATCH * (step - stage) + part, 0, capacity - 1)

    def extract(source, block, row, row_rest, col_rest, base):
        lanes = lax.broadcasted_iota(jnp.int32, (16, WIDE), 1) >= col_rest
        rows = lax.broadcasted_iota(jnp.int32, (16, WIDE), 0) >= row_rest

        def group(place):
            here = pl.ds(pl.multiple_of(row + 16 * place, 16), 16)
            return jnp.where(lanes, source[block, here, :], source[block + 1, here, :])

        groups = [group(place) for place in range(PATCH // 16 + 1)]
        groups[0] = jnp.where(rows, groups[0], groups.pop())
        total = jnp.zeros((8, WIDE), jnp.float32)
        for place, values in enumerate(groups):
            patches[base + 16 * place : base + 16 * place + 16, :] = values
            values = values.astype(jnp.float32)
            values = values * values
            total = total + (values[:8] + values[8:])
        return total[:, :HALF_LANES] + total[:, HALF_LANES:]

    def patch_base(part, which):
        trio, place = divmod(part, TRIO)
        return ((2 * trio + which) * TRIO + place) * PATCH

    def stage_half(step):
        for part in range(BATCH):
            item = at(step, 0, part)
            for which, source, fields in (
                (0, a_ref, (A_BLOCK, A_ROW, A_ROW_REST, A_COL_REST)),
                (1, b_ref, (B_BLOCK, B_ROW, B_ROW_REST, B_COL_REST)),
            ):
                block, row, row_rest, col_rest = (items_ref[field, item] for field in fields)
                energies[item % RING, which] = extract(
                    source, block, row, row_rest, col_rest, patch_base(part, which)
                )
        half = jnp.dot(patches[...], table("across"), preferred_element_type=jnp.float32)
        lanes = lax.broadcasted_iota(jnp.int32, (PATCH, HALF_LANES), 1)
        for trio in range(BATCH // TRIO):
            for which in range(2):
                for side in (slice(0, HALF_LANES), slice(HALF_LANES, WIDE)):
                    first, second, third = (
                        half[base : base + PATCH, side]
                        for base in (patch_base(TRIO * trio + n, which) for n in range(TRIO))
                    )
                    second = pltpu.roll(second, SECOND, axis=1)
                    third = pltpu.roll(third, THIRD, axis=1)
                    halves[trio, which, 0, :, side] = jnp.where(
                        lanes < SECOND, first, second
                    ).astype(jnp.bfloat16)
                    halves[trio, which, 1, :, side] = jnp.where(
                        lanes < THIRD, second, third
                    ).astype(jnp.bfloat16)

    def sides(spec, group):
        cc = spec[16 * group : 16 * group + 8, :HALF_LANES]
        cs = spec[16 * group : 16 * group + 8, HALF_LANES:]
        sc = spec[16 * group + 8 : 16 * group + 16, :HALF_LANES]
        ss = spec[16 * group + 8 : 16 * group + 16, HALF_LANES:]
        return cc - ss, sc + cs, cc + ss, sc - cs

    def stage_inverse():
        down = table("down")
        for pair in range(2 * (BATCH // TRIO)):
            trio, tile = divmod(pair, 2)
            spec_a = jnp.dot(down, halves[trio, 0, tile], preferred_element_type=jnp.float32)
            spec_b = jnp.dot(down, halves[trio, 1, tile], preferred_element_type=jnp.float32)
            for group in range(GROUPS):
                a_pr, a_pi, a_mr, a_mi = sides(spec_a, group)
                b_pr, b_pi, b_mr, b_mi = sides(spec_b, group)
                pr = a_pr * b_pr + a_pi * b_pi
                pi = a_pr * b_pi - a_pi * b_pr
                mr = a_mr * b_mr + a_mi * b_mi
                mi = a_mr * b_mi - a_mi * b_mr
                upper = jnp.concatenate([pr + mr, pi - mi], axis=1)
                lower = jnp.concatenate([pi + mi, mr - pr], axis=1)
                crosses[pair, 16 * group : 16 * group + 16, :] = jnp.concatenate(
                    [upper, lower], axis=0
                ).astype(jnp.bfloat16)
        lanes = lax.broadcasted_iota(jnp.int32, (PATCH, HALF_LANES), 1)
        for trio in range(BATCH // TRIO):
            low, high = (
                jnp.dot(
                    table("back_down"), crosses[2 * trio + tile], preferred_element_type=jnp.float32
                )
                for tile in range(2)
            )
            for side in (slice(0, HALF_LANES), slice(HALF_LANES, WIDE)):
                first = low[:, side]
                second = jnp.where(lanes >= SECOND, first, high[:, side])
                second = pltpu.roll(second, HALF_LANES - SECOND, axis=1)
                third = pltpu.roll(high[:, side], HALF_LANES - THIRD, axis=1)
                for place, inverse in enumerate((first, second, third)):
                    base = (TRIO * trio + place) * PATCH
                    inverses[base : base + PATCH, side] = inverse.astype(jnp.bfloat16)

    def stage_score(step):
        corr_all = jnp.dot(
            inverses[...], table("back_across"), preferred_element_type=jnp.float32
        )
        rows = lax.broadcasted_iota(jnp.int32, (8, HALF_LANES), 0)
        lanes = lax.broadcasted_iota(jnp.int32, (8, HALF_LANES), 1)
        shift_rows = (rows - centre_reach).astype(jnp.float32)
        row_near = rows <= 2 * centre_reach
        for part in range(BATCH):
            item = at(step, 2, part)
            near_row = items_ref[NEAR_ROW, item]
            near_col = items_ref[NEAR_COL, item]
            ring = item % RING
            mean_a = jnp.sum(energies[ring, 0], keepdims=True) * (1.0 / (PATCH * PATCH))
            mean_b = jnp.sum(energies[ring, 1], keepdims=True) * (1.0 / (PATCH * PATCH))
            scale = 1.0 / (
                float(PATCH**4) * jnp.sqrt(mean_a + epsilon) * jnp.sqrt(mean_b + epsilon)
            )
            caps = caps_ref[pl.ds(CAP_ROWS - near_row, ABOVE + BELOW), :]
            total, row_moment, col_moment = 0.0, 0.0, 0.0
            best = None
            for half in range(2):
                corr = corr_all[
                    PATCH * part : PATCH * (part + 1),
                    half * HALF_LANES : (half + 1) * HALF_LANES,
                ]
                edge = jnp.concatenate([corr[PATCH - ABOVE :], corr[:BELOW]], axis=0)
                corrs[half][part] = edge
                far = jnp.maximum(
                    jnp.max(jnp.minimum(edge, caps).reshape(-1, 8, HALF_LANES), axis=0),
                    jnp.max(corr[BELOW : PATCH - ABOVE].reshape(-1, 8, HALF_LANES), axis=0),
                )
                if half == 0:
                    best = far
                else:
                    far = jnp.where(lanes < PATCH - HALF_LANES, far, -BIG)
                    best = jnp.maximum(best, far)
            for half in range(2):
                values = corrs[half][part, pl.ds(near_row, 8), :]
                place = lanes + half * HALF_LANES
                shift = place - near_col
                shift = jnp.where(shift >= PATCH // 2, shift - PATCH, shift)
                shift = jnp.where(shift < -(PATCH // 2), shift + PATCH, shift)
                inside = row_near & (place < PATCH)
                close = jnp.abs(shift) <= centre_reach
                weight = jnp.where(
                    inside & close, jnp.exp(sharpness * (values * scale)), 0.0
                )
                total = total + weight
                row_moment = row_moment + weight * shift_rows
                col_moment = col_moment + weight * shift.astype(jnp.float32)
                best = jnp.maximum(
                    best, jnp.where(inside & jnp.logical_not(close), values, -BIG)
                )
            totals[pl.ds(item, 1), :] = jnp.sum(total, axis=0, keepdims=True)
            row_moments[pl.ds(item, 1), :] = jnp.sum(row_moment, axis=0, keepdims=True)
            col_moments[pl.ds(item, 1), :] = jnp.sum(col_moment, axis=0, keepdims=True)
            runners[pl.ds(item, 1), :] = jnp.max(best * scale, axis=0, keepdims=True)

    to_scalars.wait()
    to_blocks.wait()

    steps = jnp.maximum((count + BATCH - 1) // BATCH, 2)
    stage_half(0)
    stage_inverse()
    stage_half(1)

    @pl.loop(2, steps)
    def _(step):
        stage_score(step)
        stage_inverse()
        stage_half(step)

    stage_score(steps)
    stage_inverse()
    stage_score(steps + 1)

    used = lax.broadcasted_iota(jnp.int32, (capacity, 1), 0) < count
    total = jnp.sum(totals[...], axis=1, keepdims=True)
    peak_row = columns_ref[:, PEAK_ROW : PEAK_ROW + 1]
    peak_col = columns_ref[:, PEAK_COL : PEAK_COL + 1]
    results = (
        peak_row + jnp.sum(row_moments[...], axis=1, keepdims=True) / total,
        peak_col + jnp.sum(col_moments[...], axis=1, keepdims=True) / total,
        jnp.maximum(jnp.max(runners[...], axis=1, keepdims=True), -2.0),
    )
    lanes = lax.broadcasted_iota(jnp.int32, (capacity, HALF_LANES), 1)
    terms = [jnp.zeros((capacity, HALF_LANES), jnp.float32)] * 3
    for value, rest in enumerate(results):
        rest = jnp.where(used, rest, 0.0)
        for term in range(3):
            here = rest.astype(jnp.bfloat16).astype(jnp.float32)
            terms[term] = jnp.where(lanes // SPREAD_LANES == value, here, terms[term])
            rest = rest - here
    slot_row = rows_ref[MESH_ROW : MESH_ROW + 1, :]
    slot_col = columns_ref[:, MESH_COL : MESH_COL + 1]
    offset = (lanes % SPREAD_LANES - RELAX).astype(jnp.float32)
    shape = (n_row * SPREAD_ROWS, capacity)
    place = lax.broadcasted_iota(jnp.int32, shape, 0)
    row = place // SPREAD_ROWS * node_rows + place % SPREAD_ROWS - RELAX
    rows_picked = jnp.where(slot_row == row.astype(jnp.float32), 1.0, 0.0).astype(jnp.bfloat16)
    for col in range(n_col):
        here = slot_col == offset + float(col * NODE_LANES)
        sent = sum(
            jnp.dot(
                rows_picked,
                jnp.where(here, term, 0.0).astype(jnp.bfloat16),
                preferred_element_type=jnp.float32,
            )
            for term in terms
        )
        for row in range(n_row):
            block = sent[SPREAD_ROWS * row : SPREAD_ROWS * (row + 1)]
            turned = pltpu.roll(block[8:], HALF_LANES // 2, axis=1)
            out_ref[row * n_col + col] = jnp.where(
                lanes[:8] < HALF_LANES // 2, block[:8], turned
            )


def list_nodes(
    capacity,
    grid,
    everyone_ref,
    table,
    columns_ref,
    rows_ref,
    listed_ref,
):
    n_row, n_col, a_rows, node_rows = grid
    me = (lax.axis_index("row") * n_col + lax.axis_index("col")).astype(jnp.float32)
    exact = functools.partial(lax.dot_general, preferred_element_type=jnp.float32)
    plain = (((1,), (0,)), ((), ()))
    turned = (((1,), (1,)), ((), ()))

    slot = lax.broadcasted_iota(jnp.int32, (capacity, HALF_LANES), 0).astype(jnp.float32)
    before = jnp.zeros((1, HALF_LANES), jnp.float32)
    found = jnp.zeros((capacity, 3 * HALF_LANES), jnp.float32)
    for block in range(n_row * n_col // 8):
        records = everyone_ref[8 * block : 8 * block + 8, a_rows : a_rows + 16, :]
        records = records.reshape(HALF_LANES, HALF_LANES)
        mine = exact(records, table("repeat"), plain) == me
        ones = jnp.where(mine, 1.0, 0.0).astype(jnp.bfloat16)
        counts = exact(ones, table("within"), plain)
        within, loads = counts[:, :HALF_LANES], counts[:, HALF_LANES:]
        base = exact(table("below"), loads.astype(jnp.bfloat16), plain) + before
        slots = jnp.where(mine, within + base, -1.0)
        row_loads = exact(table("count"), ones, turned)
        row_base = exact(row_loads.astype(jnp.bfloat16), table("above"), plain)[:1] + before
        holds = (slot >= row_base) & (slot < row_base + row_loads[:1])
        local = lax.broadcasted_iota(jnp.int32, (HALF_LANES, HALF_LANES), 0) % 16
        mesh_row = (local + 8 * block // n_col * node_rows).astype(jnp.float32)
        found = found + exact(
            jnp.where(holds, 1.0, 0.0).astype(jnp.bfloat16),
            jnp.concatenate(
                [records, slots.astype(jnp.bfloat16), mesh_row.astype(jnp.bfloat16)], axis=1
            ),
            plain,
        )
        before = before + jnp.sum(loads, axis=0, keepdims=True)

    same = found[:, HALF_LANES : 2 * HALF_LANES] == slot
    taken = jnp.concatenate(
        [jnp.where(same, found[:, :HALF_LANES], 0.0), found[:, 2 * HALF_LANES :]], axis=1
    ).astype(jnp.bfloat16)
    columns_ref[...] = exact(taken, table("fields"), plain)
    rows = exact(table("turned"), taken, turned)
    rows_ref[...] = rows

    def field(index):
        return rows[index : index + 1, :]

    def divide(value, by):
        whole = jnp.floor((value + 0.5) * (1.0 / by))
        return whole, value - whole * by

    half = float(PATCH // 2)
    b_top = jnp.maximum(16.0 * field(ROW_HIGH) + field(ROW_LOW) - half, 0.0)
    b_left = jnp.maximum(16.0 * field(COL_HIGH) + field(COL_LOW) - half, 0.0)
    a_top = STRIDE * field(MESH_ROW) + STRIDE // 2
    a_left = STRIDE * field(MESH_COL) + (STRIDE // 2 + half)
    b_group, b_row_rest = divide(b_top, 16)
    b_block, b_col_rest = divide(b_left, PATCH)
    a_group, a_row_rest = divide(a_top, 16)
    a_block, a_col_rest = divide(a_left, PATCH)
    near_row = field(PEAK_ROW) + b_row_rest - a_row_rest + (ABOVE - centre_reach)
    near_col = divide(field(PEAK_COL) + b_col_rest - a_col_rest, PATCH)[1]
    for index, value in (
        (B_BLOCK, b_block),
        (B_ROW, 16.0 * b_group),
        (B_ROW_REST, b_row_rest),
        (B_COL_REST, b_col_rest),
        (A_BLOCK, a_block),
        (A_ROW, 16.0 * a_group),
        (A_ROW_REST, a_row_rest),
        (A_COL_REST, a_col_rest),
        (NEAR_ROW, near_row),
        (NEAR_COL, near_col),
    ):
        listed_ref[index : index + 1, :] = value.astype(jnp.int32)
    listed_ref[FIELDS:, :] = jnp.zeros((16 - FIELDS, capacity), jnp.int32)
    return jnp.max(before).astype(jnp.int32)


def cut_kernel(tile_ref, out_ref):
    strip = tile_ref[...]
    for block in range(out_ref.shape[0]):
        out_ref[block] = cut(strip, block * PATCH)


def cut_tile(tile):
    rows, cols = tile.shape
    blocks = -(-cols // PATCH)
    return pl.pallas_call(
        cut_kernel,
        grid=(rows // HALF_LANES,),
        out_shape=jax.ShapeDtypeStruct((blocks, rows + 16, WIDE), jnp.bfloat16),
        in_specs=[pl.BlockSpec((HALF_LANES, cols), lambda step: (step, 0))],
        out_specs=pl.BlockSpec((blocks, HALF_LANES, WIDE), lambda step: (0, step, 0)),
        cost_estimate=pl.CostEstimate(
            flops=0, bytes_accessed=2 * rows * (cols + blocks * WIDE), transcendentals=0
        ),
    )(tile)


def correlate(capacity, everyone, blocks, grid):
    n_row, n_col, a_rows, node_rows = grid
    tables, places = all_tables()
    a_blocks = (n_col * everyone.shape[2] + 76) // PATCH + 2
    vmem = pl.BlockSpec(memory_space=pltpu.VMEM)
    rows = pltpu.VMEM((capacity, HALF_LANES), jnp.float32)
    return pl.pallas_call(
        functools.partial(correlate_kernel, capacity, grid, places),
        out_shape=jax.ShapeDtypeStruct(
            (n_row * n_col, SPREAD_ROWS // 2, HALF_LANES), jnp.float32
        ),
        in_specs=[vmem, pl.BlockSpec(memory_space=pl.ANY), vmem],
        out_specs=vmem,
        scratch_shapes=[
            pltpu.VMEM((2 * BATCH * PATCH, WIDE), jnp.bfloat16),
            pltpu.VMEM((BATCH // TRIO, 2, 2, PATCH, WIDE), jnp.bfloat16),
            pltpu.VMEM((BATCH // TRIO * 2, PAIRED, WIDE), jnp.bfloat16),
            pltpu.VMEM((BATCH * PATCH, WIDE), jnp.bfloat16),
            pltpu.VMEM((BATCH, ABOVE + BELOW, HALF_LANES), jnp.float32),
            pltpu.VMEM((BATCH, ABOVE + BELOW, HALF_LANES), jnp.float32),
            pltpu.VMEM((RING, 2, 8, HALF_LANES), jnp.float32),
        ]
        + [rows] * 4
        + [
            pltpu.VMEM((a_blocks, n_row * a_rows + PATCH, WIDE), jnp.bfloat16),
            pltpu.VMEM(blocks.shape, jnp.bfloat16),
            rows,
            pltpu.VMEM((16, capacity), jnp.int32),
            pltpu.SMEM((16, capacity), jnp.int32),
            pltpu.SemaphoreType.DMA((2,)),
            pltpu.VMEM((2 * CAP_ROWS, HALF_LANES), jnp.float32),
            pltpu.VMEM((16, capacity), jnp.float32),
        ],
        compiler_params=pltpu.CompilerParams(vmem_limit_bytes=61 * 1024 * 1024),
    )(everyone, blocks, tables)


def per_device(a_window, b_section, owners, pos_rows, pos_cols, peaks):
    node_rows, node_cols = pos_rows.shape
    nodes = node_rows * node_cols
    n_row, n_col = lax.axis_size("row"), lax.axis_size("col")
    devices = n_row * n_col
    me_row, me_col = lax.axis_index("row"), lax.axis_index("col")
    share = max(2, (nodes * 8 // 5 + devices - 1) // devices)
    a_rows, a_cols = a_window.shape
    height, breadth = n_row * node_rows, n_col * node_cols

    mesh_col = me_col * node_cols + lax.broadcasted_iota(jnp.int32, pos_rows.shape, 1)
    records = jnp.concatenate(
        [
            owners.reshape(node_rows, node_cols),
            pos_rows // 16,
            pos_rows % 16,
            pos_cols // 16,
            pos_cols % 16,
            peaks[0],
            peaks[1],
            mesh_col,
        ],
        axis=1,
    ).astype(jnp.bfloat16)
    records = jnp.pad(records, ((0, 16 - node_rows), (0, 0)), constant_values=-1)
    sent = jnp.concatenate([a_window, records], axis=0)
    sent = jnp.broadcast_to(sent[None], (n_col,) + sent.shape)
    sent = lax.all_to_all(sent, "col", split_axis=0, concat_axis=0, tiled=True)
    everyone = lax.all_gather(sent, "row").reshape(devices, a_rows + 16, a_cols)

    grid = (n_row, n_col, a_rows, node_rows)
    spread = correlate(share * devices, everyone, cut_tile(b_section), grid)
    spread = lax.all_to_all(spread, ("row", "col"), split_axis=0, concat_axis=0, tiled=True)
    tall, broad = node_rows + 2 * RELAX, node_cols + 2 * RELAX
    spread = jnp.sum(spread, axis=0)
    half_lanes = HALF_LANES // 2
    spread = jnp.concatenate([spread[:, :half_lanes], spread[:, half_lanes:]], axis=0)[:tall]
    spread = [spread[:, SPREAD_LANES * value :][:, :broad] for value in range(3)]
    runner = spread[2][RELAX:-RELAX, RELAX:-RELAX]
    field = jnp.stack(spread[:2])
    for step in range(RELAX):
        reach = RELAX - 1 - step
        centre = field[:, 1:-1, 1:-1]
        around = (
            field[:, 2:, 1:-1] + field[:, :-2, 1:-1] + field[:, 1:-1, 2:] + field[:, 1:-1, :-2]
        )
        field = centre + stiffness * (around - 4.0 * centre)
        rows = me_row * node_rows - reach + jnp.arange(node_rows + 2 * reach)
        cols = me_col * node_cols - reach + jnp.arange(node_cols + 2 * reach)
        inside = ((rows >= 0) & (rows < height))[:, None] & ((cols >= 0) & (cols < breadth))[None]
        field = jnp.where(inside[None], field, 0.0)
    return (field, runner)


def solution(mesh):
    placed = (
        P("row", "col"),
        P("row", "col"),
        P("row", "col", None, None, None),
        P("row", "col"),
        P("row", "col"),
        P(None, "row", "col"),
    )
    return jax.shard_map(
        per_device,
        mesh=mesh,
        in_specs=placed,
        out_specs=(P(None, "row", "col"), P("row", "col")),
        check_vma=False,
    )
```

```python
import functools
import math

import jax
import jax.numpy as jnp
import numpy as np
from jax import lax
from jax.experimental import pallas as pl
from jax.experimental.pallas import tpu as pltpu
from jax.sharding import PartitionSpec as P

PATCH = 160
NODE_LANES = 16
SPREAD_LANES = 20
SPREAD_ROWS = 16
STRIDE = 8
RELAX = 2
WIDE = 256
HALF_LANES = 128
FREQS = PATCH // 2 + 1
GROUPS = 11
PAIRED = 16 * GROUPS
BIG = 3.0e38

sharpness = 80.0
epsilon = 1e-06
stiffness = 0.24
centre_reach = 2


def dft_tables():
    steps = np.arange(PATCH)
    angles = 2.0 * math.pi * ((steps[:, None] * steps[None, :FREQS]) % PATCH) / PATCH
    return (
        np.cos(angles).astype(jnp.bfloat16).astype(np.float32),
        np.sin(angles).astype(jnp.bfloat16).astype(np.float32),
    )


def kernel_tables():
    cosine, sine = dft_tables()
    weights = np.full((FREQS,), 2.0, np.float32)
    weights[0] = weights[-1] = 1.0
    across = np.zeros((WIDE, WIDE), np.float32)
    across[:PATCH, :FREQS] = cosine
    across[:PATCH, HALF_LANES : HALF_LANES + FREQS] = sine
    back_across = np.zeros((WIDE, WIDE), np.float32)
    back_across[:FREQS, :PATCH] = 0.5 * (cosine * weights).T
    back_across[HALF_LANES : HALF_LANES + FREQS, :PATCH] = 0.5 * (sine * weights).T
    down = np.zeros((PAIRED, PATCH), np.float32)
    back_down = np.zeros((PATCH, PAIRED), np.float32)
    for freq in range(FREQS):
        row = 16 * (freq // 8) + freq % 8
        down[row] = cosine[:, freq]
        down[row + 8] = sine[:, freq]
        back_down[:, row] = cosine[:, freq] * weights[freq]
        back_down[:, row + 8] = sine[:, freq] * weights[freq]
    return across, down, back_down, back_across


def listing_tables():
    lane = np.arange(HALF_LANES)
    group, place = lane // NODE_LANES, lane % NODE_LANES
    repeat = (lane[:, None] < NODE_LANES) & (place[None] == lane[:, None])
    earlier = (group[:, None] == group[None]) & (place[:, None] < place[None])
    first = np.broadcast_to(lane[:, None] < NODE_LANES, (HALF_LANES, HALF_LANES))
    below = lane[None] < lane[:, None]
    fields = np.zeros((2 * HALF_LANES, HALF_LANES), np.float32)
    fields[lane, group] = 1.0
    fields[HALF_LANES, MESH_ROW] = 1.0
    return repeat, np.concatenate([earlier, first], axis=1), below, below.T, first.T[:16], fields, (
        fields.T[:16]
    )


def all_tables():
    names = ("across", "down", "back_down", "back_across", "repeat", "within")
    names += ("below", "above", "count", "fields", "turned")
    places, parts, start = {}, [], 0
    for name, part in zip(names, kernel_tables() + listing_tables()):
        rows, lanes = part.shape
        places[name] = (start, rows, lanes)
        rows_up = -(-rows // 16) * 16
        parts.append(np.zeros((rows_up, WIDE), np.float32))
        parts[-1][:rows, :lanes] = part
        start += rows_up
    return jnp.asarray(np.concatenate(parts), jnp.bfloat16), places


OWNER, ROW_HIGH, ROW_LOW, COL_HIGH, COL_LOW, PEAK_ROW, PEAK_COL, MESH_COL, MESH_ROW = range(9)
B_BLOCK, B_ROW, B_ROW_REST, B_COL_REST = 0, 1, 2, 3
A_BLOCK, A_ROW, A_ROW_REST, A_COL_REST = 4, 5, 6, 7
NEAR_ROW, NEAR_COL = 8, 9
FIELDS = 10
BATCH = 6
TRIO = 3
ABOVE = 24
BELOW = 32
CAP_ROWS = 64
SECOND = FREQS
THIRD = 2 * FREQS - HALF_LANES


def cut(strip, start):
    if start >= strip.shape[1]:
        return jnp.zeros((strip.shape[0], WIDE), strip.dtype)
    piece = strip[:, start : min(start + PATCH, strip.shape[1])]
    gap = jnp.zeros((strip.shape[0], WIDE - piece.shape[1]), strip.dtype)
    return jnp.concatenate([piece, gap], axis=1)


def correlate_kernel(
    capacity,
    grid,
    places,
    everyone_ref,
    blocks_ref,
    tables_ref,
    out_ref,
    *scratch,
):
    patches, halves, crosses, inverses = scratch[:4]
    corrs = scratch[4:6]
    energies, totals, row_moments, col_moments, runners, a_ref, b_ref = scratch[6:13]
    columns_ref, listed_ref, items_ref, semaphores, caps_ref, rows_ref, shares_ref = scratch[13:]
    to_blocks = pltpu.make_async_copy(blocks_ref, b_ref, semaphores.at[0])
    to_blocks.start()

    def table(name):
        start, rows, lanes = places[name]
        return tables_ref[start : start + rows, :lanes]

    n_row, n_col, a_rows, node_rows = grid
    count = list_nodes(
        capacity,
        grid,
        everyone_ref,
        table,
        columns_ref,
        rows_ref,
        listed_ref,
    )
    for place in range(TRIO):
        for tile in range(2):
            freq = lax.broadcasted_iota(jnp.int32, (8, HALF_LANES), 1)
            freq = freq + (tile * HALF_LANES - place * FREQS)
            once = (freq == 0) | (freq == FREQS - 1)
            twice = (freq > 0) & (freq < FREQS - 1)
            shares_ref[place, tile] = jnp.where(twice, 4.0, jnp.where(once, 2.0, 0.0))
    caps_row = lax.broadcasted_iota(jnp.int32, caps_ref.shape, 0) - CAP_ROWS
    caps_ref[...] = jnp.where((caps_row >= 0) & (caps_row <= 2 * centre_reach), -BIG, BIG)
    to_scalars = pltpu.make_async_copy(listed_ref, items_ref, semaphores.at[1])
    to_scalars.start()

    a_ref[0] = jnp.zeros(a_ref.shape[1:], jnp.bfloat16)
    rim = jnp.zeros((a_ref.shape[0], PATCH // 2, WIDE), jnp.bfloat16)
    a_ref[:, : PATCH // 2, :] = rim
    a_ref[:, a_ref.shape[1] - PATCH // 2 :, :] = rim

    @pl.loop(0, n_row)
    def _(row):
        strip = jnp.concatenate(
            [everyone_ref[row * n_col + col, :a_rows, :] for col in range(n_col)], axis=1
        )
        place = pl.ds(pl.multiple_of(PATCH // 2 + row * a_rows, 16), a_rows)
        for block in range(1, a_ref.shape[0]):
            a_ref[block, place, :] = cut(strip, (block - 1) * PATCH)

    def at(step, stage, part):
        return jnp.clip(BATCH * (step - stage) + part, 0, capacity - 1)

    def extract(source, block, row, row_rest, col_rest, base):
        lanes = lax.broadcasted_iota(jnp.int32, (16, WIDE), 1) >= col_rest
        rows = lax.broadcasted_iota(jnp.int32, (16, WIDE), 0) >= row_rest

        def group(place):
            here = pl.ds(pl.multiple_of(row + 16 * place, 16), 16)
            return jnp.where(lanes, source[block, here, :], source[block + 1, here, :])

        groups = [group(place) for place in range(PATCH // 16 + 1)]
        groups[0] = jnp.where(rows, groups[0], groups.pop())
        for place, values in enumerate(groups):
            patches[base + 16 * place : base + 16 * place + 16, :] = values

    def patch_base(part, which):
        trio, place = divmod(part, TRIO)
        return ((2 * trio + which) * TRIO + place) * PATCH

    def stage_half(step):
        for part in range(BATCH):
            item = at(step, 0, part)
            for which, source, fields in (
                (0, a_ref, (A_BLOCK, A_ROW, A_ROW_REST, A_COL_REST)),
                (1, b_ref, (B_BLOCK, B_ROW, B_ROW_REST, B_COL_REST)),
            ):
                block, row, row_rest, col_rest = (items_ref[field, item] for field in fields)
                extract(source, block, row, row_rest, col_rest, patch_base(part, which))
        half = jnp.dot(patches[...], table("across"), preferred_element_type=jnp.float32)
        lanes = lax.broadcasted_iota(jnp.int32, (PATCH, HALF_LANES), 1)
        for trio in range(BATCH // TRIO):
            for which in range(2):
                for side in (slice(0, HALF_LANES), slice(HALF_LANES, WIDE)):
                    first, second, third = (
                        half[base : base + PATCH, side]
                        for base in (patch_base(TRIO * trio + n, which) for n in range(TRIO))
                    )
                    second = pltpu.roll(second, SECOND, axis=1)
                    third = pltpu.roll(third, THIRD, axis=1)
                    halves[trio, which, 0, :, side] = jnp.where(
                        lanes < SECOND, first, second
                    ).astype(jnp.bfloat16)
                    halves[trio, which, 1, :, side] = jnp.where(
                        lanes < THIRD, second, third
                    ).astype(jnp.bfloat16)

    def sides(spec, group):
        cc = spec[16 * group : 16 * group + 8, :HALF_LANES]
        cs = spec[16 * group : 16 * group + 8, HALF_LANES:]
        sc = spec[16 * group + 8 : 16 * group + 16, :HALF_LANES]
        ss = spec[16 * group + 8 : 16 * group + 16, HALF_LANES:]
        power = (cc * cc + cs * cs) + (sc * sc + ss * ss)
        return cc - ss, sc + cs, cc + ss, sc - cs, power

    def stage_inverse():
        down = table("down")
        top = lax.broadcasted_iota(jnp.int32, (8, HALF_LANES), 0) == 0
        for pair in range(2 * (BATCH // TRIO)):
            trio, tile = divmod(pair, 2)
            spec_a = jnp.dot(down, halves[trio, 0, tile], preferred_element_type=jnp.float32)
            spec_b = jnp.dot(down, halves[trio, 1, tile], preferred_element_type=jnp.float32)
            for group in range(GROUPS):
                a_pr, a_pi, a_mr, a_mi, a_power = sides(spec_a, group)
                b_pr, b_pi, b_mr, b_mi, b_power = sides(spec_b, group)
                if group == 0:
                    powers = [jnp.where(top, 0.5 * power, power) for power in (a_power, b_power)]
                elif group < GROUPS - 1:
                    powers = [powers[0] + a_power, powers[1] + b_power]
                else:
                    powers = [powers[0] + 0.5 * a_power, powers[1] + 0.5 * b_power]
                pr = a_pr * b_pr + a_pi * b_pi
                pi = a_pr * b_pi - a_pi * b_pr
                mr = a_mr * b_mr + a_mi * b_mi
                mi = a_mr * b_mi - a_mi * b_mr
                upper = jnp.concatenate([pr + mr, pi - mi], axis=1)
                lower = jnp.concatenate([pi + mi, mr - pr], axis=1)
                crosses[pair, 16 * group : 16 * group + 16, :] = jnp.concatenate(
                    [upper, lower], axis=0
                ).astype(jnp.bfloat16)
            energies[trio, 0, tile] = powers[0]
            energies[trio, 1, tile] = powers[1]
        lanes = lax.broadcasted_iota(jnp.int32, (PATCH, HALF_LANES), 1)
        for trio in range(BATCH // TRIO):
            low, high = (
                jnp.dot(
                    table("back_down"), crosses[2 * trio + tile], preferred_element_type=jnp.float32
                )
                for tile in range(2)
            )
            for side in (slice(0, HALF_LANES), slice(HALF_LANES, WIDE)):
                first = low[:, side]
                second = jnp.where(lanes >= SECOND, first, high[:, side])
                second = pltpu.roll(second, HALF_LANES - SECOND, axis=1)
                third = pltpu.roll(high[:, side], HALF_LANES - THIRD, axis=1)
                for place, inverse in enumerate((first, second, third)):
                    base = (TRIO * trio + place) * PATCH
                    inverses[base : base + PATCH, side] = inverse.astype(jnp.bfloat16)

    def stage_score(step):
        corr_all = jnp.dot(
            inverses[...], table("back_across"), preferred_element_type=jnp.float32
        )
        rows = lax.broadcasted_iota(jnp.int32, (8, HALF_LANES), 0)
        lanes = lax.broadcasted_iota(jnp.int32, (8, HALF_LANES), 1)
        shift_rows = (rows - centre_reach).astype(jnp.float32)
        row_near = rows <= 2 * centre_reach
        for part in range(BATCH):
            item = at(step, 2, part)
            near_row = items_ref[NEAR_ROW, item]
            near_col = items_ref[NEAR_COL, item]
            trio, place = divmod(part, TRIO)
            mean_a, mean_b = (
                jnp.sum(
                    energies[trio, which, 0] * shares_ref[place, 0]
                    + energies[trio, which, 1] * shares_ref[place, 1],
                    keepdims=True,
                )
                * (1.0 / float(PATCH**4))
                for which in range(2)
            )
            scale = 1.0 / (
                float(PATCH**4) * jnp.sqrt(mean_a + epsilon) * jnp.sqrt(mean_b + epsilon)
            )
            caps = caps_ref[pl.ds(CAP_ROWS - near_row, ABOVE + BELOW), :]
            total, row_moment, col_moment = 0.0, 0.0, 0.0
            best = None
            for half in range(2):
                corr = corr_all[
                    PATCH * part : PATCH * (part + 1),
                    half * HALF_LANES : (half + 1) * HALF_LANES,
                ]
                edge = jnp.concatenate([corr[PATCH - ABOVE :], corr[:BELOW]], axis=0)
                corrs[half][part] = edge
                far = jnp.maximum(
                    jnp.max(jnp.minimum(edge, caps).reshape(-1, 8, HALF_LANES), axis=0),
                    jnp.max(corr[BELOW : PATCH - ABOVE].reshape(-1, 8, HALF_LANES), axis=0),
                )
                if half == 0:
                    best = far
                else:
                    far = jnp.where(lanes < PATCH - HALF_LANES, far, -BIG)
                    best = jnp.maximum(best, far)
            for half in range(2):
                values = corrs[half][part, pl.ds(near_row, 8), :]
                place = lanes + half * HALF_LANES
                shift = place - near_col
                shift = jnp.where(shift >= PATCH // 2, shift - PATCH, shift)
                shift = jnp.where(shift < -(PATCH // 2), shift + PATCH, shift)
                inside = row_near & (place < PATCH)
                close = jnp.abs(shift) <= centre_reach
                weight = jnp.where(
                    inside & close, jnp.exp(sharpness * (values * scale)), 0.0
                )
                total = total + weight
                row_moment = row_moment + weight * shift_rows
                col_moment = col_moment + weight * shift.astype(jnp.float32)
                best = jnp.maximum(
                    best, jnp.where(inside & jnp.logical_not(close), values, -BIG)
                )
            totals[pl.ds(item, 1), :] = jnp.sum(total, axis=0, keepdims=True)
            row_moments[pl.ds(item, 1), :] = jnp.sum(row_moment, axis=0, keepdims=True)
            col_moments[pl.ds(item, 1), :] = jnp.sum(col_moment, axis=0, keepdims=True)
            runners[pl.ds(item, 1), :] = jnp.max(best * scale, axis=0, keepdims=True)

    to_scalars.wait()
    to_blocks.wait()

    steps = jnp.maximum((count + BATCH - 1) // BATCH, 2)
    stage_half(0)
    stage_inverse()
    stage_half(1)

    @pl.loop(2, steps)
    def _(step):
        stage_score(step)
        stage_inverse()
        stage_half(step)

    stage_score(steps)
    stage_inverse()
    stage_score(steps + 1)

    used = lax.broadcasted_iota(jnp.int32, (capacity, 1), 0) < count
    total = jnp.sum(totals[...], axis=1, keepdims=True)
    peak_row = columns_ref[:, PEAK_ROW : PEAK_ROW + 1]
    peak_col = columns_ref[:, PEAK_COL : PEAK_COL + 1]
    results = (
        peak_row + jnp.sum(row_moments[...], axis=1, keepdims=True) / total,
        peak_col + jnp.sum(col_moments[...], axis=1, keepdims=True) / total,
        jnp.maximum(jnp.max(runners[...], axis=1, keepdims=True), -2.0),
    )
    lanes = lax.broadcasted_iota(jnp.int32, (capacity, HALF_LANES), 1)
    terms = [jnp.zeros((capacity, HALF_LANES), jnp.float32)] * 3
    for value, rest in enumerate(results):
        rest = jnp.where(used, rest, 0.0)
        for term in range(3):
            here = rest.astype(jnp.bfloat16).astype(jnp.float32)
            terms[term] = jnp.where(lanes // SPREAD_LANES == value, here, terms[term])
            rest = rest - here
    slot_row = rows_ref[MESH_ROW : MESH_ROW + 1, :]
    slot_col = columns_ref[:, MESH_COL : MESH_COL + 1]
    offset = (lanes % SPREAD_LANES - RELAX).astype(jnp.float32)
    shape = (n_row * SPREAD_ROWS, capacity)
    place = lax.broadcasted_iota(jnp.int32, shape, 0)
    row = place // SPREAD_ROWS * node_rows + place % SPREAD_ROWS - RELAX
    rows_picked = jnp.where(slot_row == row.astype(jnp.float32), 1.0, 0.0).astype(jnp.bfloat16)
    for col in range(n_col):
        here = slot_col == offset + float(col * NODE_LANES)
        sent = sum(
            jnp.dot(
                rows_picked,
                jnp.where(here, term, 0.0).astype(jnp.bfloat16),
                preferred_element_type=jnp.float32,
            )
            for term in terms
        )
        for row in range(n_row):
            block = sent[SPREAD_ROWS * row : SPREAD_ROWS * (row + 1)]
            turned = pltpu.roll(block[8:], HALF_LANES // 2, axis=1)
            out_ref[row * n_col + col] = jnp.where(
                lanes[:8] < HALF_LANES // 2, block[:8], turned
            )


def list_nodes(
    capacity,
    grid,
    everyone_ref,
    table,
    columns_ref,
    rows_ref,
    listed_ref,
):
    n_row, n_col, a_rows, node_rows = grid
    me = (lax.axis_index("row") * n_col + lax.axis_index("col")).astype(jnp.float32)
    exact = functools.partial(lax.dot_general, preferred_element_type=jnp.float32)
    plain = (((1,), (0,)), ((), ()))
    turned = (((1,), (1,)), ((), ()))

    slot = lax.broadcasted_iota(jnp.int32, (capacity, HALF_LANES), 0).astype(jnp.float32)
    before = jnp.zeros((1, HALF_LANES), jnp.float32)
    found = jnp.zeros((capacity, 3 * HALF_LANES), jnp.float32)
    for block in range(n_row * n_col // 8):
        records = everyone_ref[8 * block : 8 * block + 8, a_rows : a_rows + 16, :]
        records = records.reshape(HALF_LANES, HALF_LANES)
        mine = exact(records, table("repeat"), plain) == me
        ones = jnp.where(mine, 1.0, 0.0).astype(jnp.bfloat16)
        counts = exact(ones, table("within"), plain)
        within, loads = counts[:, :HALF_LANES], counts[:, HALF_LANES:]
        base = exact(table("below"), loads.astype(jnp.bfloat16), plain) + before
        slots = jnp.where(mine, within + base, -1.0)
        row_loads = exact(table("count"), ones, turned)
        row_base = exact(row_loads.astype(jnp.bfloat16), table("above"), plain)[:1] + before
        holds = (slot >= row_base) & (slot < row_base + row_loads[:1])
        local = lax.broadcasted_iota(jnp.int32, (HALF_LANES, HALF_LANES), 0) % 16
        mesh_row = (local + 8 * block // n_col * node_rows).astype(jnp.float32)
        found = found + exact(
            jnp.where(holds, 1.0, 0.0).astype(jnp.bfloat16),
            jnp.concatenate(
                [records, slots.astype(jnp.bfloat16), mesh_row.astype(jnp.bfloat16)], axis=1
            ),
            plain,
        )
        before = before + jnp.sum(loads, axis=0, keepdims=True)

    same = found[:, HALF_LANES : 2 * HALF_LANES] == slot
    taken = jnp.concatenate(
        [jnp.where(same, found[:, :HALF_LANES], 0.0), found[:, 2 * HALF_LANES :]], axis=1
    ).astype(jnp.bfloat16)
    columns_ref[...] = exact(taken, table("fields"), plain)
    rows = exact(table("turned"), taken, turned)
    rows_ref[...] = rows

    def field(index):
        return rows[index : index + 1, :]

    def divide(value, by):
        whole = jnp.floor((value + 0.5) * (1.0 / by))
        return whole, value - whole * by

    half = float(PATCH // 2)
    b_top = jnp.maximum(16.0 * field(ROW_HIGH) + field(ROW_LOW) - half, 0.0)
    b_left = jnp.maximum(16.0 * field(COL_HIGH) + field(COL_LOW) - half, 0.0)
    a_top = STRIDE * field(MESH_ROW) + STRIDE // 2
    a_left = STRIDE * field(MESH_COL) + (STRIDE // 2 + half)
    b_group, b_row_rest = divide(b_top, 16)
    b_block, b_col_rest = divide(b_left, PATCH)
    a_group, a_row_rest = divide(a_top, 16)
    a_block, a_col_rest = divide(a_left, PATCH)
    near_row = field(PEAK_ROW) + b_row_rest - a_row_rest + (ABOVE - centre_reach)
    near_col = divide(field(PEAK_COL) + b_col_rest - a_col_rest, PATCH)[1]
    for index, value in (
        (B_BLOCK, b_block),
        (B_ROW, 16.0 * b_group),
        (B_ROW_REST, b_row_rest),
        (B_COL_REST, b_col_rest),
        (A_BLOCK, a_block),
        (A_ROW, 16.0 * a_group),
        (A_ROW_REST, a_row_rest),
        (A_COL_REST, a_col_rest),
        (NEAR_ROW, near_row),
        (NEAR_COL, near_col),
    ):
        listed_ref[index : index + 1, :] = value.astype(jnp.int32)
    listed_ref[FIELDS:, :] = jnp.zeros((16 - FIELDS, capacity), jnp.int32)
    return jnp.max(before).astype(jnp.int32)


def cut_kernel(tile_ref, out_ref):
    strip = tile_ref[...]
    for block in range(out_ref.shape[0]):
        out_ref[block] = cut(strip, block * PATCH)


def cut_tile(tile):
    rows, cols = tile.shape
    blocks = -(-cols // PATCH)
    return pl.pallas_call(
        cut_kernel,
        grid=(rows // HALF_LANES,),
        out_shape=jax.ShapeDtypeStruct((blocks, rows + 16, WIDE), jnp.bfloat16),
        in_specs=[pl.BlockSpec((HALF_LANES, cols), lambda step: (step, 0))],
        out_specs=pl.BlockSpec((blocks, HALF_LANES, WIDE), lambda step: (0, step, 0)),
        cost_estimate=pl.CostEstimate(
            flops=0, bytes_accessed=2 * rows * (cols + blocks * WIDE), transcendentals=0
        ),
    )(tile)


def correlate(capacity, everyone, blocks, grid):
    n_row, n_col, a_rows, node_rows = grid
    tables, places = all_tables()
    a_blocks = (n_col * everyone.shape[2] + 76) // PATCH + 2
    vmem = pl.BlockSpec(memory_space=pltpu.VMEM)
    rows = pltpu.VMEM((capacity, HALF_LANES), jnp.float32)
    return pl.pallas_call(
        functools.partial(correlate_kernel, capacity, grid, places),
        out_shape=jax.ShapeDtypeStruct(
            (n_row * n_col, SPREAD_ROWS // 2, HALF_LANES), jnp.float32
        ),
        in_specs=[vmem, pl.BlockSpec(memory_space=pl.ANY), vmem],
        out_specs=vmem,
        scratch_shapes=[
            pltpu.VMEM((2 * BATCH * PATCH, WIDE), jnp.bfloat16),
            pltpu.VMEM((BATCH // TRIO, 2, 2, PATCH, WIDE), jnp.bfloat16),
            pltpu.VMEM((BATCH // TRIO * 2, PAIRED, WIDE), jnp.bfloat16),
            pltpu.VMEM((BATCH * PATCH, WIDE), jnp.bfloat16),
            pltpu.VMEM((BATCH, ABOVE + BELOW, HALF_LANES), jnp.float32),
            pltpu.VMEM((BATCH, ABOVE + BELOW, HALF_LANES), jnp.float32),
            pltpu.VMEM((BATCH // TRIO, 2, 2, 8, HALF_LANES), jnp.float32),
        ]
        + [rows] * 4
        + [
            pltpu.VMEM((a_blocks, n_row * a_rows + PATCH, WIDE), jnp.bfloat16),
            pltpu.VMEM(blocks.shape, jnp.bfloat16),
            rows,
            pltpu.VMEM((16, capacity), jnp.int32),
            pltpu.SMEM((16, capacity), jnp.int32),
            pltpu.SemaphoreType.DMA((2,)),
            pltpu.VMEM((2 * CAP_ROWS, HALF_LANES), jnp.float32),
            pltpu.VMEM((16, capacity), jnp.float32),
            pltpu.VMEM((TRIO, 2, 8, HALF_LANES), jnp.float32),
        ],
        compiler_params=pltpu.CompilerParams(vmem_limit_bytes=61 * 1024 * 1024),
    )(everyone, blocks, tables)


def per_device(a_window, b_section, owners, pos_rows, pos_cols, peaks):
    node_rows, node_cols = pos_rows.shape
    nodes = node_rows * node_cols
    n_row, n_col = lax.axis_size("row"), lax.axis_size("col")
    devices = n_row * n_col
    me_row, me_col = lax.axis_index("row"), lax.axis_index("col")
    share = max(2, (nodes * 8 // 5 + devices - 1) // devices)
    a_rows, a_cols = a_window.shape
    height, breadth = n_row * node_rows, n_col * node_cols

    mesh_col = me_col * node_cols + lax.broadcasted_iota(jnp.int32, pos_rows.shape, 1)
    records = jnp.concatenate(
        [
            owners.reshape(node_rows, node_cols),
            pos_rows // 16,
            pos_rows % 16,
            pos_cols // 16,
            pos_cols % 16,
            peaks[0],
            peaks[1],
            mesh_col,
        ],
        axis=1,
    ).astype(jnp.bfloat16)
    records = jnp.pad(records, ((0, 16 - node_rows), (0, 0)), constant_values=-1)
    sent = jnp.concatenate([a_window, records], axis=0)
    sent = jnp.broadcast_to(sent[None], (n_col,) + sent.shape)
    sent = lax.all_to_all(sent, "col", split_axis=0, concat_axis=0, tiled=True)
    everyone = lax.all_gather(sent, "row").reshape(devices, a_rows + 16, a_cols)

    grid = (n_row, n_col, a_rows, node_rows)
    spread = correlate(share * devices, everyone, cut_tile(b_section), grid)
    spread = lax.all_to_all(spread, ("row", "col"), split_axis=0, concat_axis=0, tiled=True)
    tall, broad = node_rows + 2 * RELAX, node_cols + 2 * RELAX
    spread = jnp.sum(spread, axis=0)
    half_lanes = HALF_LANES // 2
    spread = jnp.concatenate([spread[:, :half_lanes], spread[:, half_lanes:]], axis=0)[:tall]
    spread = [spread[:, SPREAD_LANES * value :][:, :broad] for value in range(3)]
    runner = spread[2][RELAX:-RELAX, RELAX:-RELAX]
    field = jnp.stack(spread[:2])
    for step in range(RELAX):
        reach = RELAX - 1 - step
        centre = field[:, 1:-1, 1:-1]
        around = (
            field[:, 2:, 1:-1] + field[:, :-2, 1:-1] + field[:, 1:-1, 2:] + field[:, 1:-1, :-2]
        )
        field = centre + stiffness * (around - 4.0 * centre)
        rows = me_row * node_rows - reach + jnp.arange(node_rows + 2 * reach)
        cols = me_col * node_cols - reach + jnp.arange(node_cols + 2 * reach)
        inside = ((rows >= 0) & (rows < height))[:, None] & ((cols >= 0) & (cols < breadth))[None]
        field = jnp.where(inside[None], field, 0.0)
    return (field, runner)


def solution(mesh):
    placed = (
        P("row", "col"),
        P("row", "col"),
        P("row", "col", None, None, None),
        P("row", "col"),
        P("row", "col"),
        P(None, "row", "col"),
    )
    return jax.shard_map(
        per_device,
        mesh=mesh,
        in_specs=placed,
        out_specs=(P(None, "row", "col"), P("row", "col")),
        check_vma=False,
    )
```

```python
import functools
import math

import jax
import jax.numpy as jnp
import numpy as np
from jax import lax
from jax.experimental import pallas as pl
from jax.experimental.pallas import tpu as pltpu
from jax.sharding import PartitionSpec as P

PATCH = 160
NODE_LANES = 16
SPREAD_LANES = 20
SPREAD_ROWS = 16
STRIDE = 8
RELAX = 2
WIDE = 256
HALF_LANES = 128
FREQS = PATCH // 2 + 1
GROUPS = 11
PAIRED = 16 * GROUPS
BIG = 3.0e38

sharpness = 80.0
epsilon = 1e-06
stiffness = 0.24
centre_reach = 2


def dft_tables():
    steps = np.arange(PATCH)
    angles = 2.0 * math.pi * ((steps[:, None] * steps[None, :FREQS]) % PATCH) / PATCH
    return (
        np.cos(angles).astype(jnp.bfloat16).astype(np.float32),
        np.sin(angles).astype(jnp.bfloat16).astype(np.float32),
    )


def kernel_tables():
    cosine, sine = dft_tables()
    weights = np.full((FREQS,), 2.0, np.float32)
    weights[0] = weights[-1] = 1.0
    across = np.zeros((WIDE, WIDE), np.float32)
    across[:PATCH, :FREQS] = cosine
    across[:PATCH, HALF_LANES : HALF_LANES + FREQS] = sine
    back_across = np.zeros((WIDE, WIDE), np.float32)
    back_across[:FREQS, :PATCH] = 0.5 * (cosine * weights).T
    back_across[HALF_LANES : HALF_LANES + FREQS, :PATCH] = 0.5 * (sine * weights).T
    down = np.zeros((PAIRED, PATCH), np.float32)
    back_down = np.zeros((PATCH, PAIRED), np.float32)
    for freq in range(FREQS):
        row = 16 * (freq // 8) + freq % 8
        down[row] = cosine[:, freq]
        down[row + 8] = sine[:, freq]
        back_down[:, row] = cosine[:, freq] * weights[freq]
        back_down[:, row + 8] = sine[:, freq] * weights[freq]
    return across, down, back_down, back_across


def listing_tables():
    lane = np.arange(HALF_LANES)
    group, place = lane // NODE_LANES, lane % NODE_LANES
    repeat = (lane[:, None] < NODE_LANES) & (place[None] == lane[:, None])
    earlier = (group[:, None] == group[None]) & (place[:, None] < place[None])
    first = np.broadcast_to(lane[:, None] < NODE_LANES, (HALF_LANES, HALF_LANES))
    below = lane[None] < lane[:, None]
    fields = np.zeros((2 * HALF_LANES, HALF_LANES), np.float32)
    fields[lane, group] = 1.0
    fields[HALF_LANES, MESH_ROW] = 1.0
    return repeat, np.concatenate([earlier, first], axis=1), below, below.T, first.T[:16], fields, (
        fields.T[:16]
    )


def all_tables():
    names = ("across", "down", "back_down", "back_across", "repeat", "within")
    names += ("below", "above", "count", "fields", "turned")
    places, parts, start = {}, [], 0
    for name, part in zip(names, kernel_tables() + listing_tables()):
        rows, lanes = part.shape
        places[name] = (start, rows, lanes)
        rows_up = -(-rows // 16) * 16
        parts.append(np.zeros((rows_up, WIDE), np.float32))
        parts[-1][:rows, :lanes] = part
        start += rows_up
    return jnp.asarray(np.concatenate(parts), jnp.bfloat16), places


OWNER, ROW_HIGH, ROW_LOW, COL_HIGH, COL_LOW, PEAK_ROW, PEAK_COL, MESH_COL, MESH_ROW = range(9)
B_BLOCK, B_ROW, B_ROW_REST, B_COL_REST = 0, 1, 2, 3
A_BLOCK, A_ROW, A_ROW_REST, A_COL_REST = 4, 5, 6, 7
NEAR_ROW, NEAR_COL = 8, 9
FIELDS = 10
BATCH = 6
TRIO = 3
ABOVE = 24
BELOW = 32
CAP_ROWS = 64
SECOND = FREQS
THIRD = 2 * FREQS - HALF_LANES


def cut(strip, start):
    if start >= strip.shape[1]:
        return jnp.zeros((strip.shape[0], WIDE), strip.dtype)
    piece = strip[:, start : min(start + PATCH, strip.shape[1])]
    gap = jnp.zeros((strip.shape[0], WIDE - piece.shape[1]), strip.dtype)
    return jnp.concatenate([piece, gap], axis=1)


def correlate_kernel(
    capacity,
    grid,
    places,
    everyone_ref,
    blocks_ref,
    tables_ref,
    out_ref,
    *scratch,
):
    patches, halves, crosses, inverses = scratch[:4]
    corrs = scratch[4:6]
    energies, totals, row_moments, col_moments, runners, a_ref, b_ref = scratch[6:13]
    columns_ref, listed_ref, items_ref, semaphores, caps_ref, rows_ref, shares_ref = scratch[13:]
    to_blocks = pltpu.make_async_copy(blocks_ref, b_ref, semaphores.at[0])
    to_blocks.start()

    def table(name):
        start, rows, lanes = places[name]
        return tables_ref[start : start + rows, :lanes]

    n_row, n_col, a_rows, node_rows = grid
    count = list_nodes(
        capacity,
        grid,
        everyone_ref,
        table,
        columns_ref,
        rows_ref,
        listed_ref,
    )
    for place in range(TRIO):
        for tile in range(2):
            freq = lax.broadcasted_iota(jnp.int32, (8, HALF_LANES), 1)
            freq = freq + (tile * HALF_LANES - place * FREQS)
            once = (freq == 0) | (freq == FREQS - 1)
            twice = (freq > 0) & (freq < FREQS - 1)
            shares_ref[place, tile] = jnp.where(twice, 4.0, jnp.where(once, 2.0, 0.0))
    caps_row = lax.broadcasted_iota(jnp.int32, caps_ref.shape, 0) - CAP_ROWS
    caps_ref[...] = jnp.where((caps_row >= 0) & (caps_row <= 2 * centre_reach), -BIG, BIG)
    to_scalars = pltpu.make_async_copy(listed_ref, items_ref, semaphores.at[1])
    to_scalars.start()

    a_ref[0] = jnp.zeros(a_ref.shape[1:], jnp.bfloat16)
    rim = jnp.zeros((a_ref.shape[0], PATCH // 2, WIDE), jnp.bfloat16)
    a_ref[:, : PATCH // 2, :] = rim
    a_ref[:, a_ref.shape[1] - PATCH // 2 :, :] = rim

    @pl.loop(0, n_row)
    def _(row):
        strip = jnp.concatenate(
            [everyone_ref[row * n_col + col, :a_rows, :] for col in range(n_col)], axis=1
        )
        place = pl.ds(pl.multiple_of(PATCH // 2 + row * a_rows, 16), a_rows)
        for block in range(1, a_ref.shape[0]):
            a_ref[block, place, :] = cut(strip, (block - 1) * PATCH)

    def at(step, stage, part):
        return jnp.clip(BATCH * (step - stage) + part, 0, capacity - 1)

    def extract(source, block, row, row_rest, col_rest, base):
        lanes = lax.broadcasted_iota(jnp.int32, (16, WIDE), 1) >= col_rest
        rows = lax.broadcasted_iota(jnp.int32, (16, WIDE), 0) >= row_rest

        def group(place):
            here = pl.ds(pl.multiple_of(row + 16 * place, 16), 16)
            return jnp.where(lanes, source[block, here, :], source[block + 1, here, :])

        groups = [group(place) for place in range(PATCH // 16 + 1)]
        groups[0] = jnp.where(rows, groups[0], groups.pop())
        for place, values in enumerate(groups):
            start = base + 16 * TRIO * place
            patches[start : start + 16, :] = values

    def patch_base(part, which):
        trio, place = divmod(part, TRIO)
        return (2 * trio + which) * TRIO * PATCH + 16 * place

    def stage_half(step):
        for part in range(BATCH):
            item = at(step, 0, part)
            for which, source, fields in (
                (0, a_ref, (A_BLOCK, A_ROW, A_ROW_REST, A_COL_REST)),
                (1, b_ref, (B_BLOCK, B_ROW, B_ROW_REST, B_COL_REST)),
            ):
                block, row, row_rest, col_rest = (items_ref[field, item] for field in fields)
                extract(source, block, row, row_rest, col_rest, patch_base(part, which))
        half = jnp.dot(patches[...], table("across"), preferred_element_type=jnp.float32)
        lanes = lax.broadcasted_iota(jnp.int32, (16, HALF_LANES), 1)
        for trio in range(BATCH // TRIO):
            for which in range(2):
                for group in range(PATCH // 16):
                    rows = slice(16 * group, 16 * group + 16)
                    for side in (slice(0, HALF_LANES), slice(HALF_LANES, WIDE)):
                        first, second, third = (
                            half[base : base + 16, side]
                            for base in (
                                patch_base(TRIO * trio + n, which) + 16 * TRIO * group
                                for n in range(TRIO)
                            )
                        )
                        second = pltpu.roll(second, SECOND, axis=1)
                        third = pltpu.roll(third, THIRD, axis=1)
                        halves[trio, which, 0, rows, side] = jnp.where(
                            lanes < SECOND, first, second
                        ).astype(jnp.bfloat16)
                        halves[trio, which, 1, rows, side] = jnp.where(
                            lanes < THIRD, second, third
                        ).astype(jnp.bfloat16)

    def sides(spec, group):
        cc = spec[16 * group : 16 * group + 8, :HALF_LANES]
        cs = spec[16 * group : 16 * group + 8, HALF_LANES:]
        sc = spec[16 * group + 8 : 16 * group + 16, :HALF_LANES]
        ss = spec[16 * group + 8 : 16 * group + 16, HALF_LANES:]
        power = (cc * cc + cs * cs) + (sc * sc + ss * ss)
        return cc - ss, sc + cs, cc + ss, sc - cs, power

    def stage_inverse():
        down = table("down")
        top = lax.broadcasted_iota(jnp.int32, (8, HALF_LANES), 0) == 0
        for pair in range(2 * (BATCH // TRIO)):
            trio, tile = divmod(pair, 2)
            spec_a = jnp.dot(down, halves[trio, 0, tile], preferred_element_type=jnp.float32)
            spec_b = jnp.dot(down, halves[trio, 1, tile], preferred_element_type=jnp.float32)
            for group in range(GROUPS):
                a_pr, a_pi, a_mr, a_mi, a_power = sides(spec_a, group)
                b_pr, b_pi, b_mr, b_mi, b_power = sides(spec_b, group)
                if group == 0:
                    powers = [jnp.where(top, 0.5 * power, power) for power in (a_power, b_power)]
                elif group < GROUPS - 1:
                    powers = [powers[0] + a_power, powers[1] + b_power]
                else:
                    powers = [powers[0] + 0.5 * a_power, powers[1] + 0.5 * b_power]
                pr = a_pr * b_pr + a_pi * b_pi
                pi = a_pr * b_pi - a_pi * b_pr
                mr = a_mr * b_mr + a_mi * b_mi
                mi = a_mr * b_mi - a_mi * b_mr
                upper = jnp.concatenate([pr + mr, pi - mi], axis=1)
                lower = jnp.concatenate([pi + mi, mr - pr], axis=1)
                crosses[pair, 16 * group : 16 * group + 16, :] = jnp.concatenate(
                    [upper, lower], axis=0
                ).astype(jnp.bfloat16)
            energies[trio, 0, tile] = powers[0]
            energies[trio, 1, tile] = powers[1]
        lanes = lax.broadcasted_iota(jnp.int32, (PATCH, HALF_LANES), 1)
        for trio in range(BATCH // TRIO):
            low, high = (
                jnp.dot(
                    table("back_down"), crosses[2 * trio + tile], preferred_element_type=jnp.float32
                )
                for tile in range(2)
            )
            for side in (slice(0, HALF_LANES), slice(HALF_LANES, WIDE)):
                first = low[:, side]
                second = jnp.where(lanes >= SECOND, first, high[:, side])
                second = pltpu.roll(second, HALF_LANES - SECOND, axis=1)
                third = pltpu.roll(high[:, side], HALF_LANES - THIRD, axis=1)
                for place, inverse in enumerate((first, second, third)):
                    base = (TRIO * trio + place) * PATCH
                    inverses[base : base + PATCH, side] = inverse.astype(jnp.bfloat16)

    def stage_score(step):
        corr_all = jnp.dot(
            inverses[...], table("back_across"), preferred_element_type=jnp.float32
        )
        rows = lax.broadcasted_iota(jnp.int32, (8, HALF_LANES), 0)
        lanes = lax.broadcasted_iota(jnp.int32, (8, HALF_LANES), 1)
        shift_rows = (rows - centre_reach).astype(jnp.float32)
        row_near = rows <= 2 * centre_reach
        for part in range(BATCH):
            item = at(step, 2, part)
            near_row = items_ref[NEAR_ROW, item]
            near_col = items_ref[NEAR_COL, item]
            trio, place = divmod(part, TRIO)
            mean_a, mean_b = (
                jnp.sum(
                    energies[trio, which, 0] * shares_ref[place, 0]
                    + energies[trio, which, 1] * shares_ref[place, 1],
                    keepdims=True,
                )
                * (1.0 / float(PATCH**4))
                for which in range(2)
            )
            scale = 1.0 / (
                float(PATCH**4) * jnp.sqrt(mean_a + epsilon) * jnp.sqrt(mean_b + epsilon)
            )
            caps = caps_ref[pl.ds(CAP_ROWS - near_row, ABOVE + BELOW), :]
            total, row_moment, col_moment = 0.0, 0.0, 0.0
            best = None
            for half in range(2):
                corr = corr_all[
                    PATCH * part : PATCH * (part + 1),
                    half * HALF_LANES : (half + 1) * HALF_LANES,
                ]
                edge = jnp.concatenate([corr[PATCH - ABOVE :], corr[:BELOW]], axis=0)
                corrs[half][part] = edge
                far = jnp.maximum(
                    jnp.max(jnp.minimum(edge, caps).reshape(-1, 8, HALF_LANES), axis=0),
                    jnp.max(corr[BELOW : PATCH - ABOVE].reshape(-1, 8, HALF_LANES), axis=0),
                )
                if half == 0:
                    best = far
                else:
                    far = jnp.where(lanes < PATCH - HALF_LANES, far, -BIG)
                    best = jnp.maximum(best, far)
            for half in range(2):
                values = corrs[half][part, pl.ds(near_row, 8), :]
                place = lanes + half * HALF_LANES
                shift = place - near_col
                shift = jnp.where(shift >= PATCH // 2, shift - PATCH, shift)
                shift = jnp.where(shift < -(PATCH // 2), shift + PATCH, shift)
                inside = row_near & (place < PATCH)
                close = jnp.abs(shift) <= centre_reach
                weight = jnp.where(
                    inside & close, jnp.exp(sharpness * (values * scale)), 0.0
                )
                total = total + weight
                row_moment = row_moment + weight * shift_rows
                col_moment = col_moment + weight * shift.astype(jnp.float32)
                best = jnp.maximum(
                    best, jnp.where(inside & jnp.logical_not(close), values, -BIG)
                )
            totals[pl.ds(item, 1), :] = jnp.sum(total, axis=0, keepdims=True)
            row_moments[pl.ds(item, 1), :] = jnp.sum(row_moment, axis=0, keepdims=True)
            col_moments[pl.ds(item, 1), :] = jnp.sum(col_moment, axis=0, keepdims=True)
            runners[pl.ds(item, 1), :] = jnp.max(best * scale, axis=0, keepdims=True)

    to_scalars.wait()
    to_blocks.wait()

    steps = jnp.maximum((count + BATCH - 1) // BATCH, 2)
    stage_half(0)
    stage_inverse()
    stage_half(1)

    @pl.loop(2, steps)
    def _(step):
        stage_score(step)
        stage_inverse()
        stage_half(step)

    stage_score(steps)
    stage_inverse()
    stage_score(steps + 1)

    used = lax.broadcasted_iota(jnp.int32, (capacity, 1), 0) < count
    total = jnp.sum(totals[...], axis=1, keepdims=True)
    peak_row = columns_ref[:, PEAK_ROW : PEAK_ROW + 1]
    peak_col = columns_ref[:, PEAK_COL : PEAK_COL + 1]
    results = (
        peak_row + jnp.sum(row_moments[...], axis=1, keepdims=True) / total,
        peak_col + jnp.sum(col_moments[...], axis=1, keepdims=True) / total,
        jnp.maximum(jnp.max(runners[...], axis=1, keepdims=True), -2.0),
    )
    lanes = lax.broadcasted_iota(jnp.int32, (capacity, HALF_LANES), 1)
    terms = [jnp.zeros((capacity, HALF_LANES), jnp.float32)] * 3
    for value, rest in enumerate(results):
        rest = jnp.where(used, rest, 0.0)
        for term in range(3):
            here = rest.astype(jnp.bfloat16).astype(jnp.float32)
            terms[term] = jnp.where(lanes // SPREAD_LANES == value, here, terms[term])
            rest = rest - here
    slot_row = rows_ref[MESH_ROW : MESH_ROW + 1, :]
    slot_col = columns_ref[:, MESH_COL : MESH_COL + 1]
    offset = (lanes % SPREAD_LANES - RELAX).astype(jnp.float32)
    shape = (n_row * SPREAD_ROWS, capacity)
    place = lax.broadcasted_iota(jnp.int32, shape, 0)
    row = place // SPREAD_ROWS * node_rows + place % SPREAD_ROWS - RELAX
    rows_picked = jnp.where(slot_row == row.astype(jnp.float32), 1.0, 0.0).astype(jnp.bfloat16)
    for col in range(n_col):
        here = slot_col == offset + float(col * NODE_LANES)
        sent = sum(
            jnp.dot(
                rows_picked,
                jnp.where(here, term, 0.0).astype(jnp.bfloat16),
                preferred_element_type=jnp.float32,
            )
            for term in terms
        )
        for row in range(n_row):
            block = sent[SPREAD_ROWS * row : SPREAD_ROWS * (row + 1)]
            turned = pltpu.roll(block[8:], HALF_LANES // 2, axis=1)
            out_ref[row * n_col + col] = jnp.where(
                lanes[:8] < HALF_LANES // 2, block[:8], turned
            )


def list_nodes(
    capacity,
    grid,
    everyone_ref,
    table,
    columns_ref,
    rows_ref,
    listed_ref,
):
    n_row, n_col, a_rows, node_rows = grid
    me = (lax.axis_index("row") * n_col + lax.axis_index("col")).astype(jnp.float32)
    exact = functools.partial(lax.dot_general, preferred_element_type=jnp.float32)
    plain = (((1,), (0,)), ((), ()))
    turned = (((1,), (1,)), ((), ()))

    slot = lax.broadcasted_iota(jnp.int32, (capacity, HALF_LANES), 0).astype(jnp.float32)
    before = jnp.zeros((1, HALF_LANES), jnp.float32)
    found = jnp.zeros((capacity, 3 * HALF_LANES), jnp.float32)
    for block in range(n_row * n_col // 8):
        records = everyone_ref[8 * block : 8 * block + 8, a_rows : a_rows + 16, :]
        records = records.reshape(HALF_LANES, HALF_LANES)
        mine = exact(records, table("repeat"), plain) == me
        ones = jnp.where(mine, 1.0, 0.0).astype(jnp.bfloat16)
        counts = exact(ones, table("within"), plain)
        within, loads = counts[:, :HALF_LANES], counts[:, HALF_LANES:]
        base = exact(table("below"), loads.astype(jnp.bfloat16), plain) + before
        slots = jnp.where(mine, within + base, -1.0)
        row_loads = exact(table("count"), ones, turned)
        row_base = exact(row_loads.astype(jnp.bfloat16), table("above"), plain)[:1] + before
        holds = (slot >= row_base) & (slot < row_base + row_loads[:1])
        local = lax.broadcasted_iota(jnp.int32, (HALF_LANES, HALF_LANES), 0) % 16
        mesh_row = (local + 8 * block // n_col * node_rows).astype(jnp.float32)
        found = found + exact(
            jnp.where(holds, 1.0, 0.0).astype(jnp.bfloat16),
            jnp.concatenate(
                [records, slots.astype(jnp.bfloat16), mesh_row.astype(jnp.bfloat16)], axis=1
            ),
            plain,
        )
        before = before + jnp.sum(loads, axis=0, keepdims=True)

    same = found[:, HALF_LANES : 2 * HALF_LANES] == slot
    taken = jnp.concatenate(
        [jnp.where(same, found[:, :HALF_LANES], 0.0), found[:, 2 * HALF_LANES :]], axis=1
    ).astype(jnp.bfloat16)
    columns_ref[...] = exact(taken, table("fields"), plain)
    rows = exact(table("turned"), taken, turned)
    rows_ref[...] = rows

    def field(index):
        return rows[index : index + 1, :]

    def divide(value, by):
        whole = jnp.floor((value + 0.5) * (1.0 / by))
        return whole, value - whole * by

    half = float(PATCH // 2)
    b_top = jnp.maximum(16.0 * field(ROW_HIGH) + field(ROW_LOW) - half, 0.0)
    b_left = jnp.maximum(16.0 * field(COL_HIGH) + field(COL_LOW) - half, 0.0)
    a_top = STRIDE * field(MESH_ROW) + STRIDE // 2
    a_left = STRIDE * field(MESH_COL) + (STRIDE // 2 + half)
    b_group, b_row_rest = divide(b_top, 16)
    b_block, b_col_rest = divide(b_left, PATCH)
    a_group, a_row_rest = divide(a_top, 16)
    a_block, a_col_rest = divide(a_left, PATCH)
    near_row = field(PEAK_ROW) + b_row_rest - a_row_rest + (ABOVE - centre_reach)
    near_col = divide(field(PEAK_COL) + b_col_rest - a_col_rest, PATCH)[1]
    for index, value in (
        (B_BLOCK, b_block),
        (B_ROW, 16.0 * b_group),
        (B_ROW_REST, b_row_rest),
        (B_COL_REST, b_col_rest),
        (A_BLOCK, a_block),
        (A_ROW, 16.0 * a_group),
        (A_ROW_REST, a_row_rest),
        (A_COL_REST, a_col_rest),
        (NEAR_ROW, near_row),
        (NEAR_COL, near_col),
    ):
        listed_ref[index : index + 1, :] = value.astype(jnp.int32)
    listed_ref[FIELDS:, :] = jnp.zeros((16 - FIELDS, capacity), jnp.int32)
    return jnp.max(before).astype(jnp.int32)


def cut_kernel(tile_ref, out_ref):
    strip = tile_ref[...]
    for block in range(out_ref.shape[0]):
        out_ref[block] = cut(strip, block * PATCH)


def cut_tile(tile):
    rows, cols = tile.shape
    blocks = -(-cols // PATCH)
    return pl.pallas_call(
        cut_kernel,
        grid=(rows // HALF_LANES,),
        out_shape=jax.ShapeDtypeStruct((blocks, rows + 16, WIDE), jnp.bfloat16),
        in_specs=[pl.BlockSpec((HALF_LANES, cols), lambda step: (step, 0))],
        out_specs=pl.BlockSpec((blocks, HALF_LANES, WIDE), lambda step: (0, step, 0)),
        cost_estimate=pl.CostEstimate(
            flops=0, bytes_accessed=2 * rows * (cols + blocks * WIDE), transcendentals=0
        ),
    )(tile)


def correlate(capacity, everyone, blocks, grid):
    n_row, n_col, a_rows, node_rows = grid
    tables, places = all_tables()
    a_blocks = (n_col * everyone.shape[2] + 76) // PATCH + 2
    vmem = pl.BlockSpec(memory_space=pltpu.VMEM)
    rows = pltpu.VMEM((capacity, HALF_LANES), jnp.float32)
    return pl.pallas_call(
        functools.partial(correlate_kernel, capacity, grid, places),
        out_shape=jax.ShapeDtypeStruct(
            (n_row * n_col, SPREAD_ROWS // 2, HALF_LANES), jnp.float32
        ),
        in_specs=[vmem, pl.BlockSpec(memory_space=pl.ANY), vmem],
        out_specs=vmem,
        scratch_shapes=[
            pltpu.VMEM((2 * BATCH * PATCH, WIDE), jnp.bfloat16),
            pltpu.VMEM((BATCH // TRIO, 2, 2, PATCH, WIDE), jnp.bfloat16),
            pltpu.VMEM((BATCH // TRIO * 2, PAIRED, WIDE), jnp.bfloat16),
            pltpu.VMEM((BATCH * PATCH, WIDE), jnp.bfloat16),
            pltpu.VMEM((BATCH, ABOVE + BELOW, HALF_LANES), jnp.float32),
            pltpu.VMEM((BATCH, ABOVE + BELOW, HALF_LANES), jnp.float32),
            pltpu.VMEM((BATCH // TRIO, 2, 2, 8, HALF_LANES), jnp.float32),
        ]
        + [rows] * 4
        + [
            pltpu.VMEM((a_blocks, n_row * a_rows + PATCH, WIDE), jnp.bfloat16),
            pltpu.VMEM(blocks.shape, jnp.bfloat16),
            rows,
            pltpu.VMEM((16, capacity), jnp.int32),
            pltpu.SMEM((16, capacity), jnp.int32),
            pltpu.SemaphoreType.DMA((2,)),
            pltpu.VMEM((2 * CAP_ROWS, HALF_LANES), jnp.float32),
            pltpu.VMEM((16, capacity), jnp.float32),
            pltpu.VMEM((TRIO, 2, 8, HALF_LANES), jnp.float32),
        ],
        compiler_params=pltpu.CompilerParams(vmem_limit_bytes=61 * 1024 * 1024),
    )(everyone, blocks, tables)


def per_device(a_window, b_section, owners, pos_rows, pos_cols, peaks):
    node_rows, node_cols = pos_rows.shape
    nodes = node_rows * node_cols
    n_row, n_col = lax.axis_size("row"), lax.axis_size("col")
    devices = n_row * n_col
    me_row, me_col = lax.axis_index("row"), lax.axis_index("col")
    share = max(2, (nodes * 8 // 5 + devices - 1) // devices)
    a_rows, a_cols = a_window.shape
    height, breadth = n_row * node_rows, n_col * node_cols

    mesh_col = me_col * node_cols + lax.broadcasted_iota(jnp.int32, pos_rows.shape, 1)
    records = jnp.concatenate(
        [
            owners.reshape(node_rows, node_cols),
            pos_rows // 16,
            pos_rows % 16,
            pos_cols // 16,
            pos_cols % 16,
            peaks[0],
            peaks[1],
            mesh_col,
        ],
        axis=1,
    ).astype(jnp.bfloat16)
    records = jnp.pad(records, ((0, 16 - node_rows), (0, 0)), constant_values=-1)
    sent = jnp.concatenate([a_window, records], axis=0)
    sent = jnp.broadcast_to(sent[None], (n_col,) + sent.shape)
    sent = lax.all_to_all(sent, "col", split_axis=0, concat_axis=0, tiled=True)
    everyone = lax.all_gather(sent, "row").reshape(devices, a_rows + 16, a_cols)

    grid = (n_row, n_col, a_rows, node_rows)
    spread = correlate(share * devices, everyone, cut_tile(b_section), grid)
    spread = lax.all_to_all(spread, ("row", "col"), split_axis=0, concat_axis=0, tiled=True)
    tall, broad = node_rows + 2 * RELAX, node_cols + 2 * RELAX
    spread = jnp.sum(spread, axis=0)
    half_lanes = HALF_LANES // 2
    spread = jnp.concatenate([spread[:, :half_lanes], spread[:, half_lanes:]], axis=0)[:tall]
    spread = [spread[:, SPREAD_LANES * value :][:, :broad] for value in range(3)]
    runner = spread[2][RELAX:-RELAX, RELAX:-RELAX]
    field = jnp.stack(spread[:2])
    for step in range(RELAX):
        reach = RELAX - 1 - step
        centre = field[:, 1:-1, 1:-1]
        around = (
            field[:, 2:, 1:-1] + field[:, :-2, 1:-1] + field[:, 1:-1, 2:] + field[:, 1:-1, :-2]
        )
        field = centre + stiffness * (around - 4.0 * centre)
        rows = me_row * node_rows - reach + jnp.arange(node_rows + 2 * reach)
        cols = me_col * node_cols - reach + jnp.arange(node_cols + 2 * reach)
        inside = ((rows >= 0) & (rows < height))[:, None] & ((cols >= 0) & (cols < breadth))[None]
        field = jnp.where(inside[None], field, 0.0)
    return (field, runner)


def solution(mesh):
    placed = (
        P("row", "col"),
        P("row", "col"),
        P("row", "col", None, None, None),
        P("row", "col"),
        P("row", "col"),
        P(None, "row", "col"),
    )
    return jax.shard_map(
        per_device,
        mesh=mesh,
        in_specs=placed,
        out_specs=(P(None, "row", "col"), P("row", "col")),
        check_vma=False,
    )
```

```python
import functools
import math

import jax
import jax.numpy as jnp
import numpy as np
from jax import lax
from jax.experimental import pallas as pl
from jax.experimental.pallas import tpu as pltpu
from jax.sharding import PartitionSpec as P

PATCH = 160
NODE_LANES = 16
SPREAD_LANES = 20
SPREAD_ROWS = 16
STRIDE = 8
RELAX = 2
WIDE = 256
HALF_LANES = 128
FREQS = PATCH // 2 + 1
GROUPS = 11
PAIRED = 16 * GROUPS
BIG = 3.0e38

sharpness = 80.0
epsilon = 1e-06
stiffness = 0.24
centre_reach = 2


def dft_tables():
    steps = np.arange(PATCH)
    angles = 2.0 * math.pi * ((steps[:, None] * steps[None, :FREQS]) % PATCH) / PATCH
    return (
        np.cos(angles).astype(jnp.bfloat16).astype(np.float32),
        np.sin(angles).astype(jnp.bfloat16).astype(np.float32),
    )


def kernel_tables():
    cosine, sine = dft_tables()
    weights = np.full((FREQS,), 2.0, np.float32)
    weights[0] = weights[-1] = 1.0
    across = np.zeros((WIDE, WIDE), np.float32)
    across[:PATCH, :FREQS] = cosine
    across[:PATCH, HALF_LANES : HALF_LANES + FREQS] = sine
    back_across = np.zeros((WIDE, WIDE), np.float32)
    back_across[:FREQS, :PATCH] = 0.5 * (cosine * weights).T
    back_across[HALF_LANES : HALF_LANES + FREQS, :PATCH] = 0.5 * (sine * weights).T
    down = np.zeros((PAIRED, PATCH), np.float32)
    back_down = np.zeros((PATCH, PAIRED), np.float32)
    for freq in range(FREQS):
        row = 16 * (freq // 8) + freq % 8
        down[row] = cosine[:, freq]
        down[row + 8] = sine[:, freq]
        back_down[:, row] = cosine[:, freq] * weights[freq]
        back_down[:, row + 8] = sine[:, freq] * weights[freq]
    return across, down, back_down, back_across


def listing_tables():
    lane = np.arange(HALF_LANES)
    group, place = lane // NODE_LANES, lane % NODE_LANES
    repeat = (lane[:, None] < NODE_LANES) & (place[None] == lane[:, None])
    earlier = (group[:, None] == group[None]) & (place[:, None] < place[None])
    first = np.broadcast_to(lane[:, None] < NODE_LANES, (HALF_LANES, HALF_LANES))
    below = lane[None] < lane[:, None]
    fields = np.zeros((2 * HALF_LANES, HALF_LANES), np.float32)
    fields[lane, group] = 1.0
    fields[HALF_LANES, MESH_ROW] = 1.0
    return repeat, np.concatenate([earlier, first], axis=1), below, below.T, first.T[:16], fields, (
        fields.T[:16]
    )


def all_tables():
    names = ("across", "down", "back_down", "back_across", "repeat", "within")
    names += ("below", "above", "count", "fields", "turned")
    places, parts, start = {}, [], 0
    for name, part in zip(names, kernel_tables() + listing_tables()):
        rows, lanes = part.shape
        places[name] = (start, rows, lanes)
        rows_up = -(-rows // 16) * 16
        parts.append(np.zeros((rows_up, WIDE), np.float32))
        parts[-1][:rows, :lanes] = part
        start += rows_up
    return jnp.asarray(np.concatenate(parts), jnp.bfloat16), places


OWNER, ROW_HIGH, ROW_LOW, COL_HIGH, COL_LOW, PEAK_ROW, PEAK_COL, MESH_COL, MESH_ROW = range(9)
B_BLOCK, B_ROW, B_ROW_REST, B_COL_REST = 0, 1, 2, 3
A_BLOCK, A_ROW, A_ROW_REST, A_COL_REST = 4, 5, 6, 7
NEAR_ROW, NEAR_COL = 8, 9
FIELDS = 10
BATCH = 6
TRIO = 3
ABOVE = 24
BELOW = 32
CAP_ROWS = 64
SECOND = FREQS
THIRD = 2 * FREQS - HALF_LANES


def cut(strip, start):
    if start >= strip.shape[1]:
        return jnp.zeros((strip.shape[0], WIDE), strip.dtype)
    piece = strip[:, start : min(start + PATCH, strip.shape[1])]
    gap = jnp.zeros((strip.shape[0], WIDE - piece.shape[1]), strip.dtype)
    return jnp.concatenate([piece, gap], axis=1)


def correlate_kernel(
    capacity,
    grid,
    places,
    everyone_ref,
    blocks_ref,
    tables_ref,
    out_ref,
    *scratch,
):
    patches, halves, crosses, inverses = scratch[:4]
    corrs = scratch[4:6]
    energies, totals, row_moments, col_moments, runners, a_ref, b_ref = scratch[6:13]
    columns_ref, listed_ref, items_ref, semaphores, caps_ref, rows_ref, shares_ref = scratch[13:]
    to_blocks = pltpu.make_async_copy(blocks_ref, b_ref, semaphores.at[0])
    to_blocks.start()

    def table(name):
        start, rows, lanes = places[name]
        return tables_ref[start : start + rows, :lanes]

    n_row, n_col, a_rows, node_rows = grid
    count = list_nodes(
        capacity,
        grid,
        everyone_ref,
        table,
        columns_ref,
        rows_ref,
        listed_ref,
    )
    for place in range(TRIO):
        for tile in range(2):
            freq = lax.broadcasted_iota(jnp.int32, (8, HALF_LANES), 1)
            freq = freq + (tile * HALF_LANES - place * FREQS)
            once = (freq == 0) | (freq == FREQS - 1)
            twice = (freq > 0) & (freq < FREQS - 1)
            shares_ref[place, tile] = jnp.where(twice, 4.0, jnp.where(once, 2.0, 0.0))
    caps_row = lax.broadcasted_iota(jnp.int32, caps_ref.shape, 0) - CAP_ROWS
    caps_ref[...] = jnp.where((caps_row >= 0) & (caps_row <= 2 * centre_reach), -BIG, BIG)
    to_scalars = pltpu.make_async_copy(listed_ref, items_ref, semaphores.at[1])
    to_scalars.start()

    a_ref[0] = jnp.zeros(a_ref.shape[1:], jnp.bfloat16)
    rim = jnp.zeros((a_ref.shape[0], PATCH // 2, WIDE), jnp.bfloat16)
    a_ref[:, : PATCH // 2, :] = rim
    a_ref[:, a_ref.shape[1] - PATCH // 2 :, :] = rim

    for row in range(n_row):
        strip = jnp.concatenate(
            [everyone_ref[row * n_col + col, :a_rows, :] for col in range(n_col)], axis=1
        )
        start = PATCH // 2 + row * a_rows
        for block in range(1, a_ref.shape[0]):
            a_ref[block, start : start + a_rows, :] = cut(strip, (block - 1) * PATCH)

    def at(step, stage, part):
        return jnp.clip(BATCH * (step - stage) + part, 0, capacity - 1)

    def extract(source, block, row, row_rest, col_rest, base):
        lanes = lax.broadcasted_iota(jnp.int32, (16, WIDE), 1) >= col_rest
        rows = lax.broadcasted_iota(jnp.int32, (16, WIDE), 0) >= row_rest

        def group(place):
            here = pl.ds(pl.multiple_of(row + 16 * place, 16), 16)
            return jnp.where(lanes, source[block, here, :], source[block + 1, here, :])

        groups = [group(place) for place in range(PATCH // 16 + 1)]
        groups[0] = jnp.where(rows, groups[0], groups.pop())
        for place, values in enumerate(groups):
            patches[base + 16 * place : base + 16 * place + 16, :] = values

    def patch_base(part, which):
        trio, place = divmod(part, TRIO)
        return ((2 * trio + which) * TRIO + place) * PATCH

    def stage_half(step):
        for part in range(BATCH):
            item = at(step, 0, part)
            for which, source, fields in (
                (0, a_ref, (A_BLOCK, A_ROW, A_ROW_REST, A_COL_REST)),
                (1, b_ref, (B_BLOCK, B_ROW, B_ROW_REST, B_COL_REST)),
            ):
                block, row, row_rest, col_rest = (items_ref[field, item] for field in fields)
                extract(source, block, row, row_rest, col_rest, patch_base(part, which))
        half = jnp.dot(patches[...], table("across"), preferred_element_type=jnp.float32)
        lanes = lax.broadcasted_iota(jnp.int32, (PATCH, HALF_LANES), 1)
        for trio in range(BATCH // TRIO):
            for which in range(2):
                for side in (slice(0, HALF_LANES), slice(HALF_LANES, WIDE)):
                    first, second, third = (
                        half[base : base + PATCH, side]
                        for base in (patch_base(TRIO * trio + n, which) for n in range(TRIO))
                    )
                    second = pltpu.roll(second, SECOND, axis=1)
                    third = pltpu.roll(third, THIRD, axis=1)
                    halves[trio, which, 0, :, side] = jnp.where(
                        lanes < SECOND, first, second
                    ).astype(jnp.bfloat16)
                    halves[trio, which, 1, :, side] = jnp.where(
                        lanes < THIRD, second, third
                    ).astype(jnp.bfloat16)

    def sides(spec, group):
        cc = spec[16 * group : 16 * group + 8, :HALF_LANES]
        cs = spec[16 * group : 16 * group + 8, HALF_LANES:]
        sc = spec[16 * group + 8 : 16 * group + 16, :HALF_LANES]
        ss = spec[16 * group + 8 : 16 * group + 16, HALF_LANES:]
        power = (cc * cc + cs * cs) + (sc * sc + ss * ss)
        return cc - ss, sc + cs, cc + ss, sc - cs, power

    def stage_inverse():
        down = table("down")
        top = lax.broadcasted_iota(jnp.int32, (8, HALF_LANES), 0) == 0
        for pair in range(2 * (BATCH // TRIO)):
            trio, tile = divmod(pair, 2)
            spec_a = jnp.dot(down, halves[trio, 0, tile], preferred_element_type=jnp.float32)
            spec_b = jnp.dot(down, halves[trio, 1, tile], preferred_element_type=jnp.float32)
            for group in range(GROUPS):
                a_pr, a_pi, a_mr, a_mi, a_power = sides(spec_a, group)
                b_pr, b_pi, b_mr, b_mi, b_power = sides(spec_b, group)
                if group == 0:
                    powers = [jnp.where(top, 0.5 * power, power) for power in (a_power, b_power)]
                elif group < GROUPS - 1:
                    powers = [powers[0] + a_power, powers[1] + b_power]
                else:
                    powers = [powers[0] + 0.5 * a_power, powers[1] + 0.5 * b_power]
                pr = a_pr * b_pr + a_pi * b_pi
                pi = a_pr * b_pi - a_pi * b_pr
                mr = a_mr * b_mr + a_mi * b_mi
                mi = a_mr * b_mi - a_mi * b_mr
                upper = jnp.concatenate([pr + mr, pi - mi], axis=1)
                lower = jnp.concatenate([pi + mi, mr - pr], axis=1)
                crosses[pair, 16 * group : 16 * group + 16, :] = jnp.concatenate(
                    [upper, lower], axis=0
                ).astype(jnp.bfloat16)
            energies[trio, 0, tile] = powers[0]
            energies[trio, 1, tile] = powers[1]
        lanes = lax.broadcasted_iota(jnp.int32, (PATCH, HALF_LANES), 1)
        for trio in range(BATCH // TRIO):
            low, high = (
                jnp.dot(
                    table("back_down"), crosses[2 * trio + tile], preferred_element_type=jnp.float32
                )
                for tile in range(2)
            )
            for side in (slice(0, HALF_LANES), slice(HALF_LANES, WIDE)):
                first = low[:, side]
                second = jnp.where(lanes >= SECOND, first, high[:, side])
                second = pltpu.roll(second, HALF_LANES - SECOND, axis=1)
                third = pltpu.roll(high[:, side], HALF_LANES - THIRD, axis=1)
                for place, inverse in enumerate((first, second, third)):
                    base = (TRIO * trio + place) * PATCH
                    inverses[base : base + PATCH, side] = inverse.astype(jnp.bfloat16)

    def stage_score(step):
        corr_all = jnp.dot(
            inverses[...], table("back_across"), preferred_element_type=jnp.float32
        )
        rows = lax.broadcasted_iota(jnp.int32, (8, HALF_LANES), 0)
        lanes = lax.broadcasted_iota(jnp.int32, (8, HALF_LANES), 1)
        shift_rows = (rows - centre_reach).astype(jnp.float32)
        row_near = rows <= 2 * centre_reach
        for part in range(BATCH):
            item = at(step, 2, part)
            near_row = items_ref[NEAR_ROW, item]
            near_col = items_ref[NEAR_COL, item]
            trio, place = divmod(part, TRIO)
            mean_a, mean_b = (
                jnp.sum(
                    energies[trio, which, 0] * shares_ref[place, 0]
                    + energies[trio, which, 1] * shares_ref[place, 1],
                    keepdims=True,
                )
                * (1.0 / float(PATCH**4))
                for which in range(2)
            )
            scale = 1.0 / (
                float(PATCH**4) * jnp.sqrt(mean_a + epsilon) * jnp.sqrt(mean_b + epsilon)
            )
            caps = caps_ref[pl.ds(CAP_ROWS - near_row, ABOVE + BELOW), :]
            total, row_moment, col_moment = 0.0, 0.0, 0.0
            best = None
            for half in range(2):
                corr = corr_all[
                    PATCH * part : PATCH * (part + 1),
                    half * HALF_LANES : (half + 1) * HALF_LANES,
                ]
                edge = jnp.concatenate([corr[PATCH - ABOVE :], corr[:BELOW]], axis=0)
                corrs[half][part] = edge
                far = jnp.maximum(
                    jnp.max(jnp.minimum(edge, caps).reshape(-1, 8, HALF_LANES), axis=0),
                    jnp.max(corr[BELOW : PATCH - ABOVE].reshape(-1, 8, HALF_LANES), axis=0),
                )
                if half == 0:
                    best = far
                else:
                    far = jnp.where(lanes < PATCH - HALF_LANES, far, -BIG)
                    best = jnp.maximum(best, far)
            for half in range(2):
                values = corrs[half][part, pl.ds(near_row, 8), :]
                place = lanes + half * HALF_LANES
                shift = place - near_col
                shift = jnp.where(shift >= PATCH // 2, shift - PATCH, shift)
                shift = jnp.where(shift < -(PATCH // 2), shift + PATCH, shift)
                inside = row_near & (place < PATCH)
                close = jnp.abs(shift) <= centre_reach
                weight = jnp.where(
                    inside & close, jnp.exp(sharpness * (values * scale)), 0.0
                )
                total = total + weight
                row_moment = row_moment + weight * shift_rows
                col_moment = col_moment + weight * shift.astype(jnp.float32)
                best = jnp.maximum(
                    best, jnp.where(inside & jnp.logical_not(close), values, -BIG)
                )
            totals[pl.ds(item, 1), :] = jnp.sum(total, axis=0, keepdims=True)
            row_moments[pl.ds(item, 1), :] = jnp.sum(row_moment, axis=0, keepdims=True)
            col_moments[pl.ds(item, 1), :] = jnp.sum(col_moment, axis=0, keepdims=True)
            runners[pl.ds(item, 1), :] = jnp.max(best * scale, axis=0, keepdims=True)

    to_scalars.wait()
    to_blocks.wait()

    steps = jnp.maximum((count + BATCH - 1) // BATCH, 2)
    stage_half(0)
    stage_inverse()
    stage_half(1)

    @pl.loop(2, steps)
    def _(step):
        stage_score(step)
        stage_inverse()
        stage_half(step)

    stage_score(steps)
    stage_inverse()
    stage_score(steps + 1)

    used = lax.broadcasted_iota(jnp.int32, (capacity, 1), 0) < count
    total = jnp.sum(totals[...], axis=1, keepdims=True)
    peak_row = columns_ref[:, PEAK_ROW : PEAK_ROW + 1]
    peak_col = columns_ref[:, PEAK_COL : PEAK_COL + 1]
    results = (
        peak_row + jnp.sum(row_moments[...], axis=1, keepdims=True) / total,
        peak_col + jnp.sum(col_moments[...], axis=1, keepdims=True) / total,
        jnp.maximum(jnp.max(runners[...], axis=1, keepdims=True), -2.0),
    )
    lanes = lax.broadcasted_iota(jnp.int32, (capacity, HALF_LANES), 1)
    terms = [jnp.zeros((capacity, HALF_LANES), jnp.float32)] * 3
    for value, rest in enumerate(results):
        rest = jnp.where(used, rest, 0.0)
        for term in range(3):
            here = rest.astype(jnp.bfloat16).astype(jnp.float32)
            terms[term] = jnp.where(lanes // SPREAD_LANES == value, here, terms[term])
            rest = rest - here
    slot_row = rows_ref[MESH_ROW : MESH_ROW + 1, :]
    slot_col = columns_ref[:, MESH_COL : MESH_COL + 1]
    offset = (lanes % SPREAD_LANES - RELAX).astype(jnp.float32)
    shape = (n_row * SPREAD_ROWS, capacity)
    place = lax.broadcasted_iota(jnp.int32, shape, 0)
    row = place // SPREAD_ROWS * node_rows + place % SPREAD_ROWS - RELAX
    rows_picked = jnp.where(slot_row == row.astype(jnp.float32), 1.0, 0.0).astype(jnp.bfloat16)
    for col in range(n_col):
        here = slot_col == offset + float(col * NODE_LANES)
        sent = sum(
            jnp.dot(
                rows_picked,
                jnp.where(here, term, 0.0).astype(jnp.bfloat16),
                preferred_element_type=jnp.float32,
            )
            for term in terms
        )
        for row in range(n_row):
            block = sent[SPREAD_ROWS * row : SPREAD_ROWS * (row + 1)]
            turned = pltpu.roll(block[8:], HALF_LANES // 2, axis=1)
            out_ref[row * n_col + col] = jnp.where(
                lanes[:8] < HALF_LANES // 2, block[:8], turned
            )


def list_nodes(
    capacity,
    grid,
    everyone_ref,
    table,
    columns_ref,
    rows_ref,
    listed_ref,
):
    n_row, n_col, a_rows, node_rows = grid
    me = (lax.axis_index("row") * n_col + lax.axis_index("col")).astype(jnp.float32)
    exact = functools.partial(lax.dot_general, preferred_element_type=jnp.float32)
    plain = (((1,), (0,)), ((), ()))
    turned = (((1,), (1,)), ((), ()))

    slot = lax.broadcasted_iota(jnp.int32, (capacity, HALF_LANES), 0).astype(jnp.float32)
    before = jnp.zeros((1, HALF_LANES), jnp.float32)
    found = jnp.zeros((capacity, 3 * HALF_LANES), jnp.float32)
    for block in range(n_row * n_col // 8):
        records = everyone_ref[8 * block : 8 * block + 8, a_rows : a_rows + 16, :]
        records = records.reshape(HALF_LANES, HALF_LANES)
        mine = exact(records, table("repeat"), plain) == me
        ones = jnp.where(mine, 1.0, 0.0).astype(jnp.bfloat16)
        counts = exact(ones, table("within"), plain)
        within, loads = counts[:, :HALF_LANES], counts[:, HALF_LANES:]
        base = exact(table("below"), loads.astype(jnp.bfloat16), plain) + before
        slots = jnp.where(mine, within + base, -1.0)
        row_loads = exact(table("count"), ones, turned)
        row_base = exact(row_loads.astype(jnp.bfloat16), table("above"), plain)[:1] + before
        holds = (slot >= row_base) & (slot < row_base + row_loads[:1])
        local = lax.broadcasted_iota(jnp.int32, (HALF_LANES, HALF_LANES), 0) % 16
        mesh_row = (local + 8 * block // n_col * node_rows).astype(jnp.float32)
        found = found + exact(
            jnp.where(holds, 1.0, 0.0).astype(jnp.bfloat16),
            jnp.concatenate(
                [records, slots.astype(jnp.bfloat16), mesh_row.astype(jnp.bfloat16)], axis=1
            ),
            plain,
        )
        before = before + jnp.sum(loads, axis=0, keepdims=True)

    same = found[:, HALF_LANES : 2 * HALF_LANES] == slot
    taken = jnp.concatenate(
        [jnp.where(same, found[:, :HALF_LANES], 0.0), found[:, 2 * HALF_LANES :]], axis=1
    ).astype(jnp.bfloat16)
    columns_ref[...] = exact(taken, table("fields"), plain)
    rows = exact(table("turned"), taken, turned)
    rows_ref[...] = rows

    def field(index):
        return rows[index : index + 1, :]

    def divide(value, by):
        whole = jnp.floor((value + 0.5) * (1.0 / by))
        return whole, value - whole * by

    half = float(PATCH // 2)
    b_top = jnp.maximum(16.0 * field(ROW_HIGH) + field(ROW_LOW) - half, 0.0)
    b_left = jnp.maximum(16.0 * field(COL_HIGH) + field(COL_LOW) - half, 0.0)
    a_top = STRIDE * field(MESH_ROW) + STRIDE // 2
    a_left = STRIDE * field(MESH_COL) + (STRIDE // 2 + half)
    b_group, b_row_rest = divide(b_top, 16)
    b_block, b_col_rest = divide(b_left, PATCH)
    a_group, a_row_rest = divide(a_top, 16)
    a_block, a_col_rest = divide(a_left, PATCH)
    near_row = field(PEAK_ROW) + b_row_rest - a_row_rest + (ABOVE - centre_reach)
    near_col = divide(field(PEAK_COL) + b_col_rest - a_col_rest, PATCH)[1]
    for index, value in (
        (B_BLOCK, b_block),
        (B_ROW, 16.0 * b_group),
        (B_ROW_REST, b_row_rest),
        (B_COL_REST, b_col_rest),
        (A_BLOCK, a_block),
        (A_ROW, 16.0 * a_group),
        (A_ROW_REST, a_row_rest),
        (A_COL_REST, a_col_rest),
        (NEAR_ROW, near_row),
        (NEAR_COL, near_col),
    ):
        listed_ref[index : index + 1, :] = value.astype(jnp.int32)
    listed_ref[FIELDS:, :] = jnp.zeros((16 - FIELDS, capacity), jnp.int32)
    return jnp.max(before).astype(jnp.int32)


def pack_kernel(
    a_ref, owners_ref, rows_ref, cols_ref, peaks_ref, sent_ref, records_ref
):
    node_rows, node_cols = rows_ref.shape
    mesh_col = lax.broadcasted_iota(jnp.int32, (node_rows, node_cols), 1)
    mesh_col = mesh_col + lax.axis_index("col") * node_cols
    fields = (
        owners_ref[...],
        rows_ref[...] >> 4,
        rows_ref[...] & 15,
        cols_ref[...] >> 4,
        cols_ref[...] & 15,
        peaks_ref[0],
        peaks_ref[1],
        mesh_col,
    )
    records_ref[...] = jnp.full(records_ref.shape, -1.0, jnp.float32)
    for index, values in enumerate(fields):
        lanes = slice(index * NODE_LANES, (index + 1) * NODE_LANES)
        records_ref[:node_rows, lanes] = values.astype(jnp.float32)
    records = records_ref[...].astype(jnp.bfloat16)
    height = a_ref.shape[0]
    for receiver in range(sent_ref.shape[0]):
        sent_ref[receiver, :height, :] = a_ref[...]
        sent_ref[receiver, height:, :] = records


def pack(a_window, owners, pos_rows, pos_cols, peaks, receivers):
    height, lanes = a_window.shape
    vmem = pl.BlockSpec(memory_space=pltpu.VMEM)
    return pl.pallas_call(
        pack_kernel,
        out_shape=jax.ShapeDtypeStruct((receivers, height + 16, lanes), jnp.bfloat16),
        in_specs=[vmem] * 5,
        out_specs=vmem,
        scratch_shapes=[pltpu.VMEM((16, lanes), jnp.float32)],
    )(a_window, owners, pos_rows, pos_cols, peaks)


def cut_kernel(tile_ref, out_ref):
    strip = tile_ref[...]
    for block in range(out_ref.shape[0]):
        out_ref[block] = cut(strip, block * PATCH)


def cut_tile(tile):
    rows, cols = tile.shape
    blocks = -(-cols // PATCH)
    return pl.pallas_call(
        cut_kernel,
        grid=(rows // HALF_LANES,),
        out_shape=jax.ShapeDtypeStruct((blocks, rows + 16, WIDE), jnp.bfloat16),
        in_specs=[pl.BlockSpec((HALF_LANES, cols), lambda step: (step, 0))],
        out_specs=pl.BlockSpec((blocks, HALF_LANES, WIDE), lambda step: (0, step, 0)),
        cost_estimate=pl.CostEstimate(
            flops=0, bytes_accessed=2 * rows * (cols + blocks * WIDE), transcendentals=0
        ),
    )(tile)


def correlate(capacity, everyone, blocks, grid):
    n_row, n_col, a_rows, node_rows = grid
    tables, places = all_tables()
    a_blocks = (n_col * everyone.shape[2] + 76) // PATCH + 2
    vmem = pl.BlockSpec(memory_space=pltpu.VMEM)
    rows = pltpu.VMEM((capacity, HALF_LANES), jnp.float32)
    return pl.pallas_call(
        functools.partial(correlate_kernel, capacity, grid, places),
        out_shape=jax.ShapeDtypeStruct(
            (n_row * n_col, SPREAD_ROWS // 2, HALF_LANES), jnp.float32
        ),
        in_specs=[vmem, pl.BlockSpec(memory_space=pl.ANY), vmem],
        out_specs=vmem,
        scratch_shapes=[
            pltpu.VMEM((2 * BATCH * PATCH, WIDE), jnp.bfloat16),
            pltpu.VMEM((BATCH // TRIO, 2, 2, PATCH, WIDE), jnp.bfloat16),
            pltpu.VMEM((BATCH // TRIO * 2, PAIRED, WIDE), jnp.bfloat16),
            pltpu.VMEM((BATCH * PATCH, WIDE), jnp.bfloat16),
            pltpu.VMEM((BATCH, ABOVE + BELOW, HALF_LANES), jnp.float32),
            pltpu.VMEM((BATCH, ABOVE + BELOW, HALF_LANES), jnp.float32),
            pltpu.VMEM((BATCH // TRIO, 2, 2, 8, HALF_LANES), jnp.float32),
        ]
        + [rows] * 4
        + [
            pltpu.VMEM((a_blocks, n_row * a_rows + PATCH, WIDE), jnp.bfloat16),
            pltpu.VMEM(blocks.shape, jnp.bfloat16),
            rows,
            pltpu.VMEM((16, capacity), jnp.int32),
            pltpu.SMEM((16, capacity), jnp.int32),
            pltpu.SemaphoreType.DMA((2,)),
            pltpu.VMEM((2 * CAP_ROWS, HALF_LANES), jnp.float32),
            pltpu.VMEM((16, capacity), jnp.float32),
            pltpu.VMEM((TRIO, 2, 8, HALF_LANES), jnp.float32),
        ],
        compiler_params=pltpu.CompilerParams(vmem_limit_bytes=61 * 1024 * 1024),
    )(everyone, blocks, tables)


def per_device(a_window, b_section, owners, pos_rows, pos_cols, peaks):
    node_rows, node_cols = pos_rows.shape
    nodes = node_rows * node_cols
    n_row, n_col = lax.axis_size("row"), lax.axis_size("col")
    devices = n_row * n_col
    me_row, me_col = lax.axis_index("row"), lax.axis_index("col")
    share = max(2, (nodes * 8 // 5 + devices - 1) // devices)
    a_rows, a_cols = a_window.shape
    height, breadth = n_row * node_rows, n_col * node_cols

    sent = pack(
        a_window, owners.reshape(node_rows, node_cols), pos_rows, pos_cols, peaks, n_col
    )
    sent = lax.all_to_all(sent, "col", split_axis=0, concat_axis=0, tiled=True)
    everyone = lax.all_gather(sent, "row").reshape(devices, a_rows + 16, a_cols)

    grid = (n_row, n_col, a_rows, node_rows)
    spread = correlate(share * devices, everyone, cut_tile(b_section), grid)
    spread = lax.all_to_all(spread, ("row", "col"), split_axis=0, concat_axis=0, tiled=True)
    tall, broad = node_rows + 2 * RELAX, node_cols + 2 * RELAX
    spread = jnp.sum(spread, axis=0)
    half_lanes = HALF_LANES // 2
    spread = jnp.concatenate([spread[:, :half_lanes], spread[:, half_lanes:]], axis=0)[:tall]
    spread = [spread[:, SPREAD_LANES * value :][:, :broad] for value in range(3)]
    runner = spread[2][RELAX:-RELAX, RELAX:-RELAX]
    field = jnp.stack(spread[:2])
    for step in range(RELAX):
        reach = RELAX - 1 - step
        centre = field[:, 1:-1, 1:-1]
        around = (
            field[:, 2:, 1:-1] + field[:, :-2, 1:-1] + field[:, 1:-1, 2:] + field[:, 1:-1, :-2]
        )
        field = centre + stiffness * (around - 4.0 * centre)
        rows = me_row * node_rows - reach + jnp.arange(node_rows + 2 * reach)
        cols = me_col * node_cols - reach + jnp.arange(node_cols + 2 * reach)
        inside = ((rows >= 0) & (rows < height))[:, None] & ((cols >= 0) & (cols < breadth))[None]
        field = jnp.where(inside[None], field, 0.0)
    return (field, runner)


def solution(mesh):
    placed = (
        P("row", "col"),
        P("row", "col"),
        P("row", "col", None, None, None),
        P("row", "col"),
        P("row", "col"),
        P(None, "row", "col"),
    )
    return jax.shard_map(
        per_device,
        mesh=mesh,
        in_specs=placed,
        out_specs=(P(None, "row", "col"), P("row", "col")),
        check_vma=False,
    )
```

```python
import functools
import math

import jax
import jax.numpy as jnp
import numpy as np
from jax import lax
from jax.experimental import pallas as pl
from jax.experimental.pallas import tpu as pltpu
from jax.sharding import PartitionSpec as P

PATCH = 160
NODE_LANES = 16
SPREAD_LANES = 20
SPREAD_ROWS = 16
STRIDE = 8
RELAX = 2
WIDE = 256
HALF_LANES = 128
FREQS = PATCH // 2 + 1
GROUPS = 10
PAIRED = 16 * GROUPS
BIG = 3.0e38

sharpness = 80.0
epsilon = 1e-06
stiffness = 0.24
centre_reach = 2


def dft_tables():
    steps = np.arange(PATCH)
    angles = 2.0 * math.pi * ((steps[:, None] * steps[None, :FREQS]) % PATCH) / PATCH
    return (
        np.cos(angles).astype(jnp.bfloat16).astype(np.float32),
        np.sin(angles).astype(jnp.bfloat16).astype(np.float32),
    )


def kernel_tables():
    cosine, sine = dft_tables()
    weights = np.full((FREQS,), 2.0, np.float32)
    weights[0] = weights[-1] = 1.0
    across = np.zeros((WIDE, WIDE), np.float32)
    across[:PATCH, :FREQS] = cosine
    across[:PATCH, HALF_LANES : HALF_LANES + FREQS] = sine
    back_across = np.zeros((WIDE, WIDE), np.float32)
    back_across[:FREQS, :PATCH] = 0.5 * (cosine * weights).T
    back_across[HALF_LANES : HALF_LANES + FREQS, :PATCH] = 0.5 * (sine * weights).T
    down = np.zeros((PAIRED, PATCH), np.float32)
    back_down = np.zeros((PATCH, PAIRED), np.float32)
    for freq in range(FREQS - 1):
        row = 16 * (freq // 8) + freq % 8
        down[row] = cosine[:, freq]
        down[row + 8] = sine[:, freq] if freq else cosine[:, -1]
        back_down[:, row] = cosine[:, freq] * weights[freq]
        back_down[:, row + 8] = sine[:, freq] * weights[freq] if freq else cosine[:, -1]
    return across, down, back_down, back_across


def listing_tables():
    lane = np.arange(HALF_LANES)
    group, place = lane // NODE_LANES, lane % NODE_LANES
    repeat = (lane[:, None] < NODE_LANES) & (place[None] == lane[:, None])
    earlier = (group[:, None] == group[None]) & (place[:, None] < place[None])
    first = np.broadcast_to(lane[:, None] < NODE_LANES, (HALF_LANES, HALF_LANES))
    below = lane[None] < lane[:, None]
    fields = np.zeros((2 * HALF_LANES, HALF_LANES), np.float32)
    fields[lane, group] = 1.0
    fields[HALF_LANES, MESH_ROW] = 1.0
    return repeat, np.concatenate([earlier, first], axis=1), below, below.T, first.T[:16], fields, (
        fields.T[:16]
    )


def all_tables():
    names = ("across", "down", "back_down", "back_across", "repeat", "within")
    names += ("below", "above", "count", "fields", "turned")
    places, parts, start = {}, [], 0
    for name, part in zip(names, kernel_tables() + listing_tables()):
        rows, lanes = part.shape
        places[name] = (start, rows, lanes)
        rows_up = -(-rows // 16) * 16
        parts.append(np.zeros((rows_up, WIDE), np.float32))
        parts[-1][:rows, :lanes] = part
        start += rows_up
    return jnp.asarray(np.concatenate(parts), jnp.bfloat16), places


OWNER, ROW_HIGH, ROW_LOW, COL_HIGH, COL_LOW, PEAK_ROW, PEAK_COL, MESH_COL, MESH_ROW = range(9)
B_BLOCK, B_ROW, B_ROW_REST, B_COL_REST = 0, 1, 2, 3
A_BLOCK, A_ROW, A_ROW_REST, A_COL_REST = 4, 5, 6, 7
NEAR_ROW, NEAR_COL = 8, 9
FIELDS = 10
BATCH = 6
TRIO = 3
ABOVE = 24
BELOW = 32
CAP_ROWS = 64
SECOND = FREQS
THIRD = 2 * FREQS - HALF_LANES


def cut(strip, start):
    if start >= strip.shape[1]:
        return jnp.zeros((strip.shape[0], WIDE), strip.dtype)
    piece = strip[:, start : min(start + PATCH, strip.shape[1])]
    gap = jnp.zeros((strip.shape[0], WIDE - piece.shape[1]), strip.dtype)
    return jnp.concatenate([piece, gap], axis=1)


def correlate_kernel(
    capacity,
    grid,
    places,
    everyone_ref,
    blocks_ref,
    tables_ref,
    out_ref,
    *scratch,
):
    patches, halves, crosses, inverses = scratch[:4]
    corrs = scratch[4:6]
    energies, totals, row_moments, col_moments, runners, a_ref, b_ref = scratch[6:13]
    columns_ref, listed_ref, items_ref, semaphores, caps_ref, rows_ref, shares_ref = scratch[13:]
    to_blocks = pltpu.make_async_copy(blocks_ref, b_ref, semaphores.at[0])
    to_blocks.start()

    def table(name):
        start, rows, lanes = places[name]
        return tables_ref[start : start + rows, :lanes]

    n_row, n_col, a_rows, node_rows = grid
    count = list_nodes(
        capacity,
        grid,
        everyone_ref,
        table,
        columns_ref,
        rows_ref,
        listed_ref,
    )
    for place in range(TRIO):
        for tile in range(2):
            freq = lax.broadcasted_iota(jnp.int32, (8, HALF_LANES), 1)
            freq = freq + (tile * HALF_LANES - place * FREQS)
            once = (freq == 0) | (freq == FREQS - 1)
            twice = (freq > 0) & (freq < FREQS - 1)
            shares_ref[place, tile] = jnp.where(twice, 4.0, jnp.where(once, 2.0, 0.0))
    caps_row = lax.broadcasted_iota(jnp.int32, caps_ref.shape, 0) - CAP_ROWS
    caps_ref[...] = jnp.where((caps_row >= 0) & (caps_row <= 2 * centre_reach), -BIG, BIG)
    to_scalars = pltpu.make_async_copy(listed_ref, items_ref, semaphores.at[1])
    to_scalars.start()

    a_ref[0] = jnp.zeros(a_ref.shape[1:], jnp.bfloat16)
    rim = jnp.zeros((a_ref.shape[0], PATCH // 2, WIDE), jnp.bfloat16)
    a_ref[:, : PATCH // 2, :] = rim
    a_ref[:, a_ref.shape[1] - PATCH // 2 :, :] = rim

    for row in range(n_row):
        strip = jnp.concatenate(
            [everyone_ref[row * n_col + col, :a_rows, :] for col in range(n_col)], axis=1
        )
        start = PATCH // 2 + row * a_rows
        for block in range(1, a_ref.shape[0]):
            a_ref[block, start : start + a_rows, :] = cut(strip, (block - 1) * PATCH)

    def at(step, stage, part):
        return jnp.clip(BATCH * (step - stage) + part, 0, capacity - 1)

    def extract(source, block, row, row_rest, col_rest, base):
        lanes = lax.broadcasted_iota(jnp.int32, (16, WIDE), 1) >= col_rest
        rows = lax.broadcasted_iota(jnp.int32, (16, WIDE), 0) >= row_rest

        def group(place):
            here = pl.ds(pl.multiple_of(row + 16 * place, 16), 16)
            return jnp.where(lanes, source[block, here, :], source[block + 1, here, :])

        groups = [group(place) for place in range(PATCH // 16 + 1)]
        groups[0] = jnp.where(rows, groups[0], groups.pop())
        for place, values in enumerate(groups):
            patches[base + 16 * place : base + 16 * place + 16, :] = values

    def patch_base(part, which):
        trio, place = divmod(part, TRIO)
        return ((2 * trio + which) * TRIO + place) * PATCH

    def stage_half(step):
        for part in range(BATCH):
            item = at(step, 0, part)
            for which, source, fields in (
                (0, a_ref, (A_BLOCK, A_ROW, A_ROW_REST, A_COL_REST)),
                (1, b_ref, (B_BLOCK, B_ROW, B_ROW_REST, B_COL_REST)),
            ):
                block, row, row_rest, col_rest = (items_ref[field, item] for field in fields)
                extract(source, block, row, row_rest, col_rest, patch_base(part, which))
        half = jnp.dot(patches[...], table("across"), preferred_element_type=jnp.float32)
        lanes = lax.broadcasted_iota(jnp.int32, (PATCH, HALF_LANES), 1)
        for trio in range(BATCH // TRIO):
            for which in range(2):
                for side in (slice(0, HALF_LANES), slice(HALF_LANES, WIDE)):
                    first, second, third = (
                        half[base : base + PATCH, side]
                        for base in (patch_base(TRIO * trio + n, which) for n in range(TRIO))
                    )
                    second = pltpu.roll(second, SECOND, axis=1)
                    third = pltpu.roll(third, THIRD, axis=1)
                    halves[trio, which, 0, :, side] = jnp.where(
                        lanes < SECOND, first, second
                    ).astype(jnp.bfloat16)
                    halves[trio, which, 1, :, side] = jnp.where(
                        lanes < THIRD, second, third
                    ).astype(jnp.bfloat16)

    def sides(spec, group):
        cc = spec[16 * group : 16 * group + 8, :HALF_LANES]
        cs = spec[16 * group : 16 * group + 8, HALF_LANES:]
        sc = spec[16 * group + 8 : 16 * group + 16, :HALF_LANES]
        ss = spec[16 * group + 8 : 16 * group + 16, HALF_LANES:]
        power = (cc * cc + cs * cs) + (sc * sc + ss * ss)
        return (cc - ss, sc + cs, cc + ss, sc - cs, power), (cc, cs, sc, ss)

    def stage_inverse():
        down = table("down")
        top = lax.broadcasted_iota(jnp.int32, (8, HALF_LANES), 0) == 0
        for pair in range(2 * (BATCH // TRIO)):
            trio, tile = divmod(pair, 2)
            spec_a = jnp.dot(down, halves[trio, 0, tile], preferred_element_type=jnp.float32)
            spec_b = jnp.dot(down, halves[trio, 1, tile], preferred_element_type=jnp.float32)
            for group in range(GROUPS):
                (a_pr, a_pi, a_mr, a_mi, a_power), a_plain = sides(spec_a, group)
                (b_pr, b_pi, b_mr, b_mi, b_power), b_plain = sides(spec_b, group)
                if group == 0:
                    powers = [jnp.where(top, 0.5 * power, power) for power in (a_power, b_power)]
                else:
                    powers = [powers[0] + a_power, powers[1] + b_power]
                pr = a_pr * b_pr + a_pi * b_pi
                pi = a_pr * b_pi - a_pi * b_pr
                mr = a_mr * b_mr + a_mi * b_mi
                mi = a_mr * b_mi - a_mi * b_mr
                outs = [pr + mr, pi - mi, pi + mi, mr - pr]
                if group == 0:
                    for half in (0, 2):
                        (ar, ai), (br, bi) = a_plain[half : half + 2], b_plain[half : half + 2]
                        outs[half] = jnp.where(top, 2.0 * (ar * br + ai * bi), outs[half])
                        outs[half + 1] = jnp.where(top, 2.0 * (ar * bi - ai * br), outs[half + 1])
                upper = jnp.concatenate(outs[:2], axis=1)
                lower = jnp.concatenate(outs[2:], axis=1)
                crosses[pair, 16 * group : 16 * group + 16, :] = jnp.concatenate(
                    [upper, lower], axis=0
                ).astype(jnp.bfloat16)
            energies[trio, 0, tile] = powers[0]
            energies[trio, 1, tile] = powers[1]
        lanes = lax.broadcasted_iota(jnp.int32, (PATCH, HALF_LANES), 1)
        for trio in range(BATCH // TRIO):
            low, high = (
                jnp.dot(
                    table("back_down"), crosses[2 * trio + tile], preferred_element_type=jnp.float32
                )
                for tile in range(2)
            )
            for side in (slice(0, HALF_LANES), slice(HALF_LANES, WIDE)):
                first = low[:, side]
                second = jnp.where(lanes >= SECOND, first, high[:, side])
                second = pltpu.roll(second, HALF_LANES - SECOND, axis=1)
                third = pltpu.roll(high[:, side], HALF_LANES - THIRD, axis=1)
                for place, inverse in enumerate((first, second, third)):
                    base = (TRIO * trio + place) * PATCH
                    inverses[base : base + PATCH, side] = inverse.astype(jnp.bfloat16)

    def stage_score(step):
        corr_all = jnp.dot(
            inverses[...], table("back_across"), preferred_element_type=jnp.float32
        )
        rows = lax.broadcasted_iota(jnp.int32, (8, HALF_LANES), 0)
        lanes = lax.broadcasted_iota(jnp.int32, (8, HALF_LANES), 1)
        shift_rows = (rows - centre_reach).astype(jnp.float32)
        row_near = rows <= 2 * centre_reach
        for part in range(BATCH):
            item = at(step, 2, part)
            near_row = items_ref[NEAR_ROW, item]
            near_col = items_ref[NEAR_COL, item]
            trio, place = divmod(part, TRIO)
            mean_a, mean_b = (
                jnp.sum(
                    energies[trio, which, 0] * shares_ref[place, 0]
                    + energies[trio, which, 1] * shares_ref[place, 1],
                    keepdims=True,
                )
                * (1.0 / float(PATCH**4))
                for which in range(2)
            )
            scale = 1.0 / (
                float(PATCH**4) * jnp.sqrt(mean_a + epsilon) * jnp.sqrt(mean_b + epsilon)
            )
            caps = caps_ref[pl.ds(CAP_ROWS - near_row, ABOVE + BELOW), :]
            total, row_moment, col_moment = 0.0, 0.0, 0.0
            best = None
            for half in range(2):
                corr = corr_all[
                    PATCH * part : PATCH * (part + 1),
                    half * HALF_LANES : (half + 1) * HALF_LANES,
                ]
                edge = jnp.concatenate([corr[PATCH - ABOVE :], corr[:BELOW]], axis=0)
                corrs[half][part] = edge
                far = jnp.maximum(
                    jnp.max(jnp.minimum(edge, caps).reshape(-1, 8, HALF_LANES), axis=0),
                    jnp.max(corr[BELOW : PATCH - ABOVE].reshape(-1, 8, HALF_LANES), axis=0),
                )
                if half == 0:
                    best = far
                else:
                    far = jnp.where(lanes < PATCH - HALF_LANES, far, -BIG)
                    best = jnp.maximum(best, far)
            for half in range(2):
                values = corrs[half][part, pl.ds(near_row, 8), :]
                place = lanes + half * HALF_LANES
                shift = place - near_col
                shift = jnp.where(shift >= PATCH // 2, shift - PATCH, shift)
                shift = jnp.where(shift < -(PATCH // 2), shift + PATCH, shift)
                inside = row_near & (place < PATCH)
                close = jnp.abs(shift) <= centre_reach
                weight = jnp.where(
                    inside & close, jnp.exp(sharpness * (values * scale)), 0.0
                )
                total = total + weight
                row_moment = row_moment + weight * shift_rows
                col_moment = col_moment + weight * shift.astype(jnp.float32)
                best = jnp.maximum(
                    best, jnp.where(inside & jnp.logical_not(close), values, -BIG)
                )
            totals[pl.ds(item, 1), :] = jnp.sum(total, axis=0, keepdims=True)
            row_moments[pl.ds(item, 1), :] = jnp.sum(row_moment, axis=0, keepdims=True)
            col_moments[pl.ds(item, 1), :] = jnp.sum(col_moment, axis=0, keepdims=True)
            runners[pl.ds(item, 1), :] = jnp.max(best * scale, axis=0, keepdims=True)

    to_scalars.wait()
    to_blocks.wait()

    steps = jnp.maximum((count + BATCH - 1) // BATCH, 2)
    stage_half(0)
    stage_inverse()
    stage_half(1)

    @pl.loop(2, steps)
    def _(step):
        stage_score(step)
        stage_inverse()
        stage_half(step)

    stage_score(steps)
    stage_inverse()
    stage_score(steps + 1)

    used = lax.broadcasted_iota(jnp.int32, (capacity, 1), 0) < count
    total = jnp.sum(totals[...], axis=1, keepdims=True)
    peak_row = columns_ref[:, PEAK_ROW : PEAK_ROW + 1]
    peak_col = columns_ref[:, PEAK_COL : PEAK_COL + 1]
    results = (
        peak_row + jnp.sum(row_moments[...], axis=1, keepdims=True) / total,
        peak_col + jnp.sum(col_moments[...], axis=1, keepdims=True) / total,
        jnp.maximum(jnp.max(runners[...], axis=1, keepdims=True), -2.0),
    )
    lanes = lax.broadcasted_iota(jnp.int32, (capacity, HALF_LANES), 1)
    terms = [jnp.zeros((capacity, HALF_LANES), jnp.float32)] * 3
    for value, rest in enumerate(results):
        rest = jnp.where(used, rest, 0.0)
        for term in range(3):
            here = rest.astype(jnp.bfloat16).astype(jnp.float32)
            terms[term] = jnp.where(lanes // SPREAD_LANES == value, here, terms[term])
            rest = rest - here
    slot_row = rows_ref[MESH_ROW : MESH_ROW + 1, :]
    slot_col = columns_ref[:, MESH_COL : MESH_COL + 1]
    offset = (lanes % SPREAD_LANES - RELAX).astype(jnp.float32)
    shape = (n_row * SPREAD_ROWS, capacity)
    place = lax.broadcasted_iota(jnp.int32, shape, 0)
    row = place // SPREAD_ROWS * node_rows + place % SPREAD_ROWS - RELAX
    rows_picked = jnp.where(slot_row == row.astype(jnp.float32), 1.0, 0.0).astype(jnp.bfloat16)
    for col in range(n_col):
        here = slot_col == offset + float(col * NODE_LANES)
        sent = sum(
            jnp.dot(
                rows_picked,
                jnp.where(here, term, 0.0).astype(jnp.bfloat16),
                preferred_element_type=jnp.float32,
            )
            for term in terms
        )
        for row in range(n_row):
            block = sent[SPREAD_ROWS * row : SPREAD_ROWS * (row + 1)]
            turned = pltpu.roll(block[8:], HALF_LANES // 2, axis=1)
            out_ref[row * n_col + col] = jnp.where(
                lanes[:8] < HALF_LANES // 2, block[:8], turned
            )


def list_nodes(
    capacity,
    grid,
    everyone_ref,
    table,
    columns_ref,
    rows_ref,
    listed_ref,
):
    n_row, n_col, a_rows, node_rows = grid
    me = (lax.axis_index("row") * n_col + lax.axis_index("col")).astype(jnp.float32)
    exact = functools.partial(lax.dot_general, preferred_element_type=jnp.float32)
    plain = (((1,), (0,)), ((), ()))
    turned = (((1,), (1,)), ((), ()))

    slot = lax.broadcasted_iota(jnp.int32, (capacity, HALF_LANES), 0).astype(jnp.float32)
    before = jnp.zeros((1, HALF_LANES), jnp.float32)
    found = jnp.zeros((capacity, 3 * HALF_LANES), jnp.float32)
    for block in range(n_row * n_col // 8):
        records = everyone_ref[8 * block : 8 * block + 8, a_rows : a_rows + 16, :]
        records = records.reshape(HALF_LANES, HALF_LANES)
        mine = exact(records, table("repeat"), plain) == me
        ones = jnp.where(mine, 1.0, 0.0).astype(jnp.bfloat16)
        counts = exact(ones, table("within"), plain)
        within, loads = counts[:, :HALF_LANES], counts[:, HALF_LANES:]
        base = exact(table("below"), loads.astype(jnp.bfloat16), plain) + before
        slots = jnp.where(mine, within + base, -1.0)
        row_loads = exact(table("count"), ones, turned)
        row_base = exact(row_loads.astype(jnp.bfloat16), table("above"), plain)[:1] + before
        holds = (slot >= row_base) & (slot < row_base + row_loads[:1])
        local = lax.broadcasted_iota(jnp.int32, (HALF_LANES, HALF_LANES), 0) % 16
        mesh_row = (local + 8 * block // n_col * node_rows).astype(jnp.float32)
        found = found + exact(
            jnp.where(holds, 1.0, 0.0).astype(jnp.bfloat16),
            jnp.concatenate(
                [records, slots.astype(jnp.bfloat16), mesh_row.astype(jnp.bfloat16)], axis=1
            ),
            plain,
        )
        before = before + jnp.sum(loads, axis=0, keepdims=True)

    same = found[:, HALF_LANES : 2 * HALF_LANES] == slot
    taken = jnp.concatenate(
        [jnp.where(same, found[:, :HALF_LANES], 0.0), found[:, 2 * HALF_LANES :]], axis=1
    ).astype(jnp.bfloat16)
    columns_ref[...] = exact(taken, table("fields"), plain)
    rows = exact(table("turned"), taken, turned)
    rows_ref[...] = rows

    def field(index):
        return rows[index : index + 1, :]

    def divide(value, by):
        whole = jnp.floor((value + 0.5) * (1.0 / by))
        return whole, value - whole * by

    half = float(PATCH // 2)
    b_top = jnp.maximum(16.0 * field(ROW_HIGH) + field(ROW_LOW) - half, 0.0)
    b_left = jnp.maximum(16.0 * field(COL_HIGH) + field(COL_LOW) - half, 0.0)
    a_top = STRIDE * field(MESH_ROW) + STRIDE // 2
    a_left = STRIDE * field(MESH_COL) + (STRIDE // 2 + half)
    b_group, b_row_rest = divide(b_top, 16)
    b_block, b_col_rest = divide(b_left, PATCH)
    a_group, a_row_rest = divide(a_top, 16)
    a_block, a_col_rest = divide(a_left, PATCH)
    near_row = field(PEAK_ROW) + b_row_rest - a_row_rest + (ABOVE - centre_reach)
    near_col = divide(field(PEAK_COL) + b_col_rest - a_col_rest, PATCH)[1]
    for index, value in (
        (B_BLOCK, b_block),
        (B_ROW, 16.0 * b_group),
        (B_ROW_REST, b_row_rest),
        (B_COL_REST, b_col_rest),
        (A_BLOCK, a_block),
        (A_ROW, 16.0 * a_group),
        (A_ROW_REST, a_row_rest),
        (A_COL_REST, a_col_rest),
        (NEAR_ROW, near_row),
        (NEAR_COL, near_col),
    ):
        listed_ref[index : index + 1, :] = value.astype(jnp.int32)
    listed_ref[FIELDS:, :] = jnp.zeros((16 - FIELDS, capacity), jnp.int32)
    return jnp.max(before).astype(jnp.int32)


def cut_kernel(tile_ref, out_ref):
    strip = tile_ref[...]
    for block in range(out_ref.shape[0]):
        out_ref[block] = cut(strip, block * PATCH)


def cut_tile(tile):
    rows, cols = tile.shape
    blocks = -(-cols // PATCH)
    return pl.pallas_call(
        cut_kernel,
        grid=(rows // HALF_LANES,),
        out_shape=jax.ShapeDtypeStruct((blocks, rows + 16, WIDE), jnp.bfloat16),
        in_specs=[pl.BlockSpec((HALF_LANES, cols), lambda step: (step, 0))],
        out_specs=pl.BlockSpec((blocks, HALF_LANES, WIDE), lambda step: (0, step, 0)),
        cost_estimate=pl.CostEstimate(
            flops=0, bytes_accessed=2 * rows * (cols + blocks * WIDE), transcendentals=0
        ),
    )(tile)


def correlate(capacity, everyone, blocks, grid):
    n_row, n_col, a_rows, node_rows = grid
    tables, places = all_tables()
    a_blocks = (n_col * everyone.shape[2] + 76) // PATCH + 2
    vmem = pl.BlockSpec(memory_space=pltpu.VMEM)
    rows = pltpu.VMEM((capacity, HALF_LANES), jnp.float32)
    return pl.pallas_call(
        functools.partial(correlate_kernel, capacity, grid, places),
        out_shape=jax.ShapeDtypeStruct(
            (n_row * n_col, SPREAD_ROWS // 2, HALF_LANES), jnp.float32
        ),
        in_specs=[vmem, pl.BlockSpec(memory_space=pl.ANY), vmem],
        out_specs=vmem,
        scratch_shapes=[
            pltpu.VMEM((2 * BATCH * PATCH, WIDE), jnp.bfloat16),
            pltpu.VMEM((BATCH // TRIO, 2, 2, PATCH, WIDE), jnp.bfloat16),
            pltpu.VMEM((BATCH // TRIO * 2, PAIRED, WIDE), jnp.bfloat16),
            pltpu.VMEM((BATCH * PATCH, WIDE), jnp.bfloat16),
            pltpu.VMEM((BATCH, ABOVE + BELOW, HALF_LANES), jnp.float32),
            pltpu.VMEM((BATCH, ABOVE + BELOW, HALF_LANES), jnp.float32),
            pltpu.VMEM((BATCH // TRIO, 2, 2, 8, HALF_LANES), jnp.float32),
        ]
        + [rows] * 4
        + [
            pltpu.VMEM((a_blocks, n_row * a_rows + PATCH, WIDE), jnp.bfloat16),
            pltpu.VMEM(blocks.shape, jnp.bfloat16),
            rows,
            pltpu.VMEM((16, capacity), jnp.int32),
            pltpu.SMEM((16, capacity), jnp.int32),
            pltpu.SemaphoreType.DMA((2,)),
            pltpu.VMEM((2 * CAP_ROWS, HALF_LANES), jnp.float32),
            pltpu.VMEM((16, capacity), jnp.float32),
            pltpu.VMEM((TRIO, 2, 8, HALF_LANES), jnp.float32),
        ],
        compiler_params=pltpu.CompilerParams(vmem_limit_bytes=61 * 1024 * 1024),
    )(everyone, blocks, tables)


def per_device(a_window, b_section, owners, pos_rows, pos_cols, peaks):
    node_rows, node_cols = pos_rows.shape
    nodes = node_rows * node_cols
    n_row, n_col = lax.axis_size("row"), lax.axis_size("col")
    devices = n_row * n_col
    me_row, me_col = lax.axis_index("row"), lax.axis_index("col")
    share = max(2, (nodes * 8 // 5 + devices - 1) // devices)
    a_rows, a_cols = a_window.shape
    height, breadth = n_row * node_rows, n_col * node_cols

    mesh_col = me_col * node_cols + lax.broadcasted_iota(jnp.int32, pos_rows.shape, 1)
    records = jnp.concatenate(
        [
            owners.reshape(node_rows, node_cols),
            pos_rows // 16,
            pos_rows % 16,
            pos_cols // 16,
            pos_cols % 16,
            peaks[0],
            peaks[1],
            mesh_col,
        ],
        axis=1,
    ).astype(jnp.bfloat16)
    records = jnp.pad(records, ((0, 16 - node_rows), (0, 0)), constant_values=-1)
    sent = jnp.concatenate([a_window, records], axis=0)
    sent = jnp.broadcast_to(sent[None], (n_col,) + sent.shape)
    sent = lax.all_to_all(sent, "col", split_axis=0, concat_axis=0, tiled=True)
    everyone = lax.all_gather(sent, "row").reshape(devices, a_rows + 16, a_cols)

    grid = (n_row, n_col, a_rows, node_rows)
    spread = correlate(share * devices, everyone, cut_tile(b_section), grid)
    spread = lax.all_to_all(spread, ("row", "col"), split_axis=0, concat_axis=0, tiled=True)
    tall, broad = node_rows + 2 * RELAX, node_cols + 2 * RELAX
    spread = jnp.sum(spread, axis=0)
    half_lanes = HALF_LANES // 2
    spread = jnp.concatenate([spread[:, :half_lanes], spread[:, half_lanes:]], axis=0)[:tall]
    spread = [spread[:, SPREAD_LANES * value :][:, :broad] for value in range(3)]
    runner = spread[2][RELAX:-RELAX, RELAX:-RELAX]
    field = jnp.stack(spread[:2])
    for step in range(RELAX):
        reach = RELAX - 1 - step
        centre = field[:, 1:-1, 1:-1]
        around = (
            field[:, 2:, 1:-1] + field[:, :-2, 1:-1] + field[:, 1:-1, 2:] + field[:, 1:-1, :-2]
        )
        field = centre + stiffness * (around - 4.0 * centre)
        rows = me_row * node_rows - reach + jnp.arange(node_rows + 2 * reach)
        cols = me_col * node_cols - reach + jnp.arange(node_cols + 2 * reach)
        inside = ((rows >= 0) & (rows < height))[:, None] & ((cols >= 0) & (cols < breadth))[None]
        field = jnp.where(inside[None], field, 0.0)
    return (field, runner)


def solution(mesh):
    placed = (
        P("row", "col"),
        P("row", "col"),
        P("row", "col", None, None, None),
        P("row", "col"),
        P("row", "col"),
        P(None, "row", "col"),
    )
    return jax.shard_map(
        per_device,
        mesh=mesh,
        in_specs=placed,
        out_specs=(P(None, "row", "col"), P("row", "col")),
        check_vma=False,
    )
```

```python
import functools
import math

import jax
import jax.numpy as jnp
import numpy as np
from jax import lax
from jax.experimental import pallas as pl
from jax.experimental.pallas import tpu as pltpu
from jax.sharding import PartitionSpec as P

PATCH = 160
NODE_LANES = 16
SPREAD_LANES = 20
SPREAD_ROWS = 16
STRIDE = 8
RELAX = 2
WIDE = 256
HALF_LANES = 128
FREQS = PATCH // 2 + 1
GROUPS = 10
PAIRED = 16 * GROUPS
BIG = 3.0e38

sharpness = 80.0
epsilon = 1e-06
stiffness = 0.24
centre_reach = 2


def dft_tables():
    steps = np.arange(PATCH)
    angles = 2.0 * math.pi * ((steps[:, None] * steps[None, :FREQS]) % PATCH) / PATCH
    return (
        np.cos(angles).astype(jnp.bfloat16).astype(np.float32),
        np.sin(angles).astype(jnp.bfloat16).astype(np.float32),
    )


def kernel_tables():
    cosine, sine = dft_tables()
    weights = np.full((FREQS,), 2.0, np.float32)
    weights[0] = weights[-1] = 1.0
    across = np.zeros((WIDE, WIDE), np.float32)
    across[:PATCH, :FREQS] = cosine
    across[:PATCH, HALF_LANES : HALF_LANES + FREQS] = sine
    back_across = np.zeros((WIDE, WIDE), np.float32)
    back_across[:FREQS, :PATCH] = 0.5 * (cosine * weights).T
    back_across[HALF_LANES : HALF_LANES + FREQS, :PATCH] = 0.5 * (sine * weights).T
    down = np.zeros((PAIRED, PATCH), np.float32)
    back_down = np.zeros((PATCH, PAIRED), np.float32)
    for freq in range(FREQS - 1):
        row = 16 * (freq // 8) + freq % 8
        down[row] = cosine[:, freq]
        down[row + 8] = sine[:, freq] if freq else cosine[:, -1]
        back_down[:, row] = cosine[:, freq] * weights[freq]
        back_down[:, row + 8] = sine[:, freq] * weights[freq] if freq else cosine[:, -1]
    halves = [slice(0, HALF_LANES), slice(HALF_LANES, WIDE)]
    turns = (0, SECOND, THIRD)
    across = [
        np.concatenate([np.roll(across[:, half], turn, axis=1) for half in halves], axis=1)
        for turn in turns
    ]
    back_across = [
        np.concatenate([np.roll(back_across[half], turn, axis=0) for half in halves])
        for turn in turns
    ]
    return *across, *back_across, down, back_down


def listing_tables():
    lane = np.arange(HALF_LANES)
    group, place = lane // NODE_LANES, lane % NODE_LANES
    repeat = (lane[:, None] < NODE_LANES) & (place[None] == lane[:, None])
    earlier = (group[:, None] == group[None]) & (place[:, None] < place[None])
    first = np.broadcast_to(lane[:, None] < NODE_LANES, (HALF_LANES, HALF_LANES))
    below = lane[None] < lane[:, None]
    fields = np.zeros((2 * HALF_LANES, HALF_LANES), np.float32)
    fields[lane, group] = 1.0
    fields[HALF_LANES, MESH_ROW] = 1.0
    return repeat, np.concatenate([earlier, first], axis=1), below, below.T, first.T[:16], fields, (
        fields.T[:16]
    )


def all_tables():
    names = tuple(f"across{place}" for place in range(TRIO))
    names += tuple(f"back_across{place}" for place in range(TRIO))
    names += ("down", "back_down", "repeat", "within", "below", "above", "count", "fields", "turned")
    places, parts, start = {}, [], 0
    for name, part in zip(names, kernel_tables() + listing_tables()):
        rows, lanes = part.shape
        places[name] = (start, rows, lanes)
        rows_up = -(-rows // 16) * 16
        parts.append(np.zeros((rows_up, WIDE), np.float32))
        parts[-1][:rows, :lanes] = part
        start += rows_up
    return jnp.asarray(np.concatenate(parts), jnp.bfloat16), places


OWNER, ROW_HIGH, ROW_LOW, COL_HIGH, COL_LOW, PEAK_ROW, PEAK_COL, MESH_COL, MESH_ROW = range(9)
B_BLOCK, B_ROW, B_ROW_REST, B_COL_REST = 0, 1, 2, 3
A_BLOCK, A_ROW, A_ROW_REST, A_COL_REST = 4, 5, 6, 7
NEAR_ROW, NEAR_COL = 8, 9
FIELDS = 10
BATCH = 6
TRIO = 3
ABOVE = 24
BELOW = 32
CAP_ROWS = 64
SECOND = FREQS
THIRD = 2 * FREQS - HALF_LANES


def cut(strip, start):
    if start >= strip.shape[1]:
        return jnp.zeros((strip.shape[0], WIDE), strip.dtype)
    piece = strip[:, start : min(start + PATCH, strip.shape[1])]
    gap = jnp.zeros((strip.shape[0], WIDE - piece.shape[1]), strip.dtype)
    return jnp.concatenate([piece, gap], axis=1)


def correlate_kernel(
    capacity,
    grid,
    places,
    everyone_ref,
    blocks_ref,
    tables_ref,
    out_ref,
    *scratch,
):
    patches, halves, crosses, inverses = scratch[:4]
    corrs = scratch[4:6]
    energies, totals, row_moments, col_moments, runners, a_ref, b_ref = scratch[6:13]
    columns_ref, listed_ref, items_ref, semaphores, caps_ref, rows_ref, shares_ref = scratch[13:]
    to_blocks = pltpu.make_async_copy(blocks_ref, b_ref, semaphores.at[0])
    to_blocks.start()

    def table(name):
        start, rows, lanes = places[name]
        return tables_ref[start : start + rows, :lanes]

    n_row, n_col, a_rows, node_rows = grid
    count = list_nodes(
        capacity,
        grid,
        everyone_ref,
        table,
        columns_ref,
        rows_ref,
        listed_ref,
    )
    for place in range(TRIO):
        for tile in range(2):
            freq = lax.broadcasted_iota(jnp.int32, (8, HALF_LANES), 1)
            freq = freq + (tile * HALF_LANES - place * FREQS)
            once = (freq == 0) | (freq == FREQS - 1)
            twice = (freq > 0) & (freq < FREQS - 1)
            shares_ref[place, tile] = jnp.where(twice, 4.0, jnp.where(once, 2.0, 0.0))
    caps_row = lax.broadcasted_iota(jnp.int32, caps_ref.shape, 0) - CAP_ROWS
    caps_ref[...] = jnp.where((caps_row >= 0) & (caps_row <= 2 * centre_reach), -BIG, BIG)
    to_scalars = pltpu.make_async_copy(listed_ref, items_ref, semaphores.at[1])
    to_scalars.start()

    a_ref[0] = jnp.zeros(a_ref.shape[1:], jnp.bfloat16)
    rim = jnp.zeros((a_ref.shape[0], PATCH // 2, WIDE), jnp.bfloat16)
    a_ref[:, : PATCH // 2, :] = rim
    a_ref[:, a_ref.shape[1] - PATCH // 2 :, :] = rim

    for row in range(n_row):
        strip = jnp.concatenate(
            [everyone_ref[row * n_col + col, :a_rows, :] for col in range(n_col)], axis=1
        )
        start = PATCH // 2 + row * a_rows
        for block in range(1, a_ref.shape[0]):
            a_ref[block, start : start + a_rows, :] = cut(strip, (block - 1) * PATCH)

    def at(step, stage, part):
        return jnp.clip(BATCH * (step - stage) + part, 0, capacity - 1)

    def extract(source, block, row, row_rest, col_rest, base):
        lanes = lax.broadcasted_iota(jnp.int32, (16, WIDE), 1) >= col_rest
        rows = lax.broadcasted_iota(jnp.int32, (16, WIDE), 0) >= row_rest

        def group(place):
            here = pl.ds(pl.multiple_of(row + 16 * place, 16), 16)
            return jnp.where(lanes, source[block, here, :], source[block + 1, here, :])

        groups = [group(place) for place in range(PATCH // 16 + 1)]
        groups[0] = jnp.where(rows, groups[0], groups.pop())
        for place, values in enumerate(groups):
            patches[base + 16 * place : base + 16 * place + 16, :] = values

    trios = BATCH // TRIO

    def patch_base(part, which):
        trio, place = divmod(part, TRIO)
        return ((trios * place + trio) * 2 + which) * PATCH

    def stage_half(step):
        for part in range(BATCH):
            item = at(step, 0, part)
            for which, source, fields in (
                (0, a_ref, (A_BLOCK, A_ROW, A_ROW_REST, A_COL_REST)),
                (1, b_ref, (B_BLOCK, B_ROW, B_ROW_REST, B_COL_REST)),
            ):
                block, row, row_rest, col_rest = (items_ref[field, item] for field in fields)
                extract(source, block, row, row_rest, col_rest, patch_base(part, which))
        rows = 2 * trios * PATCH
        turned = [
            jnp.dot(
                patches[rows * place : rows * (place + 1), :],
                table(f"across{place}"),
                preferred_element_type=jnp.float32,
            )
            for place in range(TRIO)
        ]
        lanes = lax.broadcasted_iota(jnp.int32, (PATCH, HALF_LANES), 1)
        for trio in range(BATCH // TRIO):
            for which in range(2):
                for side in (slice(0, HALF_LANES), slice(HALF_LANES, WIDE)):
                    base = (2 * trio + which) * PATCH
                    first, second, third = (half[base : base + PATCH, side] for half in turned)
                    halves[trio, which, 0, :, side] = jnp.where(
                        lanes < SECOND, first, second
                    ).astype(jnp.bfloat16)
                    halves[trio, which, 1, :, side] = jnp.where(
                        lanes < THIRD, second, third
                    ).astype(jnp.bfloat16)

    def sides(spec, group):
        cc = spec[16 * group : 16 * group + 8, :HALF_LANES]
        cs = spec[16 * group : 16 * group + 8, HALF_LANES:]
        sc = spec[16 * group + 8 : 16 * group + 16, :HALF_LANES]
        ss = spec[16 * group + 8 : 16 * group + 16, HALF_LANES:]
        power = (cc * cc + cs * cs) + (sc * sc + ss * ss)
        return (cc - ss, sc + cs, cc + ss, sc - cs, power), (cc, cs, sc, ss)

    def stage_inverse():
        down = table("down")
        top = lax.broadcasted_iota(jnp.int32, (8, HALF_LANES), 0) == 0
        for pair in range(2 * (BATCH // TRIO)):
            trio, tile = divmod(pair, 2)
            spec_a = jnp.dot(down, halves[trio, 0, tile], preferred_element_type=jnp.float32)
            spec_b = jnp.dot(down, halves[trio, 1, tile], preferred_element_type=jnp.float32)
            for group in range(GROUPS):
                (a_pr, a_pi, a_mr, a_mi, a_power), a_plain = sides(spec_a, group)
                (b_pr, b_pi, b_mr, b_mi, b_power), b_plain = sides(spec_b, group)
                if group == 0:
                    powers = [jnp.where(top, 0.5 * power, power) for power in (a_power, b_power)]
                else:
                    powers = [powers[0] + a_power, powers[1] + b_power]
                pr = a_pr * b_pr + a_pi * b_pi
                pi = a_pr * b_pi - a_pi * b_pr
                mr = a_mr * b_mr + a_mi * b_mi
                mi = a_mr * b_mi - a_mi * b_mr
                outs = [pr + mr, pi - mi, pi + mi, mr - pr]
                if group == 0:
                    for half in (0, 2):
                        (ar, ai), (br, bi) = a_plain[half : half + 2], b_plain[half : half + 2]
                        outs[half] = jnp.where(top, 2.0 * (ar * br + ai * bi), outs[half])
                        outs[half + 1] = jnp.where(top, 2.0 * (ar * bi - ai * br), outs[half + 1])
                upper = jnp.concatenate(outs[:2], axis=1)
                lower = jnp.concatenate(outs[2:], axis=1)
                crosses[pair, 16 * group : 16 * group + 16, :] = jnp.concatenate(
                    [upper, lower], axis=0
                ).astype(jnp.bfloat16)
            energies[trio, 0, tile] = powers[0]
            energies[trio, 1, tile] = powers[1]
        lanes = lax.broadcasted_iota(jnp.int32, (PATCH, HALF_LANES), 1)
        for trio in range(BATCH // TRIO):
            low, high = (
                jnp.dot(
                    table("back_down"), crosses[2 * trio + tile], preferred_element_type=jnp.float32
                )
                for tile in range(2)
            )
            for side in (slice(0, HALF_LANES), slice(HALF_LANES, WIDE)):
                first = low[:, side]
                second = jnp.where(lanes >= SECOND, first, high[:, side])
                third = high[:, side]
                for place, inverse in enumerate((first, second, third)):
                    base = (trios * place + trio) * PATCH
                    inverses[base : base + PATCH, side] = inverse.astype(jnp.bfloat16)

    def stage_score(step):
        corr_all = [
            jnp.dot(
                inverses[trios * PATCH * place : trios * PATCH * (place + 1), :],
                table(f"back_across{place}"),
                preferred_element_type=jnp.float32,
            )
            for place in range(TRIO)
        ]
        rows = lax.broadcasted_iota(jnp.int32, (8, HALF_LANES), 0)
        lanes = lax.broadcasted_iota(jnp.int32, (8, HALF_LANES), 1)
        shift_rows = (rows - centre_reach).astype(jnp.float32)
        row_near = rows <= 2 * centre_reach
        for part in range(BATCH):
            item = at(step, 2, part)
            near_row = items_ref[NEAR_ROW, item]
            near_col = items_ref[NEAR_COL, item]
            trio, place = divmod(part, TRIO)
            mean_a, mean_b = (
                jnp.sum(
                    energies[trio, which, 0] * shares_ref[place, 0]
                    + energies[trio, which, 1] * shares_ref[place, 1],
                    keepdims=True,
                )
                * (1.0 / float(PATCH**4))
                for which in range(2)
            )
            scale = 1.0 / (
                float(PATCH**4) * jnp.sqrt(mean_a + epsilon) * jnp.sqrt(mean_b + epsilon)
            )
            caps = caps_ref[pl.ds(CAP_ROWS - near_row, ABOVE + BELOW), :]
            total, row_moment, col_moment = 0.0, 0.0, 0.0
            best = None
            for half in range(2):
                corr = corr_all[part % TRIO][
                    PATCH * (part // TRIO) : PATCH * (part // TRIO + 1),
                    half * HALF_LANES : (half + 1) * HALF_LANES,
                ]
                edge = jnp.concatenate([corr[PATCH - ABOVE :], corr[:BELOW]], axis=0)
                corrs[half][part] = edge
                far = jnp.maximum(
                    jnp.max(jnp.minimum(edge, caps).reshape(-1, 8, HALF_LANES), axis=0),
                    jnp.max(corr[BELOW : PATCH - ABOVE].reshape(-1, 8, HALF_LANES), axis=0),
                )
                if half == 0:
                    best = far
                else:
                    far = jnp.where(lanes < PATCH - HALF_LANES, far, -BIG)
                    best = jnp.maximum(best, far)
            for half in range(2):
                values = corrs[half][part, pl.ds(near_row, 8), :]
                place = lanes + half * HALF_LANES
                shift = place - near_col
                shift = jnp.where(shift >= PATCH // 2, shift - PATCH, shift)
                shift = jnp.where(shift < -(PATCH // 2), shift + PATCH, shift)
                inside = row_near & (place < PATCH)
                close = jnp.abs(shift) <= centre_reach
                weight = jnp.where(
                    inside & close, jnp.exp(sharpness * (values * scale)), 0.0
                )
                total = total + weight
                row_moment = row_moment + weight * shift_rows
                col_moment = col_moment + weight * shift.astype(jnp.float32)
                best = jnp.maximum(
                    best, jnp.where(inside & jnp.logical_not(close), values, -BIG)
                )
            totals[pl.ds(item, 1), :] = jnp.sum(total, axis=0, keepdims=True)
            row_moments[pl.ds(item, 1), :] = jnp.sum(row_moment, axis=0, keepdims=True)
            col_moments[pl.ds(item, 1), :] = jnp.sum(col_moment, axis=0, keepdims=True)
            runners[pl.ds(item, 1), :] = jnp.max(best * scale, axis=0, keepdims=True)

    to_scalars.wait()
    to_blocks.wait()

    steps = jnp.maximum((count + BATCH - 1) // BATCH, 2)
    stage_half(0)
    stage_inverse()
    stage_half(1)

    @pl.loop(2, steps)
    def _(step):
        stage_score(step)
        stage_inverse()
        stage_half(step)

    stage_score(steps)
    stage_inverse()
    stage_score(steps + 1)

    used = lax.broadcasted_iota(jnp.int32, (capacity, 1), 0) < count
    total = jnp.sum(totals[...], axis=1, keepdims=True)
    peak_row = columns_ref[:, PEAK_ROW : PEAK_ROW + 1]
    peak_col = columns_ref[:, PEAK_COL : PEAK_COL + 1]
    results = (
        peak_row + jnp.sum(row_moments[...], axis=1, keepdims=True) / total,
        peak_col + jnp.sum(col_moments[...], axis=1, keepdims=True) / total,
        jnp.maximum(jnp.max(runners[...], axis=1, keepdims=True), -2.0),
    )
    lanes = lax.broadcasted_iota(jnp.int32, (capacity, HALF_LANES), 1)
    terms = [jnp.zeros((capacity, HALF_LANES), jnp.float32)] * 3
    for value, rest in enumerate(results):
        rest = jnp.where(used, rest, 0.0)
        for term in range(3):
            here = rest.astype(jnp.bfloat16).astype(jnp.float32)
            terms[term] = jnp.where(lanes // SPREAD_LANES == value, here, terms[term])
            rest = rest - here
    slot_row = rows_ref[MESH_ROW : MESH_ROW + 1, :]
    slot_col = columns_ref[:, MESH_COL : MESH_COL + 1]
    offset = (lanes % SPREAD_LANES - RELAX).astype(jnp.float32)
    shape = (n_row * SPREAD_ROWS, capacity)
    place = lax.broadcasted_iota(jnp.int32, shape, 0)
    row = place // SPREAD_ROWS * node_rows + place % SPREAD_ROWS - RELAX
    rows_picked = jnp.where(slot_row == row.astype(jnp.float32), 1.0, 0.0).astype(jnp.bfloat16)
    for col in range(n_col):
        here = slot_col == offset + float(col * NODE_LANES)
        sent = sum(
            jnp.dot(
                rows_picked,
                jnp.where(here, term, 0.0).astype(jnp.bfloat16),
                preferred_element_type=jnp.float32,
            )
            for term in terms
        )
        for row in range(n_row):
            block = sent[SPREAD_ROWS * row : SPREAD_ROWS * (row + 1)]
            turned = pltpu.roll(block[8:], HALF_LANES // 2, axis=1)
            out_ref[row * n_col + col] = jnp.where(
                lanes[:8] < HALF_LANES // 2, block[:8], turned
            )


def list_nodes(
    capacity,
    grid,
    everyone_ref,
    table,
    columns_ref,
    rows_ref,
    listed_ref,
):
    n_row, n_col, a_rows, node_rows = grid
    me = (lax.axis_index("row") * n_col + lax.axis_index("col")).astype(jnp.float32)
    exact = functools.partial(lax.dot_general, preferred_element_type=jnp.float32)
    plain = (((1,), (0,)), ((), ()))
    turned = (((1,), (1,)), ((), ()))

    slot = lax.broadcasted_iota(jnp.int32, (capacity, HALF_LANES), 0).astype(jnp.float32)
    before = jnp.zeros((1, HALF_LANES), jnp.float32)
    found = jnp.zeros((capacity, 3 * HALF_LANES), jnp.float32)
    for block in range(n_row * n_col // 8):
        records = everyone_ref[8 * block : 8 * block + 8, a_rows : a_rows + 16, :]
        records = records.reshape(HALF_LANES, HALF_LANES)
        mine = exact(records, table("repeat"), plain) == me
        ones = jnp.where(mine, 1.0, 0.0).astype(jnp.bfloat16)
        counts = exact(ones, table("within"), plain)
        within, loads = counts[:, :HALF_LANES], counts[:, HALF_LANES:]
        base = exact(table("below"), loads.astype(jnp.bfloat16), plain) + before
        slots = jnp.where(mine, within + base, -1.0)
        row_loads = exact(table("count"), ones, turned)
        row_base = exact(row_loads.astype(jnp.bfloat16), table("above"), plain)[:1] + before
        holds = (slot >= row_base) & (slot < row_base + row_loads[:1])
        local = lax.broadcasted_iota(jnp.int32, (HALF_LANES, HALF_LANES), 0) % 16
        mesh_row = (local + 8 * block // n_col * node_rows).astype(jnp.float32)
        found = found + exact(
            jnp.where(holds, 1.0, 0.0).astype(jnp.bfloat16),
            jnp.concatenate(
                [records, slots.astype(jnp.bfloat16), mesh_row.astype(jnp.bfloat16)], axis=1
            ),
            plain,
        )
        before = before + jnp.sum(loads, axis=0, keepdims=True)

    same = found[:, HALF_LANES : 2 * HALF_LANES] == slot
    taken = jnp.concatenate(
        [jnp.where(same, found[:, :HALF_LANES], 0.0), found[:, 2 * HALF_LANES :]], axis=1
    ).astype(jnp.bfloat16)
    columns_ref[...] = exact(taken, table("fields"), plain)
    rows = exact(table("turned"), taken, turned)
    rows_ref[...] = rows

    def field(index):
        return rows[index : index + 1, :]

    def divide(value, by):
        whole = jnp.floor((value + 0.5) * (1.0 / by))
        return whole, value - whole * by

    half = float(PATCH // 2)
    b_top = jnp.maximum(16.0 * field(ROW_HIGH) + field(ROW_LOW) - half, 0.0)
    b_left = jnp.maximum(16.0 * field(COL_HIGH) + field(COL_LOW) - half, 0.0)
    a_top = STRIDE * field(MESH_ROW) + STRIDE // 2
    a_left = STRIDE * field(MESH_COL) + (STRIDE // 2 + half)
    b_group, b_row_rest = divide(b_top, 16)
    b_block, b_col_rest = divide(b_left, PATCH)
    a_group, a_row_rest = divide(a_top, 16)
    a_block, a_col_rest = divide(a_left, PATCH)
    near_row = field(PEAK_ROW) + b_row_rest - a_row_rest + (ABOVE - centre_reach)
    near_col = divide(field(PEAK_COL) + b_col_rest - a_col_rest, PATCH)[1]
    for index, value in (
        (B_BLOCK, b_block),
        (B_ROW, 16.0 * b_group),
        (B_ROW_REST, b_row_rest),
        (B_COL_REST, b_col_rest),
        (A_BLOCK, a_block),
        (A_ROW, 16.0 * a_group),
        (A_ROW_REST, a_row_rest),
        (A_COL_REST, a_col_rest),
        (NEAR_ROW, near_row),
        (NEAR_COL, near_col),
    ):
        listed_ref[index : index + 1, :] = value.astype(jnp.int32)
    listed_ref[FIELDS:, :] = jnp.zeros((16 - FIELDS, capacity), jnp.int32)
    return jnp.max(before).astype(jnp.int32)


def cut_kernel(tile_ref, out_ref):
    strip = tile_ref[...]
    for block in range(out_ref.shape[0]):
        out_ref[block] = cut(strip, block * PATCH)


def cut_tile(tile):
    rows, cols = tile.shape
    blocks = -(-cols // PATCH)
    return pl.pallas_call(
        cut_kernel,
        grid=(rows // HALF_LANES,),
        out_shape=jax.ShapeDtypeStruct((blocks, rows + 16, WIDE), jnp.bfloat16),
        in_specs=[pl.BlockSpec((HALF_LANES, cols), lambda step: (step, 0))],
        out_specs=pl.BlockSpec((blocks, HALF_LANES, WIDE), lambda step: (0, step, 0)),
        cost_estimate=pl.CostEstimate(
            flops=0, bytes_accessed=2 * rows * (cols + blocks * WIDE), transcendentals=0
        ),
    )(tile)


def correlate(capacity, everyone, blocks, grid):
    n_row, n_col, a_rows, node_rows = grid
    tables, places = all_tables()
    a_blocks = (n_col * everyone.shape[2] + 76) // PATCH + 2
    vmem = pl.BlockSpec(memory_space=pltpu.VMEM)
    rows = pltpu.VMEM((capacity, HALF_LANES), jnp.float32)
    return pl.pallas_call(
        functools.partial(correlate_kernel, capacity, grid, places),
        out_shape=jax.ShapeDtypeStruct(
            (n_row * n_col, SPREAD_ROWS // 2, HALF_LANES), jnp.float32
        ),
        in_specs=[vmem, pl.BlockSpec(memory_space=pl.ANY), vmem],
        out_specs=vmem,
        scratch_shapes=[
            pltpu.VMEM((2 * BATCH * PATCH, WIDE), jnp.bfloat16),
            pltpu.VMEM((BATCH // TRIO, 2, 2, PATCH, WIDE), jnp.bfloat16),
            pltpu.VMEM((BATCH // TRIO * 2, PAIRED, WIDE), jnp.bfloat16),
            pltpu.VMEM((BATCH * PATCH, WIDE), jnp.bfloat16),
            pltpu.VMEM((BATCH, ABOVE + BELOW, HALF_LANES), jnp.float32),
            pltpu.VMEM((BATCH, ABOVE + BELOW, HALF_LANES), jnp.float32),
            pltpu.VMEM((BATCH // TRIO, 2, 2, 8, HALF_LANES), jnp.float32),
        ]
        + [rows] * 4
        + [
            pltpu.VMEM((a_blocks, n_row * a_rows + PATCH, WIDE), jnp.bfloat16),
            pltpu.VMEM(blocks.shape, jnp.bfloat16),
            rows,
            pltpu.VMEM((16, capacity), jnp.int32),
            pltpu.SMEM((16, capacity), jnp.int32),
            pltpu.SemaphoreType.DMA((2,)),
            pltpu.VMEM((2 * CAP_ROWS, HALF_LANES), jnp.float32),
            pltpu.VMEM((16, capacity), jnp.float32),
            pltpu.VMEM((TRIO, 2, 8, HALF_LANES), jnp.float32),
        ],
        compiler_params=pltpu.CompilerParams(vmem_limit_bytes=61 * 1024 * 1024),
    )(everyone, blocks, tables)


def per_device(a_window, b_section, owners, pos_rows, pos_cols, peaks):
    node_rows, node_cols = pos_rows.shape
    nodes = node_rows * node_cols
    n_row, n_col = lax.axis_size("row"), lax.axis_size("col")
    devices = n_row * n_col
    me_row, me_col = lax.axis_index("row"), lax.axis_index("col")
    share = max(2, (nodes * 8 // 5 + devices - 1) // devices)
    a_rows, a_cols = a_window.shape
    height, breadth = n_row * node_rows, n_col * node_cols

    mesh_col = me_col * node_cols + lax.broadcasted_iota(jnp.int32, pos_rows.shape, 1)
    records = jnp.concatenate(
        [
            owners.reshape(node_rows, node_cols),
            pos_rows // 16,
            pos_rows % 16,
            pos_cols // 16,
            pos_cols % 16,
            peaks[0],
            peaks[1],
            mesh_col,
        ],
        axis=1,
    ).astype(jnp.bfloat16)
    records = jnp.pad(records, ((0, 16 - node_rows), (0, 0)), constant_values=-1)
    sent = jnp.concatenate([a_window, records], axis=0)
    sent = jnp.broadcast_to(sent[None], (n_col,) + sent.shape)
    sent = lax.all_to_all(sent, "col", split_axis=0, concat_axis=0, tiled=True)
    everyone = lax.all_gather(sent, "row").reshape(devices, a_rows + 16, a_cols)

    grid = (n_row, n_col, a_rows, node_rows)
    spread = correlate(share * devices, everyone, cut_tile(b_section), grid)
    spread = lax.all_to_all(spread, ("row", "col"), split_axis=0, concat_axis=0, tiled=True)
    tall, broad = node_rows + 2 * RELAX, node_cols + 2 * RELAX
    spread = jnp.sum(spread, axis=0)
    half_lanes = HALF_LANES // 2
    spread = jnp.concatenate([spread[:, :half_lanes], spread[:, half_lanes:]], axis=0)[:tall]
    spread = [spread[:, SPREAD_LANES * value :][:, :broad] for value in range(3)]
    runner = spread[2][RELAX:-RELAX, RELAX:-RELAX]
    field = jnp.stack(spread[:2])
    for step in range(RELAX):
        reach = RELAX - 1 - step
        centre = field[:, 1:-1, 1:-1]
        around = (
            field[:, 2:, 1:-1] + field[:, :-2, 1:-1] + field[:, 1:-1, 2:] + field[:, 1:-1, :-2]
        )
        field = centre + stiffness * (around - 4.0 * centre)
        rows = me_row * node_rows - reach + jnp.arange(node_rows + 2 * reach)
        cols = me_col * node_cols - reach + jnp.arange(node_cols + 2 * reach)
        inside = ((rows >= 0) & (rows < height))[:, None] & ((cols >= 0) & (cols < breadth))[None]
        field = jnp.where(inside[None], field, 0.0)
    return (field, runner)


def solution(mesh):
    placed = (
        P("row", "col"),
        P("row", "col"),
        P("row", "col", None, None, None),
        P("row", "col"),
        P("row", "col"),
        P(None, "row", "col"),
    )
    return jax.shard_map(
        per_device,
        mesh=mesh,
        in_specs=placed,
        out_specs=(P(None, "row", "col"), P("row", "col")),
        check_vma=False,
    )
```

```python
import functools
import math

import jax
import jax.numpy as jnp
import numpy as np
from jax import lax
from jax.experimental import pallas as pl
from jax.experimental.pallas import tpu as pltpu
from jax.sharding import PartitionSpec as P

PATCH = 160
NODE_LANES = 16
SPREAD_LANES = 20
SPREAD_ROWS = 16
STRIDE = 8
RELAX = 2
WIDE = 256
HALF_LANES = 128
FREQS = PATCH // 2 + 1
GROUPS = 10
PAIRED = 16 * GROUPS
BIG = 3.0e38

sharpness = 80.0
epsilon = 1e-06
stiffness = 0.24
centre_reach = 2


def dft_tables():
    steps = np.arange(PATCH)
    angles = 2.0 * math.pi * ((steps[:, None] * steps[None, :FREQS]) % PATCH) / PATCH
    return (
        np.cos(angles).astype(jnp.bfloat16).astype(np.float32),
        np.sin(angles).astype(jnp.bfloat16).astype(np.float32),
    )


def kernel_tables():
    cosine, sine = dft_tables()
    weights = np.full((FREQS,), 2.0, np.float32)
    weights[0] = weights[-1] = 1.0
    across = np.zeros((WIDE, WIDE), np.float32)
    across[:PATCH, :FREQS] = cosine
    across[:PATCH, HALF_LANES : HALF_LANES + FREQS] = sine
    back_across = np.zeros((WIDE, WIDE), np.float32)
    back_across[:FREQS, :PATCH] = 0.5 * (cosine * weights).T
    back_across[HALF_LANES : HALF_LANES + FREQS, :PATCH] = 0.5 * (sine * weights).T
    down = np.zeros((PAIRED, PATCH), np.float32)
    back_down = np.zeros((PATCH, PAIRED), np.float32)
    for freq in range(FREQS - 1):
        row = 16 * (freq // 8) + freq % 8
        down[row] = cosine[:, freq]
        down[row + 8] = sine[:, freq] if freq else cosine[:, -1]
        back_down[:, row] = cosine[:, freq] * weights[freq]
        back_down[:, row + 8] = sine[:, freq] * weights[freq] if freq else cosine[:, -1]
    return across, down, back_down, back_across


def listing_tables():
    lane = np.arange(HALF_LANES)
    group, place = lane // NODE_LANES, lane % NODE_LANES
    repeat = (lane[:, None] < NODE_LANES) & (place[None] == lane[:, None])
    earlier = (group[:, None] == group[None]) & (place[:, None] < place[None])
    first = np.broadcast_to(lane[:, None] < NODE_LANES, (HALF_LANES, HALF_LANES))
    below = lane[None] < lane[:, None]
    fields = np.zeros((2 * HALF_LANES, HALF_LANES), np.float32)
    fields[lane, group] = 1.0
    fields[HALF_LANES, MESH_ROW] = 1.0
    return repeat, np.concatenate([earlier, first], axis=1), below, below.T, first.T[:16], fields, (
        fields.T[:16]
    )


def all_tables():
    names = ("across", "down", "back_down", "back_across", "repeat", "within")
    names += ("below", "above", "count", "fields", "turned")
    places, parts, start = {}, [], 0
    for name, part in zip(names, kernel_tables() + listing_tables()):
        rows, lanes = part.shape
        places[name] = (start, rows, lanes)
        rows_up = -(-rows // 16) * 16
        parts.append(np.zeros((rows_up, WIDE), np.float32))
        parts[-1][:rows, :lanes] = part
        start += rows_up
    return jnp.asarray(np.concatenate(parts), jnp.bfloat16), places


OWNER, ROW_HIGH, ROW_LOW, COL_HIGH, COL_LOW, PEAK_ROW, PEAK_COL, MESH_COL, MESH_ROW = range(9)
B_BLOCK, B_ROW, B_ROW_REST, B_COL_REST = 0, 1, 2, 3
A_BLOCK, A_ROW, A_ROW_REST, A_COL_REST = 4, 5, 6, 7
NEAR_ROW, NEAR_COL = 8, 9
FIELDS = 10
BATCH = 9
TRIO = 3
ABOVE = 24
BELOW = 32
CAP_ROWS = 64
SECOND = FREQS
THIRD = 2 * FREQS - HALF_LANES


def cut(strip, start):
    if start >= strip.shape[1]:
        return jnp.zeros((strip.shape[0], WIDE), strip.dtype)
    piece = strip[:, start : min(start + PATCH, strip.shape[1])]
    gap = jnp.zeros((strip.shape[0], WIDE - piece.shape[1]), strip.dtype)
    return jnp.concatenate([piece, gap], axis=1)


def correlate_kernel(
    capacity,
    grid,
    places,
    everyone_ref,
    blocks_ref,
    tables_ref,
    out_ref,
    *scratch,
):
    patches, halves, crosses, inverses = scratch[:4]
    corrs = scratch[4:6]
    energies, totals, row_moments, col_moments, runners, a_ref, b_ref = scratch[6:13]
    columns_ref, listed_ref, items_ref, semaphores, caps_ref, rows_ref, shares_ref = scratch[13:]
    to_blocks = pltpu.make_async_copy(blocks_ref, b_ref, semaphores.at[0])
    to_blocks.start()

    def table(name):
        start, rows, lanes = places[name]
        return tables_ref[start : start + rows, :lanes]

    n_row, n_col, a_rows, node_rows = grid
    count = list_nodes(
        capacity,
        grid,
        everyone_ref,
        table,
        columns_ref,
        rows_ref,
        listed_ref,
    )
    for place in range(TRIO):
        for tile in range(2):
            freq = lax.broadcasted_iota(jnp.int32, (8, HALF_LANES), 1)
            freq = freq + (tile * HALF_LANES - place * FREQS)
            once = (freq == 0) | (freq == FREQS - 1)
            twice = (freq > 0) & (freq < FREQS - 1)
            shares_ref[place, tile] = jnp.where(twice, 4.0, jnp.where(once, 2.0, 0.0))
    caps_row = lax.broadcasted_iota(jnp.int32, caps_ref.shape, 0) - CAP_ROWS
    caps_ref[...] = jnp.where((caps_row >= 0) & (caps_row <= 2 * centre_reach), -BIG, BIG)
    to_scalars = pltpu.make_async_copy(listed_ref, items_ref, semaphores.at[1])
    to_scalars.start()

    a_ref[0] = jnp.zeros(a_ref.shape[1:], jnp.bfloat16)
    rim = jnp.zeros((a_ref.shape[0], PATCH // 2, WIDE), jnp.bfloat16)
    a_ref[:, : PATCH // 2, :] = rim
    a_ref[:, a_ref.shape[1] - PATCH // 2 :, :] = rim

    for row in range(n_row):
        strip = jnp.concatenate(
            [everyone_ref[row * n_col + col, :a_rows, :] for col in range(n_col)], axis=1
        )
        start = PATCH // 2 + row * a_rows
        for block in range(1, a_ref.shape[0]):
            a_ref[block, start : start + a_rows, :] = cut(strip, (block - 1) * PATCH)

    def at(step, stage, part):
        return jnp.clip(BATCH * (step - stage) + part, 0, capacity - 1)

    def extract(source, block, row, row_rest, col_rest, base):
        lanes = lax.broadcasted_iota(jnp.int32, (16, WIDE), 1) >= col_rest
        rows = lax.broadcasted_iota(jnp.int32, (16, WIDE), 0) >= row_rest

        def group(place):
            here = pl.ds(pl.multiple_of(row + 16 * place, 16), 16)
            return jnp.where(lanes, source[block, here, :], source[block + 1, here, :])

        groups = [group(place) for place in range(PATCH // 16 + 1)]
        groups[0] = jnp.where(rows, groups[0], groups.pop())
        for place, values in enumerate(groups):
            patches[base + 16 * place : base + 16 * place + 16, :] = values

    def patch_base(part, which):
        trio, place = divmod(part, TRIO)
        return ((2 * trio + which) * TRIO + place) * PATCH

    def stage_half(step):
        for part in range(BATCH):
            item = at(step, 0, part)
            for which, source, fields in (
                (0, a_ref, (A_BLOCK, A_ROW, A_ROW_REST, A_COL_REST)),
                (1, b_ref, (B_BLOCK, B_ROW, B_ROW_REST, B_COL_REST)),
            ):
                block, row, row_rest, col_rest = (items_ref[field, item] for field in fields)
                extract(source, block, row, row_rest, col_rest, patch_base(part, which))
        half = jnp.dot(patches[...], table("across"), preferred_element_type=jnp.float32)
        lanes = lax.broadcasted_iota(jnp.int32, (PATCH, HALF_LANES), 1)
        for trio in range(BATCH // TRIO):
            for which in range(2):
                for side in (slice(0, HALF_LANES), slice(HALF_LANES, WIDE)):
                    first, second, third = (
                        half[base : base + PATCH, side]
                        for base in (patch_base(TRIO * trio + n, which) for n in range(TRIO))
                    )
                    second = pltpu.roll(second, SECOND, axis=1)
                    third = pltpu.roll(third, THIRD, axis=1)
                    halves[trio, which, 0, :, side] = jnp.where(
                        lanes < SECOND, first, second
                    ).astype(jnp.bfloat16)
                    halves[trio, which, 1, :, side] = jnp.where(
                        lanes < THIRD, second, third
                    ).astype(jnp.bfloat16)

    def sides(spec, group):
        cc = spec[16 * group : 16 * group + 8, :HALF_LANES]
        cs = spec[16 * group : 16 * group + 8, HALF_LANES:]
        sc = spec[16 * group + 8 : 16 * group + 16, :HALF_LANES]
        ss = spec[16 * group + 8 : 16 * group + 16, HALF_LANES:]
        power = (cc * cc + cs * cs) + (sc * sc + ss * ss)
        return (cc - ss, sc + cs, cc + ss, sc - cs, power), (cc, cs, sc, ss)

    def stage_inverse():
        down = table("down")
        top = lax.broadcasted_iota(jnp.int32, (8, HALF_LANES), 0) == 0
        for pair in range(2 * (BATCH // TRIO)):
            trio, tile = divmod(pair, 2)
            spec_a = jnp.dot(down, halves[trio, 0, tile], preferred_element_type=jnp.float32)
            spec_b = jnp.dot(down, halves[trio, 1, tile], preferred_element_type=jnp.float32)
            for group in range(GROUPS):
                (a_pr, a_pi, a_mr, a_mi, a_power), a_plain = sides(spec_a, group)
                (b_pr, b_pi, b_mr, b_mi, b_power), b_plain = sides(spec_b, group)
                if group == 0:
                    powers = [jnp.where(top, 0.5 * power, power) for power in (a_power, b_power)]
                else:
                    powers = [powers[0] + a_power, powers[1] + b_power]
                pr = a_pr * b_pr + a_pi * b_pi
                pi = a_pr * b_pi - a_pi * b_pr
                mr = a_mr * b_mr + a_mi * b_mi
                mi = a_mr * b_mi - a_mi * b_mr
                outs = [pr + mr, pi - mi, pi + mi, mr - pr]
                if group == 0:
                    for half in (0, 2):
                        (ar, ai), (br, bi) = a_plain[half : half + 2], b_plain[half : half + 2]
                        outs[half] = jnp.where(top, 2.0 * (ar * br + ai * bi), outs[half])
                        outs[half + 1] = jnp.where(top, 2.0 * (ar * bi - ai * br), outs[half + 1])
                upper = jnp.concatenate(outs[:2], axis=1)
                lower = jnp.concatenate(outs[2:], axis=1)
                crosses[pair, 16 * group : 16 * group + 16, :] = jnp.concatenate(
                    [upper, lower], axis=0
                ).astype(jnp.bfloat16)
            energies[trio, 0, tile] = powers[0]
            energies[trio, 1, tile] = powers[1]
        lanes = lax.broadcasted_iota(jnp.int32, (PATCH, HALF_LANES), 1)
        for trio in range(BATCH // TRIO):
            low, high = (
                jnp.dot(
                    table("back_down"), crosses[2 * trio + tile], preferred_element_type=jnp.float32
                )
                for tile in range(2)
            )
            for side in (slice(0, HALF_LANES), slice(HALF_LANES, WIDE)):
                first = low[:, side]
                second = jnp.where(lanes >= SECOND, first, high[:, side])
                second = pltpu.roll(second, HALF_LANES - SECOND, axis=1)
                third = pltpu.roll(high[:, side], HALF_LANES - THIRD, axis=1)
                for place, inverse in enumerate((first, second, third)):
                    base = (TRIO * trio + place) * PATCH
                    inverses[base : base + PATCH, side] = inverse.astype(jnp.bfloat16)

    def stage_score(step):
        corr_all = jnp.dot(
            inverses[...], table("back_across"), preferred_element_type=jnp.float32
        )
        rows = lax.broadcasted_iota(jnp.int32, (8, HALF_LANES), 0)
        lanes = lax.broadcasted_iota(jnp.int32, (8, HALF_LANES), 1)
        shift_rows = (rows - centre_reach).astype(jnp.float32)
        row_near = rows <= 2 * centre_reach
        for part in range(BATCH):
            item = at(step, 2, part)
            near_row = items_ref[NEAR_ROW, item]
            near_col = items_ref[NEAR_COL, item]
            trio, place = divmod(part, TRIO)
            mean_a, mean_b = (
                jnp.sum(
                    energies[trio, which, 0] * shares_ref[place, 0]
                    + energies[trio, which, 1] * shares_ref[place, 1],
                    keepdims=True,
                )
                * (1.0 / float(PATCH**4))
                for which in range(2)
            )
            scale = 1.0 / (
                float(PATCH**4) * jnp.sqrt(mean_a + epsilon) * jnp.sqrt(mean_b + epsilon)
            )
            caps = caps_ref[pl.ds(CAP_ROWS - near_row, ABOVE + BELOW), :]
            total, row_moment, col_moment = 0.0, 0.0, 0.0
            best = None
            for half in range(2):
                corr = corr_all[
                    PATCH * part : PATCH * (part + 1),
                    half * HALF_LANES : (half + 1) * HALF_LANES,
                ]
                edge = jnp.concatenate([corr[PATCH - ABOVE :], corr[:BELOW]], axis=0)
                corrs[half][part] = edge
                far = jnp.maximum(
                    jnp.max(jnp.minimum(edge, caps).reshape(-1, 8, HALF_LANES), axis=0),
                    jnp.max(corr[BELOW : PATCH - ABOVE].reshape(-1, 8, HALF_LANES), axis=0),
                )
                if half == 0:
                    best = far
                else:
                    far = jnp.where(lanes < PATCH - HALF_LANES, far, -BIG)
                    best = jnp.maximum(best, far)
            for half in range(2):
                values = corrs[half][part, pl.ds(near_row, 8), :]
                place = lanes + half * HALF_LANES
                shift = place - near_col
                shift = jnp.where(shift >= PATCH // 2, shift - PATCH, shift)
                shift = jnp.where(shift < -(PATCH // 2), shift + PATCH, shift)
                inside = row_near & (place < PATCH)
                close = jnp.abs(shift) <= centre_reach
                weight = jnp.where(
                    inside & close, jnp.exp(sharpness * (values * scale)), 0.0
                )
                total = total + weight
                row_moment = row_moment + weight * shift_rows
                col_moment = col_moment + weight * shift.astype(jnp.float32)
                best = jnp.maximum(
                    best, jnp.where(inside & jnp.logical_not(close), values, -BIG)
                )
            totals[pl.ds(item, 1), :] = jnp.sum(total, axis=0, keepdims=True)
            row_moments[pl.ds(item, 1), :] = jnp.sum(row_moment, axis=0, keepdims=True)
            col_moments[pl.ds(item, 1), :] = jnp.sum(col_moment, axis=0, keepdims=True)
            runners[pl.ds(item, 1), :] = jnp.max(best * scale, axis=0, keepdims=True)

    to_scalars.wait()
    to_blocks.wait()

    steps = jnp.maximum((count + BATCH - 1) // BATCH, 2)
    stage_half(0)
    stage_inverse()
    stage_half(1)

    @pl.loop(2, steps)
    def _(step):
        stage_score(step)
        stage_inverse()
        stage_half(step)

    stage_score(steps)
    stage_inverse()
    stage_score(steps + 1)

    used = lax.broadcasted_iota(jnp.int32, (capacity, 1), 0) < count
    total = jnp.sum(totals[...], axis=1, keepdims=True)
    peak_row = columns_ref[:, PEAK_ROW : PEAK_ROW + 1]
    peak_col = columns_ref[:, PEAK_COL : PEAK_COL + 1]
    results = (
        peak_row + jnp.sum(row_moments[...], axis=1, keepdims=True) / total,
        peak_col + jnp.sum(col_moments[...], axis=1, keepdims=True) / total,
        jnp.maximum(jnp.max(runners[...], axis=1, keepdims=True), -2.0),
    )
    lanes = lax.broadcasted_iota(jnp.int32, (capacity, HALF_LANES), 1)
    terms = [jnp.zeros((capacity, HALF_LANES), jnp.float32)] * 3
    for value, rest in enumerate(results):
        rest = jnp.where(used, rest, 0.0)
        for term in range(3):
            here = rest.astype(jnp.bfloat16).astype(jnp.float32)
            terms[term] = jnp.where(lanes // SPREAD_LANES == value, here, terms[term])
            rest = rest - here
    slot_row = rows_ref[MESH_ROW : MESH_ROW + 1, :]
    slot_col = columns_ref[:, MESH_COL : MESH_COL + 1]
    offset = (lanes % SPREAD_LANES - RELAX).astype(jnp.float32)
    shape = (n_row * SPREAD_ROWS, capacity)
    place = lax.broadcasted_iota(jnp.int32, shape, 0)
    row = place // SPREAD_ROWS * node_rows + place % SPREAD_ROWS - RELAX
    rows_picked = jnp.where(slot_row == row.astype(jnp.float32), 1.0, 0.0).astype(jnp.bfloat16)
    for col in range(n_col):
        here = slot_col == offset + float(col * NODE_LANES)
        sent = sum(
            jnp.dot(
                rows_picked,
                jnp.where(here, term, 0.0).astype(jnp.bfloat16),
                preferred_element_type=jnp.float32,
            )
            for term in terms
        )
        for row in range(n_row):
            block = sent[SPREAD_ROWS * row : SPREAD_ROWS * (row + 1)]
            turned = pltpu.roll(block[8:], HALF_LANES // 2, axis=1)
            out_ref[row * n_col + col] = jnp.where(
                lanes[:8] < HALF_LANES // 2, block[:8], turned
            )


def list_nodes(
    capacity,
    grid,
    everyone_ref,
    table,
    columns_ref,
    rows_ref,
    listed_ref,
):
    n_row, n_col, a_rows, node_rows = grid
    me = (lax.axis_index("row") * n_col + lax.axis_index("col")).astype(jnp.float32)
    exact = functools.partial(lax.dot_general, preferred_element_type=jnp.float32)
    plain = (((1,), (0,)), ((), ()))
    turned = (((1,), (1,)), ((), ()))

    slot = lax.broadcasted_iota(jnp.int32, (capacity, HALF_LANES), 0).astype(jnp.float32)
    before = jnp.zeros((1, HALF_LANES), jnp.float32)
    found = jnp.zeros((capacity, 3 * HALF_LANES), jnp.float32)
    for block in range(n_row * n_col // 8):
        records = everyone_ref[8 * block : 8 * block + 8, a_rows : a_rows + 16, :]
        records = records.reshape(HALF_LANES, HALF_LANES)
        mine = exact(records, table("repeat"), plain) == me
        ones = jnp.where(mine, 1.0, 0.0).astype(jnp.bfloat16)
        counts = exact(ones, table("within"), plain)
        within, loads = counts[:, :HALF_LANES], counts[:, HALF_LANES:]
        base = exact(table("below"), loads.astype(jnp.bfloat16), plain) + before
        slots = jnp.where(mine, within + base, -1.0)
        row_loads = exact(table("count"), ones, turned)
        row_base = exact(row_loads.astype(jnp.bfloat16), table("above"), plain)[:1] + before
        holds = (slot >= row_base) & (slot < row_base + row_loads[:1])
        local = lax.broadcasted_iota(jnp.int32, (HALF_LANES, HALF_LANES), 0) % 16
        mesh_row = (local + 8 * block // n_col * node_rows).astype(jnp.float32)
        found = found + exact(
            jnp.where(holds, 1.0, 0.0).astype(jnp.bfloat16),
            jnp.concatenate(
                [records, slots.astype(jnp.bfloat16), mesh_row.astype(jnp.bfloat16)], axis=1
            ),
            plain,
        )
        before = before + jnp.sum(loads, axis=0, keepdims=True)

    same = found[:, HALF_LANES : 2 * HALF_LANES] == slot
    taken = jnp.concatenate(
        [jnp.where(same, found[:, :HALF_LANES], 0.0), found[:, 2 * HALF_LANES :]], axis=1
    ).astype(jnp.bfloat16)
    columns_ref[...] = exact(taken, table("fields"), plain)
    rows = exact(table("turned"), taken, turned)
    rows_ref[...] = rows

    def field(index):
        return rows[index : index + 1, :]

    def divide(value, by):
        whole = jnp.floor((value + 0.5) * (1.0 / by))
        return whole, value - whole * by

    half = float(PATCH // 2)
    b_top = jnp.maximum(16.0 * field(ROW_HIGH) + field(ROW_LOW) - half, 0.0)
    b_left = jnp.maximum(16.0 * field(COL_HIGH) + field(COL_LOW) - half, 0.0)
    a_top = STRIDE * field(MESH_ROW) + STRIDE // 2
    a_left = STRIDE * field(MESH_COL) + (STRIDE // 2 + half)
    b_group, b_row_rest = divide(b_top, 16)
    b_block, b_col_rest = divide(b_left, PATCH)
    a_group, a_row_rest = divide(a_top, 16)
    a_block, a_col_rest = divide(a_left, PATCH)
    near_row = field(PEAK_ROW) + b_row_rest - a_row_rest + (ABOVE - centre_reach)
    near_col = divide(field(PEAK_COL) + b_col_rest - a_col_rest, PATCH)[1]
    for index, value in (
        (B_BLOCK, b_block),
        (B_ROW, 16.0 * b_group),
        (B_ROW_REST, b_row_rest),
        (B_COL_REST, b_col_rest),
        (A_BLOCK, a_block),
        (A_ROW, 16.0 * a_group),
        (A_ROW_REST, a_row_rest),
        (A_COL_REST, a_col_rest),
        (NEAR_ROW, near_row),
        (NEAR_COL, near_col),
    ):
        listed_ref[index : index + 1, :] = value.astype(jnp.int32)
    listed_ref[FIELDS:, :] = jnp.zeros((16 - FIELDS, capacity), jnp.int32)
    return jnp.max(before).astype(jnp.int32)


def cut_kernel(tile_ref, out_ref):
    strip = tile_ref[...]
    for block in range(out_ref.shape[0]):
        out_ref[block] = cut(strip, block * PATCH)


def cut_tile(tile):
    rows, cols = tile.shape
    blocks = -(-cols // PATCH)
    return pl.pallas_call(
        cut_kernel,
        grid=(rows // HALF_LANES,),
        out_shape=jax.ShapeDtypeStruct((blocks, rows + 16, WIDE), jnp.bfloat16),
        in_specs=[pl.BlockSpec((HALF_LANES, cols), lambda step: (step, 0))],
        out_specs=pl.BlockSpec((blocks, HALF_LANES, WIDE), lambda step: (0, step, 0)),
        cost_estimate=pl.CostEstimate(
            flops=0, bytes_accessed=2 * rows * (cols + blocks * WIDE), transcendentals=0
        ),
    )(tile)


def correlate(capacity, everyone, blocks, grid):
    n_row, n_col, a_rows, node_rows = grid
    tables, places = all_tables()
    a_blocks = (n_col * everyone.shape[2] + 76) // PATCH + 2
    vmem = pl.BlockSpec(memory_space=pltpu.VMEM)
    rows = pltpu.VMEM((capacity, HALF_LANES), jnp.float32)
    return pl.pallas_call(
        functools.partial(correlate_kernel, capacity, grid, places),
        out_shape=jax.ShapeDtypeStruct(
            (n_row * n_col, SPREAD_ROWS // 2, HALF_LANES), jnp.float32
        ),
        in_specs=[vmem, pl.BlockSpec(memory_space=pl.ANY), vmem],
        out_specs=vmem,
        scratch_shapes=[
            pltpu.VMEM((2 * BATCH * PATCH, WIDE), jnp.bfloat16),
            pltpu.VMEM((BATCH // TRIO, 2, 2, PATCH, WIDE), jnp.bfloat16),
            pltpu.VMEM((BATCH // TRIO * 2, PAIRED, WIDE), jnp.bfloat16),
            pltpu.VMEM((BATCH * PATCH, WIDE), jnp.bfloat16),
            pltpu.VMEM((BATCH, ABOVE + BELOW, HALF_LANES), jnp.float32),
            pltpu.VMEM((BATCH, ABOVE + BELOW, HALF_LANES), jnp.float32),
            pltpu.VMEM((BATCH // TRIO, 2, 2, 8, HALF_LANES), jnp.float32),
        ]
        + [rows] * 4
        + [
            pltpu.VMEM((a_blocks, n_row * a_rows + PATCH, WIDE), jnp.bfloat16),
            pltpu.VMEM(blocks.shape, jnp.bfloat16),
            rows,
            pltpu.VMEM((16, capacity), jnp.int32),
            pltpu.SMEM((16, capacity), jnp.int32),
            pltpu.SemaphoreType.DMA((2,)),
            pltpu.VMEM((2 * CAP_ROWS, HALF_LANES), jnp.float32),
            pltpu.VMEM((16, capacity), jnp.float32),
            pltpu.VMEM((TRIO, 2, 8, HALF_LANES), jnp.float32),
        ],
        compiler_params=pltpu.CompilerParams(vmem_limit_bytes=61 * 1024 * 1024),
    )(everyone, blocks, tables)


def per_device(a_window, b_section, owners, pos_rows, pos_cols, peaks):
    node_rows, node_cols = pos_rows.shape
    nodes = node_rows * node_cols
    n_row, n_col = lax.axis_size("row"), lax.axis_size("col")
    devices = n_row * n_col
    me_row, me_col = lax.axis_index("row"), lax.axis_index("col")
    share = max(2, (nodes * 8 // 5 + devices - 1) // devices)
    a_rows, a_cols = a_window.shape
    height, breadth = n_row * node_rows, n_col * node_cols

    mesh_col = me_col * node_cols + lax.broadcasted_iota(jnp.int32, pos_rows.shape, 1)
    records = jnp.concatenate(
        [
            owners.reshape(node_rows, node_cols),
            pos_rows // 16,
            pos_rows % 16,
            pos_cols // 16,
            pos_cols % 16,
            peaks[0],
            peaks[1],
            mesh_col,
        ],
        axis=1,
    ).astype(jnp.bfloat16)
    records = jnp.pad(records, ((0, 16 - node_rows), (0, 0)), constant_values=-1)
    sent = jnp.concatenate([a_window, records], axis=0)
    sent = jnp.broadcast_to(sent[None], (n_col,) + sent.shape)
    sent = lax.all_to_all(sent, "col", split_axis=0, concat_axis=0, tiled=True)
    everyone = lax.all_gather(sent, "row").reshape(devices, a_rows + 16, a_cols)

    grid = (n_row, n_col, a_rows, node_rows)
    spread = correlate(share * devices, everyone, cut_tile(b_section), grid)
    spread = lax.all_to_all(spread, ("row", "col"), split_axis=0, concat_axis=0, tiled=True)
    tall, broad = node_rows + 2 * RELAX, node_cols + 2 * RELAX
    spread = jnp.sum(spread, axis=0)
    half_lanes = HALF_LANES // 2
    spread = jnp.concatenate([spread[:, :half_lanes], spread[:, half_lanes:]], axis=0)[:tall]
    spread = [spread[:, SPREAD_LANES * value :][:, :broad] for value in range(3)]
    runner = spread[2][RELAX:-RELAX, RELAX:-RELAX]
    field = jnp.stack(spread[:2])
    for step in range(RELAX):
        reach = RELAX - 1 - step
        centre = field[:, 1:-1, 1:-1]
        around = (
            field[:, 2:, 1:-1] + field[:, :-2, 1:-1] + field[:, 1:-1, 2:] + field[:, 1:-1, :-2]
        )
        field = centre + stiffness * (around - 4.0 * centre)
        rows = me_row * node_rows - reach + jnp.arange(node_rows + 2 * reach)
        cols = me_col * node_cols - reach + jnp.arange(node_cols + 2 * reach)
        inside = ((rows >= 0) & (rows < height))[:, None] & ((cols >= 0) & (cols < breadth))[None]
        field = jnp.where(inside[None], field, 0.0)
    return (field, runner)


def solution(mesh):
    placed = (
        P("row", "col"),
        P("row", "col"),
        P("row", "col", None, None, None),
        P("row", "col"),
        P("row", "col"),
        P(None, "row", "col"),
    )
    return jax.shard_map(
        per_device,
        mesh=mesh,
        in_specs=placed,
        out_specs=(P(None, "row", "col"), P("row", "col")),
        check_vma=False,
    )
```
